32 devices in a mesh: grp: 2 (over y), lon: 4 (over z), lat: 2 (over x), ch: 2 (over core).
Axes of the slice: x: 2, y: 2, z: 4, core: 2. Of those that a mesh axis runs over, the one named last changes fastest.
Arguments:
- patches: bfloat16 [512, 384, 768], P(('grp', 'lat'), 'lon', 'ch'), parts along dimension 0, may hold values from -6 to 6
- filter_norm_gain: bfloat16 [768], P('ch'), may hold values from 0.099609375 to 1.8984375
- filter_norm_bias: bfloat16 [768], P('ch'), may hold values from -6 to 6
- filter_in: bfloat16 [2, 8, 96, 96], P(None, 'ch'), may hold values from -0.625 to 0.625
- filter_in_bias: bfloat16 [2, 768], P(None, 'ch'), may hold values from -1.5 to 1.5
- filter_out: bfloat16 [2, 8, 96, 96], P(None, 'ch'), may hold values from -0.625 to 0.625
- filter_out_bias: bfloat16 [2, 768], P(None, 'ch'), may hold values from -0.875 to 0.875
- kept_lat: int32 [8], P('ch'), may hold values from 32 to 64, as said below
- kept_lon: int32 [8], P('ch'), may hold values from 64 to 128, as said below
- norm_gain: bfloat16 [768], replicated, may hold values from 0.099609375 to 1.8984375
- norm_bias: bfloat16 [768], replicated, may hold values from -6 to 6
- dense_in: bfloat16 [768, 1536], P(None, 'ch'), may hold values from -0.21875 to 0.21875
- dense_in_bias: bfloat16 [1536], P('ch'), may hold values from -6 to 6
- dense_out: bfloat16 [1536, 768], P('ch'), may hold values from -0.15625 to 0.15625
- dense_out_bias: bfloat16 [768], P('ch'), may hold values from -4 to 4
Outputs:
- block_out: bfloat16 [4, 4, 32, 384, 768], P(('grp', 'lat'), 'lon', None, None, 'ch'), parts along dimension 0
The draws below stay inside these ranges and needn't reach their ends.
There are 2 independent parts, one for each index of `grp`. The reference program is written for one: setup_inputs(seed, part) draws one part's arguments, and reference() takes and returns one part's arrays. A program takes and returns all parts, laid end to end along the dimension named above; an argument that names none is the same for every part. Nothing has to cross between parts.
Inputs may be any that keep to these rules, and one draw needn't show every extreme that they name: Block b keeps latitude frequencies -kept_lat[b] to kept_lat[b] - 1; in every draw some block keeps all 128. Block b keeps longitude frequencies 0 to kept_lon[b] - 1; in every draw some block keeps 128.
All inputs are finite; a program needn't handle non-finite values.
Results may differ from the reference program's by a relative error of at most 0.0095.
Values may be sent and summed in bfloat16 or wider, within the bound.
No kernel may reach another device: no remote copies, remote signals or barrier semaphores. Data moves between devices by JAX's collectives and lax.ppermute only.
A program may use at most 192 MiB of HBM per device.

```python
import math
import jax
import jax.numpy as jnp
from jax import lax

H = 256
W = 384
C = 768
NB = 8
BS = 96
HID = 1536
MLAT = 64
KEEP_LON = 128
N_LON = 4
N_LAT = 2


def capped_counts(key, ceiling):
    counts = jax.random.randint(jax.random.fold_in(key, 1), (NB,), ceiling // 2, ceiling + 1, dtype=jnp.int32)
    chosen = jax.random.randint(jax.random.fold_in(key, 2), (), 0, NB, dtype=jnp.int32)
    return jnp.where(jnp.arange(NB, dtype=jnp.int32) == chosen, ceiling, counts).astype(jnp.int32)


def channel_scales(lowest, ratio):
    position = jnp.arange(C, dtype=jnp.float32) / (C - 1)
    return lowest * jnp.exp(position * jnp.log(ratio))


def draw_patches(key, part):
    key = jax.random.fold_in(key, 5)
    level_key = jax.random.fold_in(key, 7)
    values = jax.random.normal(key, (H, W, C), jnp.float32)
    values = jnp.clip(values, -3.0, 3.0) * channel_scales(0.5, 2.0)
    level = jax.random.uniform(level_key, (H, W, 1), jnp.float32, 0.5, 1.5)
    values = values + level * channel_scales(0.2, 10.0)
    return jnp.clip(values, -6.0, 6.0).astype(jnp.bfloat16)


def draw_kept_lat(key, part):
    return capped_counts(jax.random.fold_in(key, 11), MLAT)


def draw_kept_lon(key, part):
    return capped_counts(jax.random.fold_in(key, 17), KEEP_LON)


def shard_levels(rng, shape, shards, smallest, high):
    loudness, own = 1.0, jax.random.fold_in(rng, 6)
    for dim, shards_of in shards:
        heights = jnp.exp(jax.random.uniform(jax.random.fold_in(own, dim), (shards_of,), jnp.float32, smallest / len(shards), high / len(shards)))
        loudness = loudness * jnp.repeat(heights, shape[dim] // shards_of).reshape([-1 if axis == dim else 1 for axis in range(len(shape))])
    return loudness


def bell_draw(stream_key, extent, width, bound, pieces=(), kind=jnp.bfloat16):
    gain = shard_levels(stream_key, extent, pieces, -0.22, 0.18) if pieces else 1.0
    entries = jax.random.normal(stream_key, extent, jnp.float32) * width * gain
    return jnp.minimum(jnp.maximum(entries, -bound), bound).astype(kind)


def setup_inputs(seed: int = 0, part: int = 0) -> dict:
    arg_keys = jax.random.split(jax.random.key(seed), 16)
    part_keys = jax.random.split(jax.random.fold_in(arg_keys[15], part), 16)
    return {
        "patches": draw_patches(jax.random.fold_in(jax.random.fold_in(arg_keys[15], part), 71), part),
        "filter_norm_gain": jnp.clip(1.0 + 0.18 * jax.random.normal(arg_keys[1], (C,), jnp.float32), 0.099609375, 1.8984375).astype(jnp.bfloat16),
        "filter_norm_bias": bell_draw(arg_keys[2], (C,), 0.5, 6.0, ((0, 2),)),
        "filter_in": bell_draw(arg_keys[3], (2, NB, BS, BS), BS ** -0.5, 0.625, ((1, 2),)),
        "filter_in_bias": bell_draw(arg_keys[4], (2, C), 0.1, 1.5, ((1, 2),)),
        "filter_out": bell_draw(arg_keys[5], (2, NB, BS, BS), BS ** -0.5, 0.625, ((1, 2),)),
        "filter_out_bias": bell_draw(arg_keys[6], (2, C), 0.06, 0.875, ((1, 2),)),
        "kept_lat": draw_kept_lat(jax.random.fold_in(arg_keys[15], 71), part),
        "kept_lon": draw_kept_lon(jax.random.fold_in(arg_keys[15], 71), part),
        "norm_gain": jnp.clip(1.0 + 0.18 * jax.random.normal(arg_keys[9], (C,), jnp.float32), 0.099609375, 1.8984375).astype(jnp.bfloat16),
        "norm_bias": bell_draw(arg_keys[10], (C,), 0.5, 6.0),
        "dense_in": bell_draw(arg_keys[11], (C, HID), C ** -0.5, 0.21875, ((1, 2),)),
        "dense_in_bias": bell_draw(arg_keys[12], (HID,), 0.5, 6.0, ((0, 2),)),
        "dense_out": bell_draw(arg_keys[13], (HID, C), HID ** -0.5, 0.15625, ((0, 2),)),
        "dense_out_bias": bell_draw(arg_keys[14], (C,), 0.3, 4.0, ((0, 2),)),
    }


shrink_level = 0.01
norm_epsilon = 1e-05

def lon_forward(number, length):
    freq_ids = jnp.arange(number, dtype=jnp.int32)
    cell_ids = jnp.arange(length, dtype=jnp.int32)
    phase_turns = cell_ids[:, None] * freq_ids[None, :] % length
    angles = phase_turns.astype(jnp.float32) * (2.0 * math.pi / length)
    factor = 1.0 / math.sqrt(length)
    return jnp.stack([jnp.cos(angles) * factor, -jnp.sin(angles) * factor], axis=1).astype(jnp.bfloat16)

def lon_inverse(freq_ids, length):
    cell_ids = jnp.arange(length, dtype=jnp.int32)
    phase_turns = freq_ids[:, None] * cell_ids[None, :] % length
    angles = phase_turns.astype(jnp.float32) * (2.0 * math.pi / length)
    factor = 1.0 / math.sqrt(length)
    weight = jnp.where(freq_ids == 0, 1.0, 2.0).astype(jnp.float32)[:, None]
    return jnp.stack([jnp.cos(angles) * factor * weight, -jnp.sin(angles) * factor * weight]).astype(jnp.bfloat16)

def band_ids(half_band, length):
    slot_ids = jnp.arange(2 * half_band, dtype=jnp.int32)
    return jnp.where(slot_ids < half_band, slot_ids, slot_ids + length - 2 * half_band)

def lat_forward(row_ids, half_band, length):
    phase_turns = band_ids(half_band, length)[:, None] * row_ids[None, :] % length
    angles = phase_turns.astype(jnp.float32) * (2.0 * math.pi / length)
    factor = 1.0 / math.sqrt(length)
    cosine = jnp.cos(angles) * factor
    sine_part = jnp.sin(angles) * factor
    upper_half = jnp.concatenate([cosine, sine_part], axis=1)
    bottom = jnp.concatenate([-sine_part, cosine], axis=1)
    return jnp.concatenate([upper_half, bottom], axis=0).astype(jnp.bfloat16)

def lat_inverse(row_ids, half_band, length):
    phase_turns = row_ids[:, None] * band_ids(half_band, length)[None, :] % length
    angles = phase_turns.astype(jnp.float32) * (2.0 * math.pi / length)
    factor = 1.0 / math.sqrt(length)
    cosine = jnp.cos(angles) * factor
    sine_part = jnp.sin(angles) * factor
    upper_half = jnp.concatenate([cosine, -sine_part], axis=1)
    bottom = jnp.concatenate([sine_part, cosine], axis=1)
    return jnp.concatenate([upper_half, bottom], axis=0).astype(jnp.bfloat16)

def complex_layer(values, weight, offset):
    products = jnp.einsum('tjkbc,ubcd->tujkbd', values.astype(jnp.float32), weight.astype(jnp.float32))
    offset = offset.astype(jnp.float32)
    real_part = products[0, 0] - products[1, 1] + offset[0]
    imag_part = products[1, 0] + products[0, 1] + offset[1]
    return jnp.stack([real_part, imag_part])

def reference(patches, filter_norm_gain, filter_norm_bias, filter_in, filter_in_bias, filter_out, filter_out_bias, kept_lat, kept_lon, norm_gain, norm_bias, dense_in, dense_in_bias, dense_out, dense_out_bias):
    block_width = C // NB
    raw = patches.astype(jnp.float32)
    pre_center = lax.optimization_barrier(jnp.mean(raw, axis=-1, keepdims=True))
    pre_spread = lax.optimization_barrier(jnp.mean((raw - pre_center) ** 2, axis=-1, keepdims=True))
    prenormed = ((raw - pre_center) * lax.rsqrt(pre_spread + norm_epsilon) * filter_norm_gain.astype(jnp.float32) + filter_norm_bias.astype(jnp.float32)).astype(jnp.bfloat16)
    spectrum = jnp.einsum('hwc,wtk->thkc', prenormed.astype(jnp.float32), lon_forward(KEEP_LON, W).astype(jnp.float32))
    spectrum = spectrum.astype(jnp.bfloat16)
    row_ids = jnp.arange(H, dtype=jnp.int32)
    banded = jnp.dot(lat_forward(row_ids, MLAT, H).astype(jnp.float32), spectrum.reshape(2 * H, -1).astype(jnp.float32), preferred_element_type=jnp.float32)
    banded = banded.astype(jnp.bfloat16).reshape(2, 2 * MLAT, KEEP_LON, NB, block_width)
    first = complex_layer(banded, filter_in, filter_in_bias.reshape(2, NB, block_width))
    first = jnp.maximum(first, 0.0).astype(jnp.bfloat16)
    second = complex_layer(first, filter_out, filter_out_bias.reshape(2, NB, block_width))
    shrunk = jnp.sign(second) * jnp.maximum(jnp.abs(second) - shrink_level, 0.0)
    band_slots = jnp.arange(2 * MLAT, dtype=jnp.int32)
    signed_band = jnp.where(band_slots < MLAT, band_slots, band_slots - 2 * MLAT)
    lat_ok = (signed_band[:, None] >= -kept_lat[None, :]) & (signed_band[:, None] < kept_lat[None, :])
    lon_ok = jnp.arange(KEEP_LON, dtype=jnp.int32)[:, None] < kept_lon[None, :]
    keep_mask = (lat_ok[:, None, :] & lon_ok[None, :, :]).astype(jnp.float32)[..., None]
    kept_modes = (shrunk * keep_mask).astype(jnp.bfloat16).reshape(4 * MLAT, -1)
    spatial = jnp.dot(lat_inverse(row_ids, MLAT, H).astype(jnp.float32), kept_modes.astype(jnp.float32), preferred_element_type=jnp.float32)
    spatial = spatial.astype(jnp.bfloat16).reshape(2, H, KEEP_LON, C)
    freq_ids = jnp.arange(KEEP_LON, dtype=jnp.int32)
    fine_part = jnp.einsum('thkc,tkw->hwc', spatial.astype(jnp.float32), lon_inverse(freq_ids, W).astype(jnp.float32))
    mixed = (raw + fine_part).astype(jnp.bfloat16)
    wide = mixed.astype(jnp.float32).reshape(H * W, C)
    center = lax.optimization_barrier(jnp.mean(wide, axis=-1, keepdims=True))
    spread = lax.optimization_barrier(jnp.mean((wide - center) ** 2, axis=-1, keepdims=True))
    normed = ((wide - center) * lax.rsqrt(spread + norm_epsilon) * norm_gain.astype(jnp.float32) + norm_bias.astype(jnp.float32)).astype(jnp.bfloat16)
    hidden = jnp.dot(normed.astype(jnp.float32), dense_in.astype(jnp.float32), preferred_element_type=jnp.float32)
    hidden = jax.nn.gelu(hidden + dense_in_bias.astype(jnp.float32), approximate=False).astype(jnp.bfloat16)
    summed = jnp.dot(hidden.astype(jnp.float32), dense_out.astype(jnp.float32), preferred_element_type=jnp.float32)
    result = (wide + summed + dense_out_bias.astype(jnp.float32)).astype(jnp.bfloat16)
    return result.reshape(N_LAT, N_LON, H // (N_LAT * N_LON), W, C)
```

```python
import functools
import math

import jax
import jax.numpy as jnp
import numpy as np
from jax import lax
from jax.experimental import pallas as pl
from jax.experimental.pallas import tpu as pltpu
from jax.sharding import PartitionSpec as P

H = 256
W = 384
C = 768
MLAT = 64
KEEP_LON = 128

shrink_level = 0.01
norm_epsilon = 1e-05

BF = jnp.bfloat16
F32 = jnp.float32


def angle_table(rows, cols, length):
    phase = rows[:, None] * cols[None, :] % length
    return phase * (2.0 * math.pi / length)


def lat_slots(lat_count, lon_count):
    per = MLAT // (lat_count * lon_count)
    freq, kind = [], []
    for dev in range(lat_count * lon_count):
        for pair in range(dev * per, dev * per + per):
            freq += [0, MLAT] if pair == 0 else [pair, pair]
            kind += [0, 0] if pair == 0 else [0, 1]
        freq.append(MLAT if dev == 0 else 0)
        kind.append(1 if dev == 0 else 2)
    return np.array(freq), np.array(kind)


def lat_tables(lat_count, lon_count):
    freq, kind = lat_slots(lat_count, lon_count)
    angles = angle_table(freq, np.arange(H), H)
    table = np.where(kind[:, None] == 0, np.cos(angles), -np.sin(angles)) / math.sqrt(H)
    table = np.where(kind[:, None] == 2, 0.0, table)
    return table.astype(np.float32)


def lon_tables(order):
    freqs = np.arange(KEEP_LON)
    angles = angle_table(freqs, order, W)
    factor = 1.0 / math.sqrt(W)
    weight = np.where(freqs == 0, 1.0, 2.0)[:, None]
    forward = np.concatenate([np.cos(angles) * factor, -np.sin(angles) * factor], axis=0)
    inverse = np.concatenate(
        [np.cos(angles) * factor * weight, -np.sin(angles) * factor * weight], axis=0
    ).T
    return forward.astype(np.float32).astype(jnp.bfloat16), inverse.astype(np.float32).astype(jnp.bfloat16)


def spread8(table):
    return np.kron(table, np.eye(8, dtype=np.float32)).astype(jnp.bfloat16)


def lat_forward_kernel(cells_ref, table_ref, send_ref, keep_ref):
    rows = cells_ref.shape[0]
    values = cells_ref[...].astype(F32).reshape(rows, 2, 8, cells_ref.shape[2])
    width = cells_ref.shape[2]
    pair = jnp.concatenate(
        [values[:, 0].reshape(rows * 8, width), values[:, 1].reshape(rows * 8, width)], axis=1
    ).astype(BF)
    half = table_ref.shape[0] // 2
    for part, out_ref in ((0, send_ref), (1, keep_ref)):
        total = jnp.dot(
            table_ref[part * half : (part + 1) * half, :], pair, preferred_element_type=F32
        )
        slots = half // 8
        out_ref[...] = jnp.concatenate(
            [
                total[:, :width].reshape(slots, 8, width),
                total[:, width:].reshape(slots, 8, width),
            ],
            axis=1,
        ).astype(BF)


def lat_forward(cells, table):
    rows, cols, width = cells.shape
    slots = table.shape[0] // 16
    block = pl.BlockSpec((slots, 16, width), lambda i: (0, i, 0))
    return pl.pallas_call(
        lat_forward_kernel,
        grid=(cols // 16,),
        in_specs=[
            pl.BlockSpec((rows, 16, width), lambda i: (0, i, 0)),
            pl.BlockSpec(table.shape, lambda i: (0, 0)),
        ],
        out_specs=[block, block],
        out_shape=[jax.ShapeDtypeStruct((slots, cols, width), BF)] * 2,
        compiler_params=pltpu.CompilerParams(vmem_limit_bytes=40 << 20),
        cost_estimate=pl.CostEstimate(
            flops=2 * table.size * cols // 8 * width,
            bytes_accessed=4 * rows * cols * width,
            transcendentals=0,
        ),
        name="lat_forward",
    )(cells, table)


def lat_inverse_kernel(own_ref, other_ref, table_ref, patches_ref, out_ref):
    rows, _, width = patches_ref.shape
    slots = own_ref.shape[0] * own_ref.shape[1]

    def flat(ref):
        values = ref[...].astype(F32).reshape(slots, 2, 8, width)
        return jnp.concatenate(
            [values[:, 0].reshape(slots * 8, width), values[:, 1].reshape(slots * 8, width)], axis=1
        ).astype(BF)

    half = table_ref.shape[1] // 2
    total = jnp.dot(table_ref[:, :half], flat(own_ref), preferred_element_type=F32)
    total += jnp.dot(table_ref[:, half:], flat(other_ref), preferred_element_type=F32)
    fine = jnp.concatenate(
        [total[:, :width].reshape(rows, 8, width), total[:, width:].reshape(rows, 8, width)], axis=1
    )
    out_ref[...] = (patches_ref[...].astype(F32) + fine).astype(BF)


def lat_inverse(own, other, table, patches, first_block):
    groups, slots, cols, width = own.shape
    rows = patches.shape[0]
    spec = pl.BlockSpec((groups, slots, 16, width), lambda i: (0, 0, i, 0))
    return pl.pallas_call(
        lat_inverse_kernel,
        grid=(cols // 16,),
        in_specs=[
            spec,
            spec,
            pl.BlockSpec(table.shape, lambda i: (0, 0)),
            pl.BlockSpec((rows, 16, width), lambda i: (0, first_block + i, 0)),
        ],
        out_specs=pl.BlockSpec((rows, 16, width), lambda i: (0, i, 0)),
        out_shape=jax.ShapeDtypeStruct((rows, cols, width), BF),
        compiler_params=pltpu.CompilerParams(vmem_limit_bytes=40 << 20),
        cost_estimate=pl.CostEstimate(
            flops=2 * table.size * cols // 8 * width,
            bytes_accessed=6 * rows * cols * width,
            transcendentals=0,
        ),
        name="lat_inverse",
    )(own, other, table, patches)


def modes_kernel(
    chunks,
    first_pair_ref,
    lat_lo_ref,
    lon_lo_ref,
    *refs,
):
    pair_refs = refs[:chunks]
    spare_refs = refs[chunks : 2 * chunks]
    forward_ref, inverse_ref, w_in_ref, b_in_ref, w_out_ref, b_out_ref = refs[
        2 * chunks : 2 * chunks + 6
    ]
    out_refs = refs[2 * chunks + 6 :]
    width = pair_refs[0].shape[-1]
    groups, _, cols, _ = pair_refs[0].shape
    step = pl.program_id(0)
    pairs = pl.num_programs(0)
    pair_id = first_pair_ref[0] + step
    special = pair_id == 0
    keep = KEEP_LON

    def columns(refs, row):
        return jnp.concatenate(
            [ref[:, row].reshape(groups * cols, width) for ref in refs], axis=0
        )

    both = jnp.concatenate([columns(pair_refs, 0), columns(pair_refs, 1)], axis=1)
    spectrum = jnp.dot(forward_ref[...], both, preferred_element_type=F32)
    a_re, a_im = spectrum[:keep, :width], spectrum[keep:, :width]
    b_re, b_im = spectrum[:keep, width:], spectrum[keep:, width:]

    def filtered(plus_re, plus_im, minus_re, minus_im):
        banded = jnp.concatenate(
            [
                jnp.concatenate([plus_re, plus_im], axis=1),
                jnp.concatenate([minus_re, minus_im], axis=1),
            ],
            axis=0,
        ).astype(BF)
        first = jnp.dot(banded, w_in_ref[...], preferred_element_type=F32) + b_in_ref[...]
        first = jnp.maximum(first, 0.0).astype(BF)
        second = jnp.dot(first, w_out_ref[...], preferred_element_type=F32) + b_out_ref[...]
        shrunk = second - jnp.clip(second, -shrink_level, shrink_level)
        freq = lax.broadcasted_iota(jnp.int32, (keep, 2 * width), 0)
        lon_ok = freq < lon_lo_ref[...]
        plus_ok = lon_ok & (pair_id < lat_lo_ref[...])
        minus_id = jnp.where(special, MLAT, pair_id)
        minus_ok = lon_ok & (minus_id <= lat_lo_ref[...])
        plus = jnp.where(plus_ok, shrunk[:keep], 0.0)
        minus = jnp.where(minus_ok, shrunk[keep:], 0.0)
        return plus[:, :width], plus[:, width:], minus[:, :width], minus[:, width:]

    def back(values, refs, row):
        grid_values = jnp.dot(inverse_ref[...], values, preferred_element_type=F32).astype(BF)
        for i, ref in enumerate(refs):
            piece = grid_values[i * groups * cols : (i + 1) * groups * cols]
            for r in range(piece.shape[1] // width):
                ref[:, pl.ds(row + r, 1)] = piece[:, r * width : (r + 1) * width].reshape(
                    groups, 1, cols, width
                )

    @pl.when(special)
    def _():
        spare = jnp.dot(forward_ref[...], columns(spare_refs, 0), preferred_element_type=F32)
        e_re, e_im = spare[:keep], spare[keep:]
        p_re, p_im, m_re, m_im = filtered(a_re, a_im, b_re + e_im, b_im - e_re)
        values = jnp.concatenate(
            [jnp.concatenate([p_re, m_re], axis=1), jnp.concatenate([p_im, m_im], axis=1)], axis=0
        ).astype(BF)
        back(values, out_refs, 2 * step)
        back(jnp.concatenate([-m_im, m_re], axis=0).astype(BF), out_refs, 2 * pairs)

    @pl.when(jnp.logical_not(special))
    def _():
        p_re, p_im, m_re, m_im = filtered(a_re - b_im, a_im + b_re, a_re + b_im, a_im - b_re)
        values = jnp.concatenate(
            [
                jnp.concatenate([p_re + m_re, p_im - m_im], axis=1),
                jnp.concatenate([p_im + m_im, m_re - p_re], axis=1),
            ],
            axis=0,
        ).astype(BF)
        back(values, out_refs, 2 * step)

    @pl.when(jnp.logical_and(step == 0, jnp.logical_not(special)))
    def _():
        for ref in out_refs:
            ref[:, pl.ds(2 * pairs, 1)] = jnp.zeros((groups, 1, cols, width), BF)


def modes(received, first_pair, lat_keep, lon_keep, forward, inverse, w_in, b_in, w_out, b_out):
    chunks = len(received)
    groups, slots, cols, width = received[0].shape
    pairs = slots // 2
    pair_spec = pl.BlockSpec((groups, 2, cols, width), lambda i: (0, i, 0, 0))
    spare_spec = pl.BlockSpec((groups, 1, cols, width), lambda i: (0, slots - 1, 0, 0))
    whole = lambda array: pl.BlockSpec(array.shape, lambda i: (0,) * array.ndim)
    return pl.pallas_call(
        functools.partial(modes_kernel, chunks),
        grid=(pairs,),
        in_specs=[pl.BlockSpec(memory_space=pltpu.SMEM), whole(lat_keep), whole(lon_keep)]
        + [pair_spec] * chunks
        + [spare_spec] * chunks
        + [whole(forward), whole(inverse), whole(w_in), whole(b_in), whole(w_out), whole(b_out)],
        out_specs=[pl.BlockSpec((groups, slots, cols, width), lambda i: (0, 0, 0, 0))] * chunks,
        out_shape=[jax.ShapeDtypeStruct((groups, slots, cols, width), BF)] * chunks,
        compiler_params=pltpu.CompilerParams(vmem_limit_bytes=48 << 20),
        cost_estimate=pl.CostEstimate(
            flops=pairs * 2 * (2 * 2 * KEEP_LON * W * 2 * width + 4 * KEEP_LON * 4 * width * width),
            bytes_accessed=4 * chunks * groups * slots * cols * width,
            transcendentals=0,
        ),
        name="modes",
    )(
        first_pair, lat_keep, lon_keep, *received, *received,
        forward, inverse, w_in, b_in, w_out, b_out,
    )


def mlp_kernel(
    flag_ref, own_ref, other_ref, gain_ref, bias_ref, w_in_ref, b_in_ref, w_out_ref, b_out_ref,
    out_ref,
):
    width = own_ref.shape[-1]
    cells = own_ref.shape[1] * own_ref.shape[2]
    own = own_ref[0].reshape(cells, width)
    other = other_ref[0].reshape(cells, width)
    flip = flag_ref[0] == 1
    low = jnp.where(flip, other, own)
    high = jnp.where(flip, own, other)
    wide = jnp.concatenate([low, high], axis=1).astype(F32)
    center = jnp.mean(wide, axis=1, keepdims=True)
    off = wide - center
    spread = jnp.mean(off * off, axis=1, keepdims=True)
    normed = (off * lax.rsqrt(spread + norm_epsilon) * gain_ref[...] + bias_ref[...]).astype(BF)
    hidden = jnp.dot(normed, w_in_ref[...], preferred_element_type=F32) + b_in_ref[...]
    hidden = (hidden * (0.5 + 0.5 * lax.erf(hidden * math.sqrt(0.5)))).astype(BF)
    total = jnp.dot(hidden, w_out_ref[...], preferred_element_type=F32) + wide + b_out_ref[...]
    total = total.astype(BF)
    rows, cols = own_ref.shape[1], own_ref.shape[2]
    out_ref[0, 0] = total[:, :width].reshape(rows, cols, width)
    out_ref[0, 1] = total[:, width:].reshape(rows, cols, width)


def mlp(flag, own, other, gain, bias, w_in, b_in, w_out, b_out):
    groups, rows, cols, width = own.shape
    whole = lambda array: pl.BlockSpec(array.shape, lambda i: (0,) * array.ndim)
    cell_spec = pl.BlockSpec((1, rows, cols, width), lambda i: (i, 0, 0, 0))
    cells = groups * rows * cols
    return pl.pallas_call(
        mlp_kernel,
        grid=(groups,),
        in_specs=[pl.BlockSpec(memory_space=pltpu.SMEM), cell_spec, cell_spec]
        + [whole(a) for a in (gain, bias, w_in, b_in, w_out, b_out)],
        out_specs=pl.BlockSpec((1, 2, rows, cols, width), lambda i: (i, 0, 0, 0, 0)),
        out_shape=jax.ShapeDtypeStruct((groups, 2, rows, cols, width), BF),
        compiler_params=pltpu.CompilerParams(vmem_limit_bytes=48 << 20),
        cost_estimate=pl.CostEstimate(
            flops=4 * cells * w_in.size,
            bytes_accessed=8 * cells * width,
            transcendentals=cells * w_in.shape[1],
        ),
        name="channel_mlp",
    )(flag, own, other, gain, bias, w_in, b_in, w_out, b_out)


def block_diagonal(weight):
    blocks, n = weight.shape[1], weight.shape[2]
    eye = jnp.eye(blocks, dtype=weight.dtype)
    spread = (weight[:, :, :, None, :] * eye[None, :, None, :, None]).reshape(
        2, blocks * n, blocks * n
    )
    return jnp.concatenate(
        [
            jnp.concatenate([spread[0], spread[1]], axis=1),
            jnp.concatenate([-spread[1], spread[0]], axis=1),
        ],
        axis=0,
    )


def swap(values, axis):
    return lax.ppermute(values, axis, [(0, 1), (1, 0)])


def column_plan(
    chunk_cols,
    patches,
    filter_norm_gain,
    filter_norm_bias,
    filter_in,
    filter_in_bias,
    filter_out,
    filter_out_bias,
    kept_lat,
    kept_lon,
    norm_gain,
    norm_bias,
    dense_in,
    dense_in_bias,
    dense_out,
    dense_out_bias,
):
    lon_count = lax.axis_size("lon")
    lat_count = lax.axis_size("lat")
    rows, cols, width = patches.shape
    chunks = cols // chunk_cols
    band_rows = rows // lon_count
    block_width = filter_in.shape[2]
    lat_id = lax.axis_index("lat")
    lon_id = lax.axis_index("lon")
    ch_id = lax.axis_index("ch")
    pairs = MLAT // (lat_count * lon_count)
    slots = 2 * pairs + 1

    lat_table = lat_tables(lat_count, lon_count).reshape(lat_count, lon_count * slots, H)
    forward_all, inverse_all = [], []
    for a in range(lat_count):
        here = lat_table[:, :, a * rows : (a + 1) * rows]
        ordered = np.concatenate([here[1 - a], here[a]], axis=0)
        forward_all.append(spread8(ordered))
        ordered = np.concatenate([here[a], here[1 - a]], axis=0)
        inverse_all.append(spread8(ordered.T))
    forward_lat = lax.dynamic_index_in_dim(jnp.asarray(np.stack(forward_all)), lat_id, 0, False)
    inverse_lat = lax.dynamic_index_in_dim(jnp.asarray(np.stack(inverse_all)), lat_id, 0, False)
    order = np.arange(W).reshape(lon_count, chunks, chunk_cols).transpose(1, 0, 2).reshape(-1)
    forward_lon, inverse_lon = (jnp.asarray(t) for t in lon_tables(order))

    received = []
    for i in range(chunks):
        raw = patches[:, i * chunk_cols : (i + 1) * chunk_cols].astype(F32)
        center = jnp.mean(raw, axis=-1)
        off = raw - center[..., None]
        square = jnp.sum(off * off, axis=-1)
        theirs = swap(jnp.stack([center, square]), "ch")
        mean = 0.5 * (center + theirs[0])
        gap = center - theirs[0]
        spread = (square + theirs[1]) / C + 0.25 * gap * gap
        scale = lax.rsqrt(spread + norm_epsilon)
        prenormed = (
            (raw - mean[..., None]) * scale[..., None] * filter_norm_gain.astype(F32)
            + filter_norm_bias.astype(F32)
        ).astype(BF)
        send, keep = lat_forward(prenormed, forward_lat)
        total = (keep.astype(F32) + swap(send, "lat").astype(F32)).astype(BF)
        received.append(
            lax.all_to_all(
                total.reshape(lon_count, slots, chunk_cols, width), "lon", 0, 0, tiled=True
            )
        )

    w_in = block_diagonal(filter_in)
    w_out = block_diagonal(filter_out)
    b_in = filter_in_bias.reshape(1, -1).astype(F32)
    b_out = filter_out_bias.reshape(1, -1).astype(F32)
    lat_keep = jnp.tile(jnp.repeat(kept_lat, block_width), 2).reshape(1, -1)
    lon_keep = jnp.tile(jnp.repeat(kept_lon, block_width), 2).reshape(1, -1)
    first_pair = ((lat_id * lon_count + lon_id) * pairs).astype(jnp.int32).reshape(1)
    filtered = modes(
        received, first_pair, lat_keep, lon_keep, forward_lon, inverse_lon, w_in, b_in, w_out, b_out
    )

    m_in = jnp.concatenate([dense_in, swap(dense_in, "ch")], axis=1)
    m_in_bias = jnp.concatenate([dense_in_bias, swap(dense_in_bias, "ch")]).astype(F32)[None]
    m_out = jnp.concatenate([dense_out, swap(dense_out, "ch")], axis=0)
    m_out_bias = lax.all_gather(dense_out_bias, "ch", axis=0, tiled=True).astype(F32)[None]
    gain = norm_gain.astype(F32)[None]
    bias = norm_bias.astype(F32)[None]
    flag = ch_id.astype(jnp.int32).reshape(1)

    pieces = []
    for i in range(chunks):
        own = lax.all_to_all(filtered[i], "lon", 0, 0, tiled=True)
        other = swap(own, "lat")
        mixed = lat_inverse(own, other, inverse_lat, patches, i * chunk_cols // 16)
        halves = mixed.reshape(lon_count, 2, band_rows // 2, chunk_cols, width)
        mine = lax.dynamic_index_in_dim(halves, ch_id, 1, False)
        sent = lax.dynamic_index_in_dim(halves, 1 - ch_id, 1, False)
        done = mlp(
            flag, mine, swap(sent, "ch"), gain, bias, m_in, m_in_bias, m_out, m_out_bias
        )
        pieces.append(
            lax.all_to_all(
                done.reshape(lon_count * 2, band_rows // 2, chunk_cols, width),
                ("lon", "ch"), 0, 0, tiled=True,
            ).reshape(lon_count, 2, band_rows // 2, chunk_cols, width)
        )
    result = jnp.stack(pieces).transpose(2, 3, 1, 0, 4, 5)
    return result.reshape(1, 1, band_rows, lon_count * cols, width)


def lon_forward(number, length):
    freq_ids = jnp.arange(number, dtype=jnp.int32)
    cell_ids = jnp.arange(length, dtype=jnp.int32)
    phase_turns = cell_ids[:, None] * freq_ids[None, :] % length
    angles = phase_turns.astype(jnp.float32) * (2.0 * math.pi / length)
    factor = 1.0 / math.sqrt(length)
    return jnp.stack([jnp.cos(angles) * factor, -jnp.sin(angles) * factor], axis=1).astype(
        jnp.bfloat16
    )


def lon_inverse(freq_ids, length):
    cell_ids = jnp.arange(length, dtype=jnp.int32)
    phase_turns = freq_ids[:, None] * cell_ids[None, :] % length
    angles = phase_turns.astype(jnp.float32) * (2.0 * math.pi / length)
    factor = 1.0 / math.sqrt(length)
    weight = jnp.where(freq_ids == 0, 1.0, 2.0).astype(jnp.float32)[:, None]
    return jnp.stack(
        [jnp.cos(angles) * factor * weight, -jnp.sin(angles) * factor * weight]
    ).astype(jnp.bfloat16)


def band_ids(half_band, length):
    slot_ids = jnp.arange(2 * half_band, dtype=jnp.int32)
    return jnp.where(slot_ids < half_band, slot_ids, slot_ids + length - 2 * half_band)


def lat_forward_table(row_ids, half_band, length):
    phase_turns = band_ids(half_band, length)[:, None] * row_ids[None, :] % length
    angles = phase_turns.astype(jnp.float32) * (2.0 * math.pi / length)
    factor = 1.0 / math.sqrt(length)
    cosine = jnp.cos(angles) * factor
    sine_part = jnp.sin(angles) * factor
    upper_half = jnp.concatenate([cosine, sine_part], axis=1)
    bottom = jnp.concatenate([-sine_part, cosine], axis=1)
    return jnp.concatenate([upper_half, bottom], axis=0).astype(jnp.bfloat16)


def lat_inverse_table(row_ids, half_band, length):
    phase_turns = row_ids[:, None] * band_ids(half_band, length)[None, :] % length
    angles = phase_turns.astype(jnp.float32) * (2.0 * math.pi / length)
    factor = 1.0 / math.sqrt(length)
    cosine = jnp.cos(angles) * factor
    sine_part = jnp.sin(angles) * factor
    upper_half = jnp.concatenate([cosine, -sine_part], axis=1)
    bottom = jnp.concatenate([sine_part, cosine], axis=1)
    return jnp.concatenate([upper_half, bottom], axis=0).astype(jnp.bfloat16)


def complex_layer(values, weight, offset):
    products = jnp.einsum("tjkbc,ubcd->tujkbd", values, weight, preferred_element_type=jnp.float32)
    offset = offset.astype(jnp.float32)
    real_part = products[0, 0] - products[1, 1] + offset[0]
    imag_part = products[1, 0] + products[0, 1] + offset[1]
    return jnp.stack([real_part, imag_part])


def channel_mlp(mixed_full, norm_gain, norm_bias, weight_in, bias_in, weight_out):
    wide = mixed_full.astype(jnp.float32)
    center = jnp.mean(wide, axis=-1, keepdims=True)
    spread = jnp.mean((wide - center) ** 2, axis=-1, keepdims=True)
    normed = (
        (wide - center) * lax.rsqrt(spread + norm_epsilon) * norm_gain.astype(jnp.float32)
        + norm_bias.astype(jnp.float32)
    ).astype(jnp.bfloat16)
    hidden = jnp.einsum("rwc,cu->rwu", normed, weight_in, preferred_element_type=jnp.float32)
    hidden = jax.nn.gelu(hidden + bias_in.astype(jnp.float32), approximate=False).astype(
        jnp.bfloat16
    )
    return jnp.einsum("rwu,uc->rwc", hidden, weight_out, preferred_element_type=jnp.float32)


def row_plan(
    patches,
    filter_norm_gain,
    filter_norm_bias,
    filter_in,
    filter_in_bias,
    filter_out,
    filter_out_bias,
    kept_lat,
    kept_lon,
    norm_gain,
    norm_bias,
    dense_in,
    dense_in_bias,
    dense_out,
    dense_out_bias,
):
    lon_count = lax.axis_size("lon")
    lat_count = lax.axis_size("lat")
    band_rows = patches.shape[0] // lon_count
    local_channels = patches.shape[2]
    local_blocks = filter_in.shape[1]
    block_width = filter_in.shape[2]
    row_span = lon_count * band_rows
    local_freqs = KEEP_LON // (lon_count * lat_count)
    local_rows = lax.all_to_all(patches, "lon", split_axis=0, concat_axis=1, tiled=True)
    raw = local_rows.astype(jnp.float32)
    cell_total = lax.psum(jnp.sum(raw, axis=-1, keepdims=True), "ch")
    pre_center = cell_total / C
    centered = raw - pre_center
    square_total = lax.psum(jnp.sum(centered * centered, axis=-1, keepdims=True), "ch")
    pre_spread = square_total / C
    prenormed = (
        centered * lax.rsqrt(pre_spread + norm_epsilon) * filter_norm_gain.astype(jnp.float32)
        + filter_norm_bias.astype(jnp.float32)
    ).astype(jnp.bfloat16)
    spectrum = jnp.einsum(
        "rwc,wtk->trkc", prenormed, lon_forward(KEEP_LON, W), preferred_element_type=jnp.float32
    )
    spectrum = spectrum.astype(jnp.bfloat16)
    slot_ids = jnp.arange(H, dtype=jnp.int32)
    group_ids = slot_ids // band_rows
    direct_rows = (
        group_ids % lat_count * row_span + group_ids // lat_count * band_rows + slot_ids % band_rows
    )
    pencil = lax.all_to_all(spectrum, ("lon", "lat"), split_axis=2, concat_axis=1, tiled=True)
    banded = jnp.dot(
        lat_forward_table(direct_rows, MLAT, H),
        pencil.reshape(2 * H, -1),
        preferred_element_type=jnp.float32,
    )
    banded = banded.astype(jnp.bfloat16).reshape(
        2, 2 * MLAT, local_freqs, local_blocks, block_width
    )
    first = complex_layer(banded, filter_in, filter_in_bias.reshape(2, local_blocks, block_width))
    first = jnp.maximum(first, 0.0).astype(jnp.bfloat16)
    second = complex_layer(first, filter_out, filter_out_bias.reshape(2, local_blocks, block_width))
    shrunk = jnp.sign(second) * jnp.maximum(jnp.abs(second) - shrink_level, 0.0)
    column_ids = (
        lax.axis_index("lon") * lat_count + lax.axis_index("lat")
    ) * local_freqs + jnp.arange(local_freqs, dtype=jnp.int32)
    band_slots = jnp.arange(2 * MLAT, dtype=jnp.int32)
    signed_band = jnp.where(band_slots < MLAT, band_slots, band_slots - 2 * MLAT)
    lat_ok = (signed_band[:, None] >= -kept_lat[None, :]) & (
        signed_band[:, None] < kept_lat[None, :]
    )
    lon_ok = column_ids[:, None] < kept_lon[None, :]
    keep_mask = (lat_ok[:, None, :] & lon_ok[None, :, :]).astype(jnp.float32)[..., None]
    kept_modes = (shrunk * keep_mask).astype(jnp.bfloat16).reshape(4 * MLAT, -1)
    spatial = jnp.dot(
        lat_inverse_table(direct_rows, MLAT, H), kept_modes, preferred_element_type=jnp.float32
    )
    spatial = spatial.astype(jnp.bfloat16).reshape(2, H, local_freqs, local_channels)
    returned = lax.all_to_all(spatial, ("lon", "lat"), split_axis=1, concat_axis=2, tiled=True)
    back_freqs = jnp.arange(KEEP_LON, dtype=jnp.int32)
    fine_part = jnp.einsum(
        "trkc,tkw->rwc", returned, lon_inverse(back_freqs, W), preferred_element_type=jnp.float32
    )
    mixed = (raw + fine_part).astype(jnp.bfloat16)
    gathered = lax.all_gather(mixed, "ch", axis=2, tiled=True)
    partial_terms = channel_mlp(gathered, norm_gain, norm_bias, dense_in, dense_in_bias, dense_out)
    summed = lax.psum_scatter(
        partial_terms.astype(jnp.bfloat16), "ch", scatter_dimension=2, tiled=True
    ).astype(jnp.float32)
    result = (mixed.astype(jnp.float32) + summed + dense_out_bias.astype(jnp.float32)).astype(
        jnp.bfloat16
    )
    return result.reshape(1, 1, band_rows, W, local_channels)


def solution(mesh):
    placed = (
        P(("grp", "lat"), "lon", "ch"),
        P("ch"),
        P("ch"),
        P(None, "ch", None, None),
        P(None, "ch"),
        P(None, "ch", None, None),
        P(None, "ch"),
        P("ch"),
        P("ch"),
        P(),
        P(),
        P(None, "ch"),
        P("ch"),
        P("ch", None),
        P("ch"),
    )
    sizes = mesh.shape
    lat_count, lon_count = sizes["lat"], sizes["lon"]
    cols = W // lon_count
    fits = lat_count == 2 and sizes["ch"] == 2 and MLAT % (lat_count * lon_count) == 0
    fits = fits and cols % 32 == 0 and H % (2 * lat_count * lon_count) == 0
    plan = functools.partial(column_plan, 32) if fits else row_plan
    return jax.shard_map(
        plan,
        mesh=mesh,
        in_specs=placed,
        out_specs=P(("grp", "lat"), "lon", None, None, "ch"),
        check_vma=False,
    )
```

```python
import functools
import math

import jax
import jax.numpy as jnp
import numpy as np
from jax import lax
from jax.experimental import pallas as pl
from jax.experimental.pallas import tpu as pltpu
from jax.sharding import PartitionSpec as P

H = 256
W = 384
C = 768
MLAT = 64
KEEP_LON = 128

shrink_level = 0.01
norm_epsilon = 1e-05

COST_SHARE = 1
LATE_SHARE = 8

BF = jnp.bfloat16
F32 = jnp.float32


def angle_table(rows, cols, length):
    phase = rows[:, None] * cols[None, :] % length
    return phase * (2.0 * math.pi / length)


def lat_slots(lat_count, lon_count):
    per = MLAT // (lat_count * lon_count)
    freq, kind = [], []
    for dev in range(lat_count * lon_count):
        for pair in range(dev * per, dev * per + per):
            freq += [0, MLAT] if pair == 0 else [pair, pair]
            kind += [0, 0] if pair == 0 else [0, 1]
        freq.append(MLAT if dev == 0 else 0)
        kind.append(1 if dev == 0 else 2)
    return np.array(freq), np.array(kind)


def lat_tables(lat_count, lon_count):
    freq, kind = lat_slots(lat_count, lon_count)
    angles = angle_table(freq, np.arange(H), H)
    table = np.where(kind[:, None] == 0, np.cos(angles), -np.sin(angles)) / math.sqrt(H)
    table = np.where(kind[:, None] == 2, 0.0, table)
    return table.astype(np.float32)


def lon_tables(order):
    freqs = np.arange(KEEP_LON)
    angles = angle_table(freqs, order, W)
    factor = 1.0 / math.sqrt(W)
    weight = np.where(freqs == 0, 1.0, 2.0)[:, None]
    forward = np.concatenate([np.cos(angles) * factor, -np.sin(angles) * factor], axis=0)
    inverse = np.concatenate(
        [np.cos(angles) * factor * weight, -np.sin(angles) * factor * weight], axis=0
    ).T
    return forward.astype(np.float32).astype(jnp.bfloat16), inverse.astype(np.float32).astype(jnp.bfloat16)


def spread8(table):
    return np.kron(table, np.eye(8, dtype=np.float32)).astype(jnp.bfloat16)


def lat_forward_kernel(where_ref, cells_ref, table_ref, send_ref, keep_ref):
    rows, _, width = cells_ref.shape
    lon_count, slots, _, _ = send_ref.shape
    values = cells_ref[...].astype(F32).reshape(rows, 2, 8, width)
    pair = jnp.concatenate(
        [values[:, 0].reshape(rows * 8, width), values[:, 1].reshape(rows * 8, width)], axis=1
    ).astype(BF)
    half = table_ref.shape[1] // 2
    for part, out_ref in ((0, send_ref), (1, keep_ref)):
        total = jnp.dot(
            table_ref[0, part * half : (part + 1) * half, :], pair, preferred_element_type=F32
        )
        total = jnp.concatenate(
            [
                total[:, :width].reshape(lon_count, slots, 8, width),
                total[:, width:].reshape(lon_count, slots, 8, width),
            ],
            axis=2,
        ).astype(BF)
        for z in range(lon_count):
            out_ref[lax.rem(z + lon_count - where_ref[0], lon_count)] = total[z]


def lat_forward(where, cells, table, lon_count):
    rows, cols, width = cells.shape
    slots = table.shape[1] // (16 * lon_count)
    block = pl.BlockSpec((lon_count, slots, 16, width), lambda i, where: (0, 0, i, 0))
    return pl.pallas_call(
        lat_forward_kernel,
        grid_spec=pltpu.PrefetchScalarGridSpec(
            num_scalar_prefetch=1,
            grid=(cols // 16,),
            in_specs=[
                pl.BlockSpec((rows, 16, width), lambda i, where: (0, i, 0)),
                pl.BlockSpec((1,) + table.shape[1:], lambda i, where: (where[2], 0, 0)),
            ],
            out_specs=[block, block],
        ),
        out_shape=[jax.ShapeDtypeStruct((lon_count, slots, cols, width), BF)] * 2,
        compiler_params=pltpu.CompilerParams(vmem_limit_bytes=40 << 20),
        cost_estimate=pl.CostEstimate(
            flops=2 * table[0].size * cols // 8 * width // COST_SHARE,
            bytes_accessed=4 * rows * cols * width // COST_SHARE,
            transcendentals=0,
        ),
        name="lat_forward",
    )(where, cells, table)


def lat_inverse_kernel(
    where_ref, own_ref, other_ref, table_ref, patches_ref, mine_ref, sent_ref, flat_ref
):
    rows, _, width = patches_ref.shape
    lon_count, slots = own_ref.shape[:2]
    blank = jnp.zeros((flat_ref.shape[1] - slots * 8, 2 * width), BF)
    for side, ref in enumerate((own_ref, other_ref)):
        for s in range(lon_count):
            values = ref[s].astype(F32).reshape(slots, 2, 8, width)
            flat = jnp.concatenate(
                [values[:, 0].reshape(slots * 8, width), values[:, 1].reshape(slots * 8, width)],
                axis=1,
            )
            source = lax.rem(where_ref[0] + (lon_count - s), lon_count)
            flat_ref[side * lon_count + source] = jnp.concatenate([flat.astype(BF), blank], axis=0)
    total = jnp.dot(
        table_ref[0], flat_ref[...].reshape(-1, 2 * width), preferred_element_type=F32
    )
    fine = jnp.concatenate(
        [total[:, :width].reshape(rows, 8, width), total[:, width:].reshape(rows, 8, width)], axis=1
    )
    mixed = (patches_ref[...].astype(F32) + fine).astype(BF)
    mixed = mixed.reshape(lon_count, 2, rows // (2 * lon_count), 16, width)

    @pl.when(where_ref[1] == 0)
    def _():
        mine_ref[...] = mixed[:, 0]
        sent_ref[...] = mixed[:, 1]

    @pl.when(where_ref[1] != 0)
    def _():
        mine_ref[...] = mixed[:, 1]
        sent_ref[...] = mixed[:, 0]


def lat_inverse(where, own, other, table, patches, first_col):
    lon_count, slots, cols, width = own.shape
    rows = patches.shape[0]
    first_block = first_col // 16
    spec = pl.BlockSpec((lon_count, slots, 16, width), lambda i, where: (0, 0, i, 0))
    half = rows // (2 * lon_count)
    out_spec = pl.BlockSpec((lon_count, half, 16, width), lambda i, where: (0, 0, i, 0))
    return pl.pallas_call(
        lat_inverse_kernel,
        grid_spec=pltpu.PrefetchScalarGridSpec(
            num_scalar_prefetch=1,
            grid=(cols // 16,),
            in_specs=[
                spec,
                spec,
                pl.BlockSpec((1,) + table.shape[1:], lambda i, where: (where[2], 0, 0)),
                pl.BlockSpec((rows, 16, width), lambda i, where: (0, first_block + i, 0)),
            ],
            out_specs=[out_spec, out_spec],
            scratch_shapes=[
                pltpu.VMEM((2 * lon_count, table.shape[2] // (2 * lon_count), 2 * width), BF)
            ],
        ),
        out_shape=[jax.ShapeDtypeStruct((lon_count, half, cols, width), BF)] * 2,
        compiler_params=pltpu.CompilerParams(vmem_limit_bytes=40 << 20),
        cost_estimate=pl.CostEstimate(
            flops=2 * table[0].size * cols // 8 * width // LATE_SHARE,
            bytes_accessed=6 * rows * cols * width // LATE_SHARE,
            transcendentals=0,
        ),
        name="lat_inverse",
    )(where, own, other, table, patches)


def modes_kernel(inputs, first_pair_ref, lat_keep_ref, lon_keep_ref, *refs):
    pair_refs = refs[:inputs]
    spare_refs = refs[inputs : 2 * inputs]
    forward_ref, inverse_ref, w_in_ref, b_in_ref, w_out_ref, b_out_ref = refs[
        2 * inputs : 2 * inputs + 6
    ]
    out_refs = refs[2 * inputs + 6 :]
    width = pair_refs[0].shape[-1]
    step = pl.program_id(0)
    pairs = pl.num_programs(0)
    pair_id = first_pair_ref[0] + step
    special = pair_id == 0
    keep = KEEP_LON

    def columns(refs, row):
        return jnp.concatenate([ref[row] for ref in refs], axis=0)

    both = jnp.concatenate([columns(pair_refs, 0), columns(pair_refs, 1)], axis=1)
    spectrum = jnp.dot(forward_ref[...], both, preferred_element_type=F32)
    a_re, a_im = spectrum[:keep, :width], spectrum[keep:, :width]
    b_re, b_im = spectrum[:keep, width:], spectrum[keep:, width:]

    def filtered(plus_re, plus_im, minus_re, minus_im):
        banded = jnp.concatenate(
            [
                jnp.concatenate([plus_re, plus_im], axis=1),
                jnp.concatenate([minus_re, minus_im], axis=1),
            ],
            axis=0,
        ).astype(BF)
        first = jnp.dot(banded, w_in_ref[...], preferred_element_type=F32) + b_in_ref[...]
        first = jnp.maximum(first, 0.0).astype(BF)
        second = jnp.dot(first, w_out_ref[...], preferred_element_type=F32) + b_out_ref[...]
        shrunk = second - jnp.clip(second, -shrink_level, shrink_level)
        freq = lax.broadcasted_iota(jnp.int32, (keep, 2 * width), 0)
        lon_ok = freq < lon_keep_ref[...]
        plus_ok = lon_ok & (pair_id < lat_keep_ref[...])
        minus_id = jnp.where(special, MLAT, pair_id)
        minus_ok = lon_ok & (minus_id <= lat_keep_ref[...])
        plus = jnp.where(plus_ok, shrunk[:keep], 0.0)
        minus = jnp.where(minus_ok, shrunk[keep:], 0.0)
        return plus[:, :width], plus[:, width:], minus[:, :width], minus[:, width:]

    def back(values, row):
        grid_values = jnp.dot(inverse_ref[...], values, preferred_element_type=F32).astype(BF)
        start = 0
        for ref in out_refs:
            cols = ref.shape[1]
            for r in range(grid_values.shape[1] // width):
                ref[row + r] = grid_values[start : start + cols, r * width : (r + 1) * width]
            start += cols

    @pl.when(special)
    def _():
        spare = jnp.dot(forward_ref[...], columns(spare_refs, 0), preferred_element_type=F32)
        e_re, e_im = spare[:keep], spare[keep:]
        p_re, p_im, m_re, m_im = filtered(a_re, a_im, b_re + e_im, b_im - e_re)
        values = jnp.concatenate(
            [jnp.concatenate([p_re, m_re], axis=1), jnp.concatenate([p_im, m_im], axis=1)], axis=0
        ).astype(BF)
        back(values, 2 * step)
        back(jnp.concatenate([-m_im, m_re], axis=0).astype(BF), 2 * pairs)

    @pl.when(jnp.logical_not(special))
    def _():
        p_re, p_im, m_re, m_im = filtered(a_re - b_im, a_im + b_re, a_re + b_im, a_im - b_re)
        values = jnp.concatenate(
            [
                jnp.concatenate([p_re + m_re, p_im - m_im], axis=1),
                jnp.concatenate([p_im + m_im, m_re - p_re], axis=1),
            ],
            axis=0,
        ).astype(BF)
        back(values, 2 * step)

    @pl.when(jnp.logical_and(step == 0, jnp.logical_not(special)))
    def _():
        for ref in out_refs:
            ref[2 * pairs] = jnp.zeros(ref.shape[1:], BF)


def modes(received, first_pair, lat_keep, lon_keep, forward, inverse, w_in, b_in, w_out, b_out):
    lon_count = len(received[0])
    flat = [values for chunk in received for values in chunk]
    slots, _, width = flat[0].shape
    pairs = slots // 2
    pair_specs = [pl.BlockSpec((2, r.shape[1], width), lambda i: (i, 0, 0)) for r in flat]
    spare_specs = [pl.BlockSpec((1, r.shape[1], width), lambda i: (slots - 1, 0, 0)) for r in flat]
    whole = lambda array: pl.BlockSpec(array.shape, lambda i: (0,) * array.ndim)
    out = pl.pallas_call(
        functools.partial(modes_kernel, len(flat)),
        grid=(pairs,),
        in_specs=[pl.BlockSpec(memory_space=pltpu.SMEM), whole(lat_keep), whole(lon_keep)]
        + pair_specs
        + spare_specs
        + [whole(forward), whole(inverse), whole(w_in), whole(b_in), whole(w_out), whole(b_out)],
        out_specs=[pl.BlockSpec(r.shape, lambda i: (0, 0, 0)) for r in flat],
        out_shape=[jax.ShapeDtypeStruct(r.shape, BF) for r in flat],
        compiler_params=pltpu.CompilerParams(vmem_limit_bytes=48 << 20),
        cost_estimate=pl.CostEstimate(
            flops=pairs * 2 * (2 * 2 * KEEP_LON * W * 2 * width + 4 * KEEP_LON * 4 * width * width) // COST_SHARE,
            bytes_accessed=4 * slots * W * width // COST_SHARE,
            transcendentals=0,
        ),
        name="modes",
    )(
        first_pair, lat_keep, lon_keep, *flat, *flat,
        forward, inverse, w_in, b_in, w_out, b_out,
    )
    return [list(out[i : i + lon_count]) for i in range(0, len(flat), lon_count)]


def mlp_kernel(
    where_ref, own_ref, other_ref, gain_ref, bias_ref, w_in_ref, b_in_ref, w_out_ref, b_out_ref,
    *out_refs,
):
    _, rows, cols, width = own_ref.shape
    cells = rows * cols
    own = own_ref[0].reshape(cells, width)
    other = other_ref[0].reshape(cells, width)
    flip = where_ref[1] == 1
    low = jnp.where(flip, other, own)
    high = jnp.where(flip, own, other)
    wide = jnp.concatenate([low, high], axis=1).astype(F32)
    center = jnp.mean(wide, axis=1, keepdims=True)
    off = wide - center
    spread = jnp.mean(off * off, axis=1, keepdims=True)
    normed = (off * lax.rsqrt(spread + norm_epsilon) * gain_ref[...] + bias_ref[...]).astype(BF)
    hidden = jnp.dot(normed, w_in_ref[...], preferred_element_type=F32) + b_in_ref[...]
    hidden = (hidden * (0.5 + 0.5 * lax.erf(hidden * math.sqrt(0.5)))).astype(BF)
    total = jnp.dot(hidden, w_out_ref[...], preferred_element_type=F32) + wide + b_out_ref[...]
    total = total.astype(BF)
    low, high = total[:, :width], total[:, width:]
    mine = jnp.where(flip, high, low).reshape(rows, cols, width)
    sent = jnp.where(flip, low, high).reshape(rows, cols, width)
    for s, ref in enumerate(out_refs):

        @pl.when(pl.program_id(0) == s)
        def _():
            ref[0] = mine
            ref[1] = sent


def mlp(where, own, other, gain, bias, w_in, b_in, w_out, b_out):
    lon_count, rows, cols, width = own.shape
    whole = lambda array: pl.BlockSpec(array.shape, lambda i, where: (0,) * array.ndim)
    cell_spec = pl.BlockSpec(
        (1, rows, cols, width), lambda i, where: (lax.rem(where[0] + i, lon_count), 0, 0, 0)
    )
    cells = lon_count * rows * cols
    return pl.pallas_call(
        mlp_kernel,
        grid_spec=pltpu.PrefetchScalarGridSpec(
            num_scalar_prefetch=1,
            grid=(lon_count,),
            in_specs=[cell_spec, cell_spec]
            + [whole(a) for a in (gain, bias, w_in, b_in, w_out, b_out)],
            out_specs=[pl.BlockSpec((2, rows, cols, width), lambda i, where: (0, 0, 0, 0))]
            * lon_count,
        ),
        out_shape=[jax.ShapeDtypeStruct((2, rows, cols, width), BF)] * lon_count,
        compiler_params=pltpu.CompilerParams(vmem_limit_bytes=48 << 20),
        cost_estimate=pl.CostEstimate(
            flops=4 * cells * w_in.size // LATE_SHARE,
            bytes_accessed=8 * cells * width // LATE_SHARE,
            transcendentals=cells * w_in.shape[1] // LATE_SHARE,
        ),
        name="channel_mlp",
    )(where, own, other, gain, bias, w_in, b_in, w_out, b_out)


def assemble_kernel(where_ref, their_ref, *refs):
    my_refs, out_ref = refs[:-1], refs[-1]
    half = their_ref.shape[1]
    flip = where_ref[1] == 1
    for s, ref in enumerate(my_refs):

        @pl.when(pl.program_id(0) == s)
        def _():
            mine, theirs = ref[0], their_ref[0]
            out_ref[:half] = jnp.where(flip, theirs, mine)
            out_ref[half:] = jnp.where(flip, mine, theirs)


def assemble(where, result, mine, theirs, first_col, block_cols):
    lon_count, rows, cols, width = theirs.shape
    block = math.gcd(math.gcd(cols, block_cols), first_col)
    steps = cols // block

    def piece(s):
        def index(g, j, where):
            return 0, 0, jnp.where(g == s, j, jnp.where(g < s, 0, steps - 1)), 0

        return pl.BlockSpec((1, rows, block, width), index)

    def place(g, j, where):
        source = lax.rem(where[0] + (lon_count - g), lon_count)
        return 0, source * (block_cols // block) + first_col // block + j, 0

    specs = [pl.BlockSpec((1, rows, block, width), lambda g, j, where: (g, 0, j, 0))]
    specs += [piece(s) for s in range(lon_count)]
    operands = [where, theirs, *mine]
    aliases = {}
    kernel = assemble_kernel
    if result is not None:
        aliases = {len(operands): 0}
        operands.append(result)
        specs.append(pl.BlockSpec(memory_space=pl.ANY))

        def kernel(where_ref, *refs):
            assemble_kernel(where_ref, *refs[:-2], refs[-1])

    return pl.pallas_call(
        kernel,
        grid_spec=pltpu.PrefetchScalarGridSpec(
            num_scalar_prefetch=1,
            grid=(lon_count, steps),
            in_specs=specs,
            out_specs=pl.BlockSpec((2 * rows, block, width), place),
        ),
        out_shape=jax.ShapeDtypeStruct((2 * rows, lon_count * block_cols, width), BF),
        input_output_aliases=aliases,
        cost_estimate=pl.CostEstimate(
            flops=0, bytes_accessed=8 * lon_count * rows * cols * width, transcendentals=0
        ),
        name="assemble",
    )(*operands)


def block_diagonal(weight):
    blocks, n = weight.shape[1], weight.shape[2]
    eye = jnp.eye(blocks, dtype=weight.dtype)
    spread = (weight[:, :, :, None, :] * eye[None, :, None, :, None]).reshape(
        2, blocks * n, blocks * n
    )
    return jnp.concatenate(
        [
            jnp.concatenate([spread[0], spread[1]], axis=1),
            jnp.concatenate([-spread[1], spread[0]], axis=1),
        ],
        axis=0,
    )


def swap(values, axis):
    return lax.ppermute(values, axis, [(0, 1), (1, 0)])


def shift(values, steps, lon_count):
    if steps == 0:
        return values
    return lax.ppermute(values, "lon", [(z, (z + steps) % lon_count) for z in range(lon_count)])


def column_plan(
    widths,
    patches,
    filter_norm_gain,
    filter_norm_bias,
    filter_in,
    filter_in_bias,
    filter_out,
    filter_out_bias,
    kept_lat,
    kept_lon,
    norm_gain,
    norm_bias,
    dense_in,
    dense_in_bias,
    dense_out,
    dense_out_bias,
):
    lon_count = lax.axis_size("lon")
    lat_count = lax.axis_size("lat")
    rows, cols, width = patches.shape
    chunks = len(widths)
    starts = [sum(widths[:i]) for i in range(chunks)]
    block_width = filter_in.shape[2]
    lat_id = lax.axis_index("lat")
    lon_id = lax.axis_index("lon")
    ch_id = lax.axis_index("ch")
    pairs = MLAT // (lat_count * lon_count)
    slots = 2 * pairs + 1

    lat_table = lat_tables(lat_count, lon_count).reshape(lat_count, lon_count, slots, H)
    forward_all, inverse_all = [], []
    for a in range(lat_count):
        here = lat_table[..., a * rows : (a + 1) * rows]
        ordered = np.concatenate([here[1 - a], here[a]], axis=0).reshape(-1, rows)
        forward_all.append(spread8(ordered))
        ordered = np.concatenate([here[a], here[1 - a]], axis=0)
        ordered = np.pad(ordered, ((0, 0), (0, slots % 2), (0, 0))).reshape(-1, rows)
        inverse_all.append(spread8(ordered.T))
    forward_lat, inverse_lat = jnp.asarray(np.stack(forward_all)), jnp.asarray(np.stack(inverse_all))

    ids = np.arange(W).reshape(lon_count, cols)

    def column_order(devices):
        return np.concatenate([ids[devices, c : c + w].reshape(-1) for c, w in zip(starts, widths)])

    steps = np.arange(lon_count)
    from_here = [lon_tables(column_order((z - steps) % lon_count))[0] for z in range(lon_count)]
    to_there = [lon_tables(column_order((z + steps) % lon_count))[1] for z in range(lon_count)]

    fence = lax.optimization_barrier
    where = jnp.stack([lon_id, ch_id, lat_id]).astype(jnp.int32)

    def row_transform(i, source):
        raw = source[:, starts[i] : starts[i] + widths[i]].astype(F32)
        center = jnp.mean(raw, axis=-1)
        off = raw - center[..., None]
        square = jnp.sum(off * off, axis=-1)
        theirs = swap(jnp.stack([center, square]), "ch")
        mean = 0.5 * (center + theirs[0])
        gap = center - theirs[0]
        spread = (square + theirs[1]) / C + 0.25 * gap * gap
        scale = lax.rsqrt(spread + norm_epsilon)
        prenormed = (
            (raw - mean[..., None]) * scale[..., None] * filter_norm_gain.astype(F32)
            + filter_norm_bias.astype(F32)
        ).astype(BF)
        return lat_forward(where, prenormed, forward_lat, lon_count)

    def mlp_weights(dense_in, dense_in_bias, dense_out, dense_out_bias):
        return (
            norm_gain.astype(F32)[None],
            norm_bias.astype(F32)[None],
            jnp.concatenate([dense_in, swap(dense_in, "ch")], axis=1),
            jnp.concatenate([dense_in_bias, swap(dense_in_bias, "ch")]).astype(F32)[None],
            jnp.concatenate([dense_out, swap(dense_out, "ch")], axis=0),
            lax.all_gather(dense_out_bias, "ch", axis=0, tiled=True).astype(F32)[None],
        )

    def filter_operands():
        return (
            ((lat_id * lon_count + lon_id) * pairs).astype(jnp.int32).reshape(1),
            jnp.tile(jnp.repeat(kept_lat, block_width), 2).reshape(1, -1),
            jnp.tile(jnp.repeat(kept_lon, block_width), 2).reshape(1, -1),
            lax.dynamic_index_in_dim(jnp.asarray(np.stack(from_here)), lon_id, 0, False),
            lax.dynamic_index_in_dim(jnp.asarray(np.stack(to_there)), lon_id, 0, False),
            block_diagonal(filter_in),
            filter_in_bias.reshape(1, -1).astype(F32),
            block_diagonal(filter_out),
            filter_out_bias.reshape(1, -1).astype(F32),
        )

    def along_lon(values):
        return [shift(values[s], s, lon_count) for s in range(lon_count)]

    def row_result(i, own, other):
        mine, sent = lat_inverse(where, own, other, inverse_lat, patches, starts[i])
        return mlp(where, mine, swap(sent, "ch"), *weights)

    def placed(result, i, pieces):
        theirs = swap(jnp.stack([piece[1] for piece in pieces]), "ch")
        return assemble(where, result, pieces, theirs, starts[i], cols)

    received, summed, sent, kept = [], None, None, None
    weights = None
    filter_args = None
    dense = (dense_in, dense_in_bias, dense_out, dense_out_bias)
    for step in range(chunks + 2):
        arrived = None
        if sent is not None:
            arrived = (kept, swap(sent, "lat"))
            sent = None
        if summed is not None:
            received.append(along_lon(summed))
            summed = None
        if step < chunks:
            sent, kept = row_transform(step, patches)
        elif step == chunks:
            filter_args = filter_operands()
        else:
            weights = mlp_weights(*dense)
        patches, arrived, sent, kept, received, filter_args, weights, dense = fence(
            (patches, arrived, sent, kept, received, filter_args, weights, dense)
        )
        if arrived is not None:
            summed = [
                (arrived[0][s].astype(F32) + arrived[1][s].astype(F32)).astype(BF)
                for s in range(lon_count)
            ]

    filtered = modes(received, *filter_args)

    owns = [None] * chunks
    others = [None] * chunks
    outputs = [None] * chunks
    for step in range(chunks):
        owns[step] = along_lon(filtered[step])
        if step >= 1:
            owns[step - 1] = jnp.stack(owns[step - 1])
            others[step - 1] = swap(owns[step - 1], "lat")
        if step >= 2:
            outputs[step - 2] = row_result(step - 2, owns[step - 2], others[step - 2])
        patches, filtered, owns, others, outputs = fence((patches, filtered, owns, others, outputs))

    result = None
    pieces = None
    for i in range(chunks):
        last = pieces
        pieces = along_lon(outputs[i])
        if last is not None:
            result = placed(result, i - 1, last)
        for later in (i + 1, i + 2):
            if later < chunks and outputs[later] is None:
                if others[later] is None:
                    owns[later] = jnp.stack(owns[later])
                    others[later] = swap(owns[later], "lat")
                outputs[later] = row_result(later, owns[later], others[later])
        patches, owns, others, outputs, pieces, result = fence(
            (patches, owns, others, outputs, pieces, result)
        )
    result = placed(result, chunks - 1, pieces)
    return result.reshape(1, 1, rows // lon_count, lon_count * cols, width)


def lon_forward(number, length):
    freq_ids = jnp.arange(number, dtype=jnp.int32)
    cell_ids = jnp.arange(length, dtype=jnp.int32)
    phase_turns = cell_ids[:, None] * freq_ids[None, :] % length
    angles = phase_turns.astype(jnp.float32) * (2.0 * math.pi / length)
    factor = 1.0 / math.sqrt(length)
    return jnp.stack([jnp.cos(angles) * factor, -jnp.sin(angles) * factor], axis=1).astype(
        jnp.bfloat16
    )


def lon_inverse(freq_ids, length):
    cell_ids = jnp.arange(length, dtype=jnp.int32)
    phase_turns = freq_ids[:, None] * cell_ids[None, :] % length
    angles = phase_turns.astype(jnp.float32) * (2.0 * math.pi / length)
    factor = 1.0 / math.sqrt(length)
    weight = jnp.where(freq_ids == 0, 1.0, 2.0).astype(jnp.float32)[:, None]
    return jnp.stack(
        [jnp.cos(angles) * factor * weight, -jnp.sin(angles) * factor * weight]
    ).astype(jnp.bfloat16)


def band_ids(half_band, length):
    slot_ids = jnp.arange(2 * half_band, dtype=jnp.int32)
    return jnp.where(slot_ids < half_band, slot_ids, slot_ids + length - 2 * half_band)


def lat_forward_table(row_ids, half_band, length):
    phase_turns = band_ids(half_band, length)[:, None] * row_ids[None, :] % length
    angles = phase_turns.astype(jnp.float32) * (2.0 * math.pi / length)
    factor = 1.0 / math.sqrt(length)
    cosine = jnp.cos(angles) * factor
    sine_part = jnp.sin(angles) * factor
    upper_half = jnp.concatenate([cosine, sine_part], axis=1)
    bottom = jnp.concatenate([-sine_part, cosine], axis=1)
    return jnp.concatenate([upper_half, bottom], axis=0).astype(jnp.bfloat16)


def lat_inverse_table(row_ids, half_band, length):
    phase_turns = row_ids[:, None] * band_ids(half_band, length)[None, :] % length
    angles = phase_turns.astype(jnp.float32) * (2.0 * math.pi / length)
    factor = 1.0 / math.sqrt(length)
    cosine = jnp.cos(angles) * factor
    sine_part = jnp.sin(angles) * factor
    upper_half = jnp.concatenate([cosine, -sine_part], axis=1)
    bottom = jnp.concatenate([sine_part, cosine], axis=1)
    return jnp.concatenate([upper_half, bottom], axis=0).astype(jnp.bfloat16)


def complex_layer(values, weight, offset):
    products = jnp.einsum("tjkbc,ubcd->tujkbd", values, weight, preferred_element_type=jnp.float32)
    offset = offset.astype(jnp.float32)
    real_part = products[0, 0] - products[1, 1] + offset[0]
    imag_part = products[1, 0] + products[0, 1] + offset[1]
    return jnp.stack([real_part, imag_part])


def channel_mlp(mixed_full, norm_gain, norm_bias, weight_in, bias_in, weight_out):
    wide = mixed_full.astype(jnp.float32)
    center = jnp.mean(wide, axis=-1, keepdims=True)
    spread = jnp.mean((wide - center) ** 2, axis=-1, keepdims=True)
    normed = (
        (wide - center) * lax.rsqrt(spread + norm_epsilon) * norm_gain.astype(jnp.float32)
        + norm_bias.astype(jnp.float32)
    ).astype(jnp.bfloat16)
    hidden = jnp.einsum("rwc,cu->rwu", normed, weight_in, preferred_element_type=jnp.float32)
    hidden = jax.nn.gelu(hidden + bias_in.astype(jnp.float32), approximate=False).astype(
        jnp.bfloat16
    )
    return jnp.einsum("rwu,uc->rwc", hidden, weight_out, preferred_element_type=jnp.float32)


def row_plan(
    patches,
    filter_norm_gain,
    filter_norm_bias,
    filter_in,
    filter_in_bias,
    filter_out,
    filter_out_bias,
    kept_lat,
    kept_lon,
    norm_gain,
    norm_bias,
    dense_in,
    dense_in_bias,
    dense_out,
    dense_out_bias,
):
    lon_count = lax.axis_size("lon")
    lat_count = lax.axis_size("lat")
    band_rows = patches.shape[0] // lon_count
    local_channels = patches.shape[2]
    local_blocks = filter_in.shape[1]
    block_width = filter_in.shape[2]
    row_span = lon_count * band_rows
    local_freqs = KEEP_LON // (lon_count * lat_count)
    local_rows = lax.all_to_all(patches, "lon", split_axis=0, concat_axis=1, tiled=True)
    raw = local_rows.astype(jnp.float32)
    cell_total = lax.psum(jnp.sum(raw, axis=-1, keepdims=True), "ch")
    pre_center = cell_total / C
    centered = raw - pre_center
    square_total = lax.psum(jnp.sum(centered * centered, axis=-1, keepdims=True), "ch")
    pre_spread = square_total / C
    prenormed = (
        centered * lax.rsqrt(pre_spread + norm_epsilon) * filter_norm_gain.astype(jnp.float32)
        + filter_norm_bias.astype(jnp.float32)
    ).astype(jnp.bfloat16)
    spectrum = jnp.einsum(
        "rwc,wtk->trkc", prenormed, lon_forward(KEEP_LON, W), preferred_element_type=jnp.float32
    )
    spectrum = spectrum.astype(jnp.bfloat16)
    slot_ids = jnp.arange(H, dtype=jnp.int32)
    group_ids = slot_ids // band_rows
    direct_rows = (
        group_ids % lat_count * row_span + group_ids // lat_count * band_rows + slot_ids % band_rows
    )
    pencil = lax.all_to_all(spectrum, ("lon", "lat"), split_axis=2, concat_axis=1, tiled=True)
    banded = jnp.dot(
        lat_forward_table(direct_rows, MLAT, H),
        pencil.reshape(2 * H, -1),
        preferred_element_type=jnp.float32,
    )
    banded = banded.astype(jnp.bfloat16).reshape(
        2, 2 * MLAT, local_freqs, local_blocks, block_width
    )
    first = complex_layer(banded, filter_in, filter_in_bias.reshape(2, local_blocks, block_width))
    first = jnp.maximum(first, 0.0).astype(jnp.bfloat16)
    second = complex_layer(first, filter_out, filter_out_bias.reshape(2, local_blocks, block_width))
    shrunk = jnp.sign(second) * jnp.maximum(jnp.abs(second) - shrink_level, 0.0)
    column_ids = (
        lax.axis_index("lon") * lat_count + lax.axis_index("lat")
    ) * local_freqs + jnp.arange(local_freqs, dtype=jnp.int32)
    band_slots = jnp.arange(2 * MLAT, dtype=jnp.int32)
    signed_band = jnp.where(band_slots < MLAT, band_slots, band_slots - 2 * MLAT)
    lat_ok = (signed_band[:, None] >= -kept_lat[None, :]) & (
        signed_band[:, None] < kept_lat[None, :]
    )
    lon_ok = column_ids[:, None] < kept_lon[None, :]
    keep_mask = (lat_ok[:, None, :] & lon_ok[None, :, :]).astype(jnp.float32)[..., None]
    kept_modes = (shrunk * keep_mask).astype(jnp.bfloat16).reshape(4 * MLAT, -1)
    spatial = jnp.dot(
        lat_inverse_table(direct_rows, MLAT, H), kept_modes, preferred_element_type=jnp.float32
    )
    spatial = spatial.astype(jnp.bfloat16).reshape(2, H, local_freqs, local_channels)
    returned = lax.all_to_all(spatial, ("lon", "lat"), split_axis=1, concat_axis=2, tiled=True)
    back_freqs = jnp.arange(KEEP_LON, dtype=jnp.int32)
    fine_part = jnp.einsum(
        "trkc,tkw->rwc", returned, lon_inverse(back_freqs, W), preferred_element_type=jnp.float32
    )
    mixed = (raw + fine_part).astype(jnp.bfloat16)
    gathered = lax.all_gather(mixed, "ch", axis=2, tiled=True)
    partial_terms = channel_mlp(gathered, norm_gain, norm_bias, dense_in, dense_in_bias, dense_out)
    summed = lax.psum_scatter(
        partial_terms.astype(jnp.bfloat16), "ch", scatter_dimension=2, tiled=True
    ).astype(jnp.float32)
    result = (mixed.astype(jnp.float32) + summed + dense_out_bias.astype(jnp.float32)).astype(
        jnp.bfloat16
    )
    return result.reshape(1, 1, band_rows, W, local_channels)


def solution(mesh):
    placed = (
        P(("grp", "lat"), "lon", "ch"),
        P("ch"),
        P("ch"),
        P(None, "ch", None, None),
        P(None, "ch"),
        P(None, "ch", None, None),
        P(None, "ch"),
        P("ch"),
        P("ch"),
        P(),
        P(),
        P(None, "ch"),
        P("ch"),
        P("ch", None),
        P("ch"),
    )
    sizes = mesh.shape
    lat_count, lon_count = sizes["lat"], sizes["lon"]
    cols = W // lon_count
    fits = lat_count == 2 and sizes["ch"] == 2 and MLAT % (lat_count * lon_count) == 0
    fits = fits and cols == 96 and H % (2 * lat_count * lon_count) == 0
    plan = functools.partial(column_plan, (32, 32, 32)) if fits else row_plan
    return jax.shard_map(
        plan,
        mesh=mesh,
        in_specs=placed,
        out_specs=P(("grp", "lat"), "lon", None, None, "ch"),
        check_vma=False,
    )
```

```python
import functools
import math

import jax
import jax.numpy as jnp
import numpy as np
from jax import lax
from jax.experimental import pallas as pl
from jax.experimental.pallas import tpu as pltpu
from jax.sharding import PartitionSpec as P

H = 256
W = 384
C = 768
MLAT = 64
KEEP_LON = 128

shrink_level = 0.01
norm_epsilon = 1e-05

COST_SHARE = 1
LATE_SHARE = 1

BF = jnp.bfloat16
F32 = jnp.float32


def angle_table(rows, cols, length):
    phase = rows[:, None] * cols[None, :] % length
    return phase * (2.0 * math.pi / length)


def lat_slots(lat_count, lon_count):
    per = MLAT // (lat_count * lon_count)
    freq, kind = [], []
    for dev in range(lat_count * lon_count):
        for pair in range(dev * per, dev * per + per):
            freq += [0, MLAT] if pair == 0 else [pair, pair]
            kind += [0, 0] if pair == 0 else [0, 1]
        freq.append(MLAT if dev == 0 else 0)
        kind.append(1 if dev == 0 else 2)
    return np.array(freq), np.array(kind)


def lat_tables(lat_count, lon_count):
    freq, kind = lat_slots(lat_count, lon_count)
    angles = angle_table(freq, np.arange(H), H)
    table = np.where(kind[:, None] == 0, np.cos(angles), -np.sin(angles)) / math.sqrt(H)
    table = np.where(kind[:, None] == 2, 0.0, table)
    return table.astype(np.float32)


def lon_tables(order):
    freqs = np.arange(KEEP_LON)
    angles = angle_table(freqs, order, W)
    factor = 1.0 / math.sqrt(W)
    weight = np.where(freqs == 0, 1.0, 2.0)[:, None]
    forward = np.concatenate([np.cos(angles) * factor, -np.sin(angles) * factor], axis=0)
    inverse = np.concatenate(
        [np.cos(angles) * factor * weight, -np.sin(angles) * factor * weight], axis=0
    ).T
    return forward.astype(np.float32).astype(jnp.bfloat16), inverse.astype(np.float32).astype(jnp.bfloat16)


def spread8(table):
    return np.kron(table, np.eye(8, dtype=np.float32)).astype(jnp.bfloat16)


def lat_forward_kernel(where_ref, cells_ref, table_ref, send_ref, keep_ref):
    rows, _, width = cells_ref.shape
    lon_count, slots, _, _ = send_ref.shape
    values = cells_ref[...].astype(F32).reshape(rows, 2, 8, width)
    pair = jnp.concatenate(
        [values[:, 0].reshape(rows * 8, width), values[:, 1].reshape(rows * 8, width)], axis=1
    ).astype(BF)
    half = table_ref.shape[1] // 2
    for part, out_ref in ((0, send_ref), (1, keep_ref)):
        total = jnp.dot(
            table_ref[0, part * half : (part + 1) * half, :], pair, preferred_element_type=F32
        )
        total = jnp.concatenate(
            [
                total[:, :width].reshape(lon_count, slots, 8, width),
                total[:, width:].reshape(lon_count, slots, 8, width),
            ],
            axis=2,
        ).astype(BF)
        for z in range(lon_count):
            out_ref[lax.rem(z + lon_count - where_ref[0], lon_count)] = total[z]


def lat_forward(where, cells, table, lon_count):
    rows, cols, width = cells.shape
    slots = table.shape[1] // (16 * lon_count)
    block = pl.BlockSpec((lon_count, slots, 16, width), lambda i, where: (0, 0, i, 0))
    return pl.pallas_call(
        lat_forward_kernel,
        grid_spec=pltpu.PrefetchScalarGridSpec(
            num_scalar_prefetch=1,
            grid=(cols // 16,),
            in_specs=[
                pl.BlockSpec((rows, 16, width), lambda i, where: (0, i, 0)),
                pl.BlockSpec((1,) + table.shape[1:], lambda i, where: (where[2], 0, 0)),
            ],
            out_specs=[block, block],
        ),
        out_shape=[jax.ShapeDtypeStruct((lon_count, slots, cols, width), BF)] * 2,
        compiler_params=pltpu.CompilerParams(vmem_limit_bytes=40 << 20),
        cost_estimate=pl.CostEstimate(
            flops=2 * table[0].size * cols // 8 * width // COST_SHARE,
            bytes_accessed=4 * rows * cols * width // COST_SHARE,
            transcendentals=0,
        ),
        name="lat_forward",
    )(where, cells, table)


def lat_inverse_kernel(
    where_ref, own_ref, other_ref, table_ref, patches_ref, mine_ref, sent_ref, flat_ref
):
    rows, _, width = patches_ref.shape
    lon_count, slots = own_ref.shape[:2]
    blank = jnp.zeros((flat_ref.shape[1] - slots * 8, 2 * width), BF)
    for side, ref in enumerate((own_ref, other_ref)):
        for s in range(lon_count):
            values = ref[s].astype(F32).reshape(slots, 2, 8, width)
            flat = jnp.concatenate(
                [values[:, 0].reshape(slots * 8, width), values[:, 1].reshape(slots * 8, width)],
                axis=1,
            )
            source = lax.rem(where_ref[0] + (lon_count - s), lon_count)
            flat_ref[side * lon_count + source] = jnp.concatenate([flat.astype(BF), blank], axis=0)
    total = jnp.dot(
        table_ref[0], flat_ref[...].reshape(-1, 2 * width), preferred_element_type=F32
    )
    fine = jnp.concatenate(
        [total[:, :width].reshape(rows, 8, width), total[:, width:].reshape(rows, 8, width)], axis=1
    )
    mixed = (patches_ref[...].astype(F32) + fine).astype(BF)
    mixed = mixed.reshape(lon_count, 2, rows // (2 * lon_count), 16, width)

    @pl.when(where_ref[1] == 0)
    def _():
        mine_ref[...] = mixed[:, 0]
        sent_ref[...] = mixed[:, 1]

    @pl.when(where_ref[1] != 0)
    def _():
        mine_ref[...] = mixed[:, 1]
        sent_ref[...] = mixed[:, 0]


def lat_inverse(where, own, other, table, patches, first_col):
    lon_count, slots, cols, width = own.shape
    rows = patches.shape[0]
    first_block = first_col // 16
    spec = pl.BlockSpec((lon_count, slots, 16, width), lambda i, where: (0, 0, i, 0))
    half = rows // (2 * lon_count)
    out_spec = pl.BlockSpec((lon_count, half, 16, width), lambda i, where: (0, 0, i, 0))
    return pl.pallas_call(
        lat_inverse_kernel,
        grid_spec=pltpu.PrefetchScalarGridSpec(
            num_scalar_prefetch=1,
            grid=(cols // 16,),
            in_specs=[
                spec,
                spec,
                pl.BlockSpec((1,) + table.shape[1:], lambda i, where: (where[2], 0, 0)),
                pl.BlockSpec((rows, 16, width), lambda i, where: (0, first_block + i, 0)),
            ],
            out_specs=[out_spec, out_spec],
            scratch_shapes=[
                pltpu.VMEM((2 * lon_count, table.shape[2] // (2 * lon_count), 2 * width), BF)
            ],
        ),
        out_shape=[jax.ShapeDtypeStruct((lon_count, half, cols, width), BF)] * 2,
        compiler_params=pltpu.CompilerParams(vmem_limit_bytes=40 << 20),
        cost_estimate=pl.CostEstimate(
            flops=2 * table[0].size * cols // 8 * width // LATE_SHARE,
            bytes_accessed=6 * rows * cols * width // LATE_SHARE,
            transcendentals=0,
        ),
        name="lat_inverse",
    )(where, own, other, table, patches)


def modes_kernel(inputs, first_pair_ref, lat_keep_ref, lon_keep_ref, *refs):
    pair_refs = refs[:inputs]
    spare_refs = refs[inputs : 2 * inputs]
    forward_ref, inverse_ref, w_in_ref, b_in_ref, w_out_ref, b_out_ref = refs[
        2 * inputs : 2 * inputs + 6
    ]
    out_refs = refs[2 * inputs + 6 :]
    width = pair_refs[0].shape[-1]
    step = pl.program_id(0)
    pairs = pl.num_programs(0)
    pair_id = first_pair_ref[0] + step
    special = pair_id == 0
    keep = KEEP_LON

    def columns(refs, row):
        return jnp.concatenate([ref[row] for ref in refs], axis=0)

    both = jnp.concatenate([columns(pair_refs, 0), columns(pair_refs, 1)], axis=1)
    spectrum = jnp.dot(forward_ref[...], both, preferred_element_type=F32)
    a_re, a_im = spectrum[:keep, :width], spectrum[keep:, :width]
    b_re, b_im = spectrum[:keep, width:], spectrum[keep:, width:]

    def filtered(plus_re, plus_im, minus_re, minus_im):
        banded = jnp.concatenate(
            [
                jnp.concatenate([plus_re, plus_im], axis=1),
                jnp.concatenate([minus_re, minus_im], axis=1),
            ],
            axis=0,
        ).astype(BF)
        first = jnp.dot(banded, w_in_ref[...], preferred_element_type=F32) + b_in_ref[...]
        first = jnp.maximum(first, 0.0).astype(BF)
        second = jnp.dot(first, w_out_ref[...], preferred_element_type=F32) + b_out_ref[...]
        shrunk = second - jnp.clip(second, -shrink_level, shrink_level)
        freq = lax.broadcasted_iota(jnp.int32, (keep, 2 * width), 0)
        lon_ok = freq < lon_keep_ref[...]
        plus_ok = lon_ok & (pair_id < lat_keep_ref[...])
        minus_id = jnp.where(special, MLAT, pair_id)
        minus_ok = lon_ok & (minus_id <= lat_keep_ref[...])
        plus = jnp.where(plus_ok, shrunk[:keep], 0.0)
        minus = jnp.where(minus_ok, shrunk[keep:], 0.0)
        return plus[:, :width], plus[:, width:], minus[:, :width], minus[:, width:]

    def back(values, row):
        grid_values = jnp.dot(inverse_ref[...], values, preferred_element_type=F32).astype(BF)
        start = 0
        for ref in out_refs:
            cols = ref.shape[1]
            for r in range(grid_values.shape[1] // width):
                ref[row + r] = grid_values[start : start + cols, r * width : (r + 1) * width]
            start += cols

    @pl.when(special)
    def _():
        spare = jnp.dot(forward_ref[...], columns(spare_refs, 0), preferred_element_type=F32)
        e_re, e_im = spare[:keep], spare[keep:]
        p_re, p_im, m_re, m_im = filtered(a_re, a_im, b_re + e_im, b_im - e_re)
        values = jnp.concatenate(
            [jnp.concatenate([p_re, m_re], axis=1), jnp.concatenate([p_im, m_im], axis=1)], axis=0
        ).astype(BF)
        back(values, 2 * step)
        back(jnp.concatenate([-m_im, m_re], axis=0).astype(BF), 2 * pairs)

    @pl.when(jnp.logical_not(special))
    def _():
        p_re, p_im, m_re, m_im = filtered(a_re - b_im, a_im + b_re, a_re + b_im, a_im - b_re)
        values = jnp.concatenate(
            [
                jnp.concatenate([p_re + m_re, p_im - m_im], axis=1),
                jnp.concatenate([p_im + m_im, m_re - p_re], axis=1),
            ],
            axis=0,
        ).astype(BF)
        back(values, 2 * step)

    @pl.when(jnp.logical_and(step == 0, jnp.logical_not(special)))
    def _():
        for ref in out_refs:
            ref[2 * pairs] = jnp.zeros(ref.shape[1:], BF)


def modes(received, first_pair, lat_keep, lon_keep, forward, inverse, w_in, b_in, w_out, b_out):
    lon_count = len(received[0])
    flat = [values for chunk in received for values in chunk]
    slots, _, width = flat[0].shape
    pairs = slots // 2
    pair_specs = [pl.BlockSpec((2, r.shape[1], width), lambda i: (i, 0, 0)) for r in flat]
    spare_specs = [pl.BlockSpec((1, r.shape[1], width), lambda i: (slots - 1, 0, 0)) for r in flat]
    whole = lambda array: pl.BlockSpec(array.shape, lambda i: (0,) * array.ndim)
    out = pl.pallas_call(
        functools.partial(modes_kernel, len(flat)),
        grid=(pairs,),
        in_specs=[pl.BlockSpec(memory_space=pltpu.SMEM), whole(lat_keep), whole(lon_keep)]
        + pair_specs
        + spare_specs
        + [whole(forward), whole(inverse), whole(w_in), whole(b_in), whole(w_out), whole(b_out)],
        out_specs=[pl.BlockSpec(r.shape, lambda i: (0, 0, 0)) for r in flat],
        out_shape=[jax.ShapeDtypeStruct(r.shape, BF) for r in flat],
        compiler_params=pltpu.CompilerParams(vmem_limit_bytes=48 << 20),
        cost_estimate=pl.CostEstimate(
            flops=pairs * 2 * (2 * 2 * KEEP_LON * W * 2 * width + 4 * KEEP_LON * 4 * width * width) // COST_SHARE,
            bytes_accessed=4 * slots * W * width // COST_SHARE,
            transcendentals=0,
        ),
        name="modes",
    )(
        first_pair, lat_keep, lon_keep, *flat, *flat,
        forward, inverse, w_in, b_in, w_out, b_out,
    )
    return [list(out[i : i + lon_count]) for i in range(0, len(flat), lon_count)]


def mlp_kernel(
    where_ref, own_ref, other_ref, gain_ref, bias_ref, w_in_ref, b_in_ref, w_out_ref, b_out_ref,
    *out_refs,
):
    _, rows, cols, width = own_ref.shape
    cells = rows * cols
    own = own_ref[0].reshape(cells, width)
    other = other_ref[0].reshape(cells, width)
    flip = where_ref[1] == 1
    low = jnp.where(flip, other, own)
    high = jnp.where(flip, own, other)
    wide = jnp.concatenate([low, high], axis=1).astype(F32)
    center = jnp.mean(wide, axis=1, keepdims=True)
    off = wide - center
    spread = jnp.mean(off * off, axis=1, keepdims=True)
    normed = (off * lax.rsqrt(spread + norm_epsilon) * gain_ref[...] + bias_ref[...]).astype(BF)
    hidden = jnp.dot(normed, w_in_ref[...], preferred_element_type=F32) + b_in_ref[...]
    hidden = (hidden * (0.5 + 0.5 * lax.erf(hidden * math.sqrt(0.5)))).astype(BF)
    total = jnp.dot(hidden, w_out_ref[...], preferred_element_type=F32) + wide + b_out_ref[...]
    total = total.astype(BF)
    low, high = total[:, :width], total[:, width:]
    mine = jnp.where(flip, high, low).reshape(rows, cols, width)
    sent = jnp.where(flip, low, high).reshape(rows, cols, width)
    lon_count = len(out_refs) // 2
    for s in range(lon_count):

        @pl.when(pl.program_id(0) == s)
        def _():
            out_refs[s][...] = mine
            out_refs[lon_count + s][...] = sent


def mlp(where, own, other, gain, bias, w_in, b_in, w_out, b_out):
    lon_count, rows, cols, width = own.shape
    whole = lambda array: pl.BlockSpec(array.shape, lambda i, where: (0,) * array.ndim)
    cell_spec = pl.BlockSpec(
        (1, rows, cols, width), lambda i, where: (lax.rem(where[0] + i, lon_count), 0, 0, 0)
    )
    cells = lon_count * rows * cols
    out = pl.pallas_call(
        mlp_kernel,
        grid_spec=pltpu.PrefetchScalarGridSpec(
            num_scalar_prefetch=1,
            grid=(lon_count,),
            in_specs=[cell_spec, cell_spec]
            + [whole(a) for a in (gain, bias, w_in, b_in, w_out, b_out)],
            out_specs=[pl.BlockSpec((rows, cols, width), lambda i, where: (0, 0, 0))]
            * (2 * lon_count),
        ),
        out_shape=[jax.ShapeDtypeStruct((rows, cols, width), BF)] * (2 * lon_count),
        compiler_params=pltpu.CompilerParams(vmem_limit_bytes=48 << 20),
        cost_estimate=pl.CostEstimate(
            flops=4 * cells * w_in.size // LATE_SHARE,
            bytes_accessed=8 * cells * width // LATE_SHARE,
            transcendentals=cells * w_in.shape[1] // LATE_SHARE,
        ),
        name="channel_mlp",
    )(where, own, other, gain, bias, w_in, b_in, w_out, b_out)
    return out[:lon_count], out[lon_count:]


def assemble_kernel(where_ref, *refs):
    lon_count = (len(refs) - 1) // 2
    out_ref = refs[-1]
    half = refs[0].shape[0]
    flip = where_ref[1] == 1
    for s in range(lon_count):

        @pl.when(pl.program_id(0) == s)
        def _():
            mine, theirs = refs[s][...], refs[lon_count + s][...]
            out_ref[:half] = jnp.where(flip, theirs, mine)
            out_ref[half:] = jnp.where(flip, mine, theirs)


def assemble(where, result, mine, theirs, first_col, block_cols):
    lon_count = len(mine)
    rows, cols, width = mine[0].shape
    block = math.gcd(math.gcd(cols, block_cols), first_col)
    steps = cols // block

    def piece(s):
        def index(g, j, where):
            return 0, jnp.where(g == s, j, jnp.where(g < s, 0, steps - 1)), 0

        return pl.BlockSpec((rows, block, width), index)

    def place(g, j, where):
        source = lax.rem(where[0] + (lon_count - g), lon_count)
        return 0, source * (block_cols // block) + first_col // block + j, 0

    specs = [piece(s) for s in range(lon_count)] * 2
    operands = [where, *mine, *theirs]
    aliases = {}
    kernel = assemble_kernel
    if result is not None:
        aliases = {len(operands): 0}
        operands.append(result)
        specs.append(pl.BlockSpec(memory_space=pl.ANY))

        def kernel(where_ref, *refs):
            assemble_kernel(where_ref, *refs[:-2], refs[-1])

    return pl.pallas_call(
        kernel,
        grid_spec=pltpu.PrefetchScalarGridSpec(
            num_scalar_prefetch=1,
            grid=(lon_count, steps),
            in_specs=specs,
            out_specs=pl.BlockSpec((2 * rows, block, width), place),
        ),
        out_shape=jax.ShapeDtypeStruct((2 * rows, lon_count * block_cols, width), BF),
        input_output_aliases=aliases,
        cost_estimate=pl.CostEstimate(
            flops=0, bytes_accessed=8 * lon_count * rows * cols * width // COST_SHARE, transcendentals=0
        ),
        name="assemble",
    )(*operands)


def block_diagonal(weight):
    blocks, n = weight.shape[1], weight.shape[2]
    eye = jnp.eye(blocks, dtype=weight.dtype)
    spread = (weight[:, :, :, None, :] * eye[None, :, None, :, None]).reshape(
        2, blocks * n, blocks * n
    )
    return jnp.concatenate(
        [
            jnp.concatenate([spread[0], spread[1]], axis=1),
            jnp.concatenate([-spread[1], spread[0]], axis=1),
        ],
        axis=0,
    )


def swap(values, axis):
    return lax.ppermute(values, axis, [(0, 1), (1, 0)])


def shift(values, steps, lon_count):
    if steps == 0:
        return values
    return lax.ppermute(values, "lon", [(z, (z + steps) % lon_count) for z in range(lon_count)])


def shift_across(values, steps, lon_count):
    pairs = [
        (z * 2 + c, (z + steps) % lon_count * 2 + 1 - c)
        for z in range(lon_count)
        for c in range(2)
    ]
    return lax.ppermute(values, ("lon", "ch"), pairs)


def after(value, *others):
    return lax.optimization_barrier((value,) + others)[0]


def column_plan(
    widths,
    patches,
    filter_norm_gain,
    filter_norm_bias,
    filter_in,
    filter_in_bias,
    filter_out,
    filter_out_bias,
    kept_lat,
    kept_lon,
    norm_gain,
    norm_bias,
    dense_in,
    dense_in_bias,
    dense_out,
    dense_out_bias,
):
    lon_count = lax.axis_size("lon")
    lat_count = lax.axis_size("lat")
    rows, cols, width = patches.shape
    chunks = len(widths)
    starts = [sum(widths[:i]) for i in range(chunks)]
    block_width = filter_in.shape[2]
    lat_id = lax.axis_index("lat")
    lon_id = lax.axis_index("lon")
    ch_id = lax.axis_index("ch")
    pairs = MLAT // (lat_count * lon_count)
    slots = 2 * pairs + 1

    lat_table = lat_tables(lat_count, lon_count).reshape(lat_count, lon_count, slots, H)
    forward_all, inverse_all = [], []
    for a in range(lat_count):
        here = lat_table[..., a * rows : (a + 1) * rows]
        ordered = np.concatenate([here[1 - a], here[a]], axis=0).reshape(-1, rows)
        forward_all.append(spread8(ordered))
        ordered = np.concatenate([here[a], here[1 - a]], axis=0)
        ordered = np.pad(ordered, ((0, 0), (0, slots % 2), (0, 0))).reshape(-1, rows)
        inverse_all.append(spread8(ordered.T))
    forward_lat, inverse_lat = jnp.asarray(np.stack(forward_all)), jnp.asarray(np.stack(inverse_all))

    ids = np.arange(W).reshape(lon_count, cols)

    def column_order(devices):
        return np.concatenate([ids[devices, c : c + w].reshape(-1) for c, w in zip(starts, widths)])

    steps = np.arange(lon_count)
    from_here = [lon_tables(column_order((z - steps) % lon_count))[0] for z in range(lon_count)]
    to_there = [lon_tables(column_order((z + steps) % lon_count))[1] for z in range(lon_count)]

    fence = lax.optimization_barrier
    where = jnp.stack([lon_id, ch_id, lat_id]).astype(jnp.int32)

    def row_transform(i, source):
        raw = source[:, starts[i] : starts[i] + widths[i]].astype(F32)
        center = jnp.mean(raw, axis=-1)
        off = raw - center[..., None]
        square = jnp.sum(off * off, axis=-1)
        theirs = swap(jnp.stack([center, square]), "ch")
        mean = 0.5 * (center + theirs[0])
        gap = center - theirs[0]
        spread = (square + theirs[1]) / C + 0.25 * gap * gap
        scale = lax.rsqrt(spread + norm_epsilon)
        prenormed = (
            (raw - mean[..., None]) * scale[..., None] * filter_norm_gain.astype(F32)
            + filter_norm_bias.astype(F32)
        ).astype(BF)
        return lat_forward(where, prenormed, forward_lat, lon_count)

    def mlp_weights(dense_in, dense_in_bias, dense_out, dense_out_bias):
        return (
            norm_gain.astype(F32)[None],
            norm_bias.astype(F32)[None],
            jnp.concatenate([dense_in, swap(dense_in, "ch")], axis=1),
            jnp.concatenate([dense_in_bias, swap(dense_in_bias, "ch")]).astype(F32)[None],
            jnp.concatenate([dense_out, swap(dense_out, "ch")], axis=0),
            lax.all_gather(dense_out_bias, "ch", axis=0, tiled=True).astype(F32)[None],
        )

    def filter_operands():
        return (
            ((lat_id * lon_count + lon_id) * pairs).astype(jnp.int32).reshape(1),
            jnp.tile(jnp.repeat(kept_lat, block_width), 2).reshape(1, -1),
            jnp.tile(jnp.repeat(kept_lon, block_width), 2).reshape(1, -1),
            lax.dynamic_index_in_dim(jnp.asarray(np.stack(from_here)), lon_id, 0, False),
            lax.dynamic_index_in_dim(jnp.asarray(np.stack(to_there)), lon_id, 0, False),
            block_diagonal(filter_in),
            filter_in_bias.reshape(1, -1).astype(F32),
            block_diagonal(filter_out),
            filter_out_bias.reshape(1, -1).astype(F32),
        )

    def along_lon(values):
        return [shift(values[s], s, lon_count) for s in range(lon_count)]

    def row_result(i, own, other):
        mine, sent = lat_inverse(where, own, other, inverse_lat, patches, starts[i])
        return mlp(where, mine, swap(sent, "ch"), *weights)

    def outward(outputs):
        mine, sent = outputs
        return (
            along_lon(mine),
            [shift_across(values, s, lon_count) for s, values in enumerate(sent)],
        )


    received, summed, sent, kept = [], None, None, None
    weights = None
    filter_args = None
    dense = (dense_in, dense_in_bias, dense_out, dense_out_bias)
    for step in range(chunks + 2):
        arrived = None
        if sent is not None:
            arrived = (kept, swap(sent, "lat"))
            sent = None
        if summed is not None:
            received.append(along_lon(summed))
            summed = None
        if step < chunks:
            sent, kept = row_transform(step, patches)
        elif step == chunks:
            filter_args = filter_operands()
        else:
            weights = mlp_weights(*dense)
        patches, arrived, sent, kept, received, filter_args, weights, dense = fence(
            (patches, arrived, sent, kept, received, filter_args, weights, dense)
        )
        if arrived is not None:
            summed = [
                (arrived[0][s].astype(F32) + arrived[1][s].astype(F32)).astype(BF)
                for s in range(lon_count)
            ]

    filtered = modes(received, *filter_args)

    owns = [None] * chunks
    others = [None] * chunks
    outputs = [None] * chunks
    for step in range(chunks):
        owns[step] = along_lon(filtered[step])
        if step >= 1:
            owns[step - 1] = jnp.stack(owns[step - 1])
            others[step - 1] = swap(owns[step - 1], "lat")
        if step >= 2:
            outputs[step - 2] = row_result(step - 2, owns[step - 2], others[step - 2])
        patches, filtered, owns, others, outputs = fence((patches, filtered, owns, others, outputs))

    result = None
    pieces = None
    for i in range(chunks):
        last = pieces
        pieces = outward(outputs[i])
        if last is not None:
            result = assemble(where, result, *last, starts[i - 1], cols)
        if i + 1 < chunks and outputs[i + 1] is None:
            own, _ = fence((owns[i + 1], pieces[0][1]))
            outputs[i + 1] = row_result(i + 1, own, others[i + 1])
        if i + 2 < chunks and others[i + 2] is None:
            owns[i + 2] = jnp.stack(owns[i + 2])
            others[i + 2] = swap(owns[i + 2], "lat")
        patches, owns, others, outputs, pieces, result = fence(
            (patches, owns, others, outputs, pieces, result)
        )
    result = assemble(where, result, *pieces, starts[chunks - 1], cols)
    return result.reshape(1, 1, rows // lon_count, lon_count * cols, width)


def lon_forward(number, length):
    freq_ids = jnp.arange(number, dtype=jnp.int32)
    cell_ids = jnp.arange(length, dtype=jnp.int32)
    phase_turns = cell_ids[:, None] * freq_ids[None, :] % length
    angles = phase_turns.astype(jnp.float32) * (2.0 * math.pi / length)
    factor = 1.0 / math.sqrt(length)
    return jnp.stack([jnp.cos(angles) * factor, -jnp.sin(angles) * factor], axis=1).astype(
        jnp.bfloat16
    )


def lon_inverse(freq_ids, length):
    cell_ids = jnp.arange(length, dtype=jnp.int32)
    phase_turns = freq_ids[:, None] * cell_ids[None, :] % length
    angles = phase_turns.astype(jnp.float32) * (2.0 * math.pi / length)
    factor = 1.0 / math.sqrt(length)
    weight = jnp.where(freq_ids == 0, 1.0, 2.0).astype(jnp.float32)[:, None]
    return jnp.stack(
        [jnp.cos(angles) * factor * weight, -jnp.sin(angles) * factor * weight]
    ).astype(jnp.bfloat16)


def band_ids(half_band, length):
    slot_ids = jnp.arange(2 * half_band, dtype=jnp.int32)
    return jnp.where(slot_ids < half_band, slot_ids, slot_ids + length - 2 * half_band)


def lat_forward_table(row_ids, half_band, length):
    phase_turns = band_ids(half_band, length)[:, None] * row_ids[None, :] % length
    angles = phase_turns.astype(jnp.float32) * (2.0 * math.pi / length)
    factor = 1.0 / math.sqrt(length)
    cosine = jnp.cos(angles) * factor
    sine_part = jnp.sin(angles) * factor
    upper_half = jnp.concatenate([cosine, sine_part], axis=1)
    bottom = jnp.concatenate([-sine_part, cosine], axis=1)
    return jnp.concatenate([upper_half, bottom], axis=0).astype(jnp.bfloat16)


def lat_inverse_table(row_ids, half_band, length):
    phase_turns = row_ids[:, None] * band_ids(half_band, length)[None, :] % length
    angles = phase_turns.astype(jnp.float32) * (2.0 * math.pi / length)
    factor = 1.0 / math.sqrt(length)
    cosine = jnp.cos(angles) * factor
    sine_part = jnp.sin(angles) * factor
    upper_half = jnp.concatenate([cosine, -sine_part], axis=1)
    bottom = jnp.concatenate([sine_part, cosine], axis=1)
    return jnp.concatenate([upper_half, bottom], axis=0).astype(jnp.bfloat16)


def complex_layer(values, weight, offset):
    products = jnp.einsum("tjkbc,ubcd->tujkbd", values, weight, preferred_element_type=jnp.float32)
    offset = offset.astype(jnp.float32)
    real_part = products[0, 0] - products[1, 1] + offset[0]
    imag_part = products[1, 0] + products[0, 1] + offset[1]
    return jnp.stack([real_part, imag_part])


def channel_mlp(mixed_full, norm_gain, norm_bias, weight_in, bias_in, weight_out):
    wide = mixed_full.astype(jnp.float32)
    center = jnp.mean(wide, axis=-1, keepdims=True)
    spread = jnp.mean((wide - center) ** 2, axis=-1, keepdims=True)
    normed = (
        (wide - center) * lax.rsqrt(spread + norm_epsilon) * norm_gain.astype(jnp.float32)
        + norm_bias.astype(jnp.float32)
    ).astype(jnp.bfloat16)
    hidden = jnp.einsum("rwc,cu->rwu", normed, weight_in, preferred_element_type=jnp.float32)
    hidden = jax.nn.gelu(hidden + bias_in.astype(jnp.float32), approximate=False).astype(
        jnp.bfloat16
    )
    return jnp.einsum("rwu,uc->rwc", hidden, weight_out, preferred_element_type=jnp.float32)


def row_plan(
    patches,
    filter_norm_gain,
    filter_norm_bias,
    filter_in,
    filter_in_bias,
    filter_out,
    filter_out_bias,
    kept_lat,
    kept_lon,
    norm_gain,
    norm_bias,
    dense_in,
    dense_in_bias,
    dense_out,
    dense_out_bias,
):
    lon_count = lax.axis_size("lon")
    lat_count = lax.axis_size("lat")
    band_rows = patches.shape[0] // lon_count
    local_channels = patches.shape[2]
    local_blocks = filter_in.shape[1]
    block_width = filter_in.shape[2]
    row_span = lon_count * band_rows
    local_freqs = KEEP_LON // (lon_count * lat_count)
    local_rows = lax.all_to_all(patches, "lon", split_axis=0, concat_axis=1, tiled=True)
    raw = local_rows.astype(jnp.float32)
    cell_total = lax.psum(jnp.sum(raw, axis=-1, keepdims=True), "ch")
    pre_center = cell_total / C
    centered = raw - pre_center
    square_total = lax.psum(jnp.sum(centered * centered, axis=-1, keepdims=True), "ch")
    pre_spread = square_total / C
    prenormed = (
        centered * lax.rsqrt(pre_spread + norm_epsilon) * filter_norm_gain.astype(jnp.float32)
        + filter_norm_bias.astype(jnp.float32)
    ).astype(jnp.bfloat16)
    spectrum = jnp.einsum(
        "rwc,wtk->trkc", prenormed, lon_forward(KEEP_LON, W), preferred_element_type=jnp.float32
    )
    spectrum = spectrum.astype(jnp.bfloat16)
    slot_ids = jnp.arange(H, dtype=jnp.int32)
    group_ids = slot_ids // band_rows
    direct_rows = (
        group_ids % lat_count * row_span + group_ids // lat_count * band_rows + slot_ids % band_rows
    )
    pencil = lax.all_to_all(spectrum, ("lon", "lat"), split_axis=2, concat_axis=1, tiled=True)
    banded = jnp.dot(
        lat_forward_table(direct_rows, MLAT, H),
        pencil.reshape(2 * H, -1),
        preferred_element_type=jnp.float32,
    )
    banded = banded.astype(jnp.bfloat16).reshape(
        2, 2 * MLAT, local_freqs, local_blocks, block_width
    )
    first = complex_layer(banded, filter_in, filter_in_bias.reshape(2, local_blocks, block_width))
    first = jnp.maximum(first, 0.0).astype(jnp.bfloat16)
    second = complex_layer(first, filter_out, filter_out_bias.reshape(2, local_blocks, block_width))
    shrunk = jnp.sign(second) * jnp.maximum(jnp.abs(second) - shrink_level, 0.0)
    column_ids = (
        lax.axis_index("lon") * lat_count + lax.axis_index("lat")
    ) * local_freqs + jnp.arange(local_freqs, dtype=jnp.int32)
    band_slots = jnp.arange(2 * MLAT, dtype=jnp.int32)
    signed_band = jnp.where(band_slots < MLAT, band_slots, band_slots - 2 * MLAT)
    lat_ok = (signed_band[:, None] >= -kept_lat[None, :]) & (
        signed_band[:, None] < kept_lat[None, :]
    )
    lon_ok = column_ids[:, None] < kept_lon[None, :]
    keep_mask = (lat_ok[:, None, :] & lon_ok[None, :, :]).astype(jnp.float32)[..., None]
    kept_modes = (shrunk * keep_mask).astype(jnp.bfloat16).reshape(4 * MLAT, -1)
    spatial = jnp.dot(
        lat_inverse_table(direct_rows, MLAT, H), kept_modes, preferred_element_type=jnp.float32
    )
    spatial = spatial.astype(jnp.bfloat16).reshape(2, H, local_freqs, local_channels)
    returned = lax.all_to_all(spatial, ("lon", "lat"), split_axis=1, concat_axis=2, tiled=True)
    back_freqs = jnp.arange(KEEP_LON, dtype=jnp.int32)
    fine_part = jnp.einsum(
        "trkc,tkw->rwc", returned, lon_inverse(back_freqs, W), preferred_element_type=jnp.float32
    )
    mixed = (raw + fine_part).astype(jnp.bfloat16)
    gathered = lax.all_gather(mixed, "ch", axis=2, tiled=True)
    partial_terms = channel_mlp(gathered, norm_gain, norm_bias, dense_in, dense_in_bias, dense_out)
    summed = lax.psum_scatter(
        partial_terms.astype(jnp.bfloat16), "ch", scatter_dimension=2, tiled=True
    ).astype(jnp.float32)
    result = (mixed.astype(jnp.float32) + summed + dense_out_bias.astype(jnp.float32)).astype(
        jnp.bfloat16
    )
    return result.reshape(1, 1, band_rows, W, local_channels)


def solution(mesh):
    placed = (
        P(("grp", "lat"), "lon", "ch"),
        P("ch"),
        P("ch"),
        P(None, "ch", None, None),
        P(None, "ch"),
        P(None, "ch", None, None),
        P(None, "ch"),
        P("ch"),
        P("ch"),
        P(),
        P(),
        P(None, "ch"),
        P("ch"),
        P("ch", None),
        P("ch"),
    )
    sizes = mesh.shape
    lat_count, lon_count = sizes["lat"], sizes["lon"]
    cols = W // lon_count
    fits = lat_count == 2 and sizes["ch"] == 2 and MLAT % (lat_count * lon_count) == 0
    fits = fits and cols == 96 and H % (2 * lat_count * lon_count) == 0
    plan = functools.partial(column_plan, (32, 32, 32)) if fits else row_plan
    return jax.shard_map(
        plan,
        mesh=mesh,
        in_specs=placed,
        out_specs=P(("grp", "lat"), "lon", None, None, "ch"),
        check_vma=False,
    )
```

```python
import functools
import math

import jax
import jax.numpy as jnp
import numpy as np
from jax import lax
from jax.experimental import pallas as pl
from jax.experimental.pallas import tpu as pltpu
from jax.sharding import PartitionSpec as P

H = 256
W = 384
C = 768
MLAT = 64
KEEP_LON = 128

shrink_level = 0.01
norm_epsilon = 1e-05

COST_SHARE = 1

BF = jnp.bfloat16
F32 = jnp.float32


def angle_table(rows, cols, length):
    phase = rows[:, None] * cols[None, :] % length
    return phase * (2.0 * math.pi / length)


def lat_slots(lat_count, lon_count):
    per = MLAT // (lat_count * lon_count)
    freq, kind = [], []
    for dev in range(lat_count * lon_count):
        for pair in range(dev * per, dev * per + per):
            freq += [0, MLAT] if pair == 0 else [pair, pair]
            kind += [0, 0] if pair == 0 else [0, 1]
        freq.append(MLAT if dev == 0 else 0)
        kind.append(1 if dev == 0 else 2)
    return np.array(freq), np.array(kind)


def lat_tables(lat_count, lon_count):
    freq, kind = lat_slots(lat_count, lon_count)
    angles = angle_table(freq, np.arange(H), H)
    table = np.where(kind[:, None] == 0, np.cos(angles), -np.sin(angles)) / math.sqrt(H)
    table = np.where(kind[:, None] == 2, 0.0, table)
    return table.astype(np.float32)


def lon_tables(order):
    freqs = np.arange(KEEP_LON)
    angles = angle_table(freqs, order, W)
    factor = 1.0 / math.sqrt(W)
    weight = np.where(freqs == 0, 1.0, 2.0)[:, None]
    forward = np.concatenate([np.cos(angles) * factor, -np.sin(angles) * factor], axis=0)
    inverse = np.concatenate(
        [np.cos(angles) * factor * weight, -np.sin(angles) * factor * weight], axis=0
    ).T
    return forward.astype(np.float32).astype(jnp.bfloat16), inverse.astype(np.float32).astype(jnp.bfloat16)


def spread8(table):
    return np.kron(table, np.eye(8, dtype=np.float32)).astype(jnp.bfloat16)


def lat_forward_kernel(where_ref, cells_ref, table_ref, send_ref, keep_ref):
    rows, _, width = cells_ref.shape
    lon_count, slots, _, _ = send_ref.shape
    values = cells_ref[...].astype(F32).reshape(rows, 2, 8, width)
    pair = jnp.concatenate(
        [values[:, 0].reshape(rows * 8, width), values[:, 1].reshape(rows * 8, width)], axis=1
    ).astype(BF)
    half = table_ref.shape[0] // 2
    for part, out_ref in ((0, send_ref), (1, keep_ref)):
        total = jnp.dot(
            table_ref[part * half : (part + 1) * half, :], pair, preferred_element_type=F32
        )
        total = jnp.concatenate(
            [
                total[:, :width].reshape(lon_count, slots, 8, width),
                total[:, width:].reshape(lon_count, slots, 8, width),
            ],
            axis=2,
        ).astype(BF)
        for z in range(lon_count):
            out_ref[lax.rem(z + lon_count - where_ref[0], lon_count)] = total[z]


def lat_forward(where, cells, table, lon_count):
    rows, cols, width = cells.shape
    slots = table.shape[0] // (16 * lon_count)
    block = pl.BlockSpec((lon_count, slots, 16, width), lambda i: (0, 0, i, 0))
    return pl.pallas_call(
        lat_forward_kernel,
        grid=(cols // 16,),
        in_specs=[
            pl.BlockSpec(memory_space=pltpu.SMEM),
            pl.BlockSpec((rows, 16, width), lambda i: (0, i, 0)),
            pl.BlockSpec(table.shape, lambda i: (0, 0)),
        ],
        out_specs=[block, block],
        out_shape=[jax.ShapeDtypeStruct((lon_count, slots, cols, width), BF)] * 2,
        compiler_params=pltpu.CompilerParams(vmem_limit_bytes=40 << 20),
        cost_estimate=pl.CostEstimate(
            flops=2 * table.size * cols // 8 * width // COST_SHARE,
            bytes_accessed=4 * rows * cols * width // COST_SHARE,
            transcendentals=0,
        ),
        name="lat_forward",
    )(where, cells, table)


def lat_inverse_kernel(
    where_ref, own_ref, other_ref, table_ref, patches_ref, mine_ref, sent_ref, flat_ref
):
    rows, _, width = patches_ref.shape
    lon_count, slots = own_ref.shape[:2]
    blank = jnp.zeros((flat_ref.shape[1] - slots * 8, 2 * width), BF)
    for side, ref in enumerate((own_ref, other_ref)):
        for s in range(lon_count):
            values = ref[s].astype(F32).reshape(slots, 2, 8, width)
            flat = jnp.concatenate(
                [values[:, 0].reshape(slots * 8, width), values[:, 1].reshape(slots * 8, width)],
                axis=1,
            )
            source = lax.rem(where_ref[0] + (lon_count - s), lon_count)
            flat_ref[side * lon_count + source] = jnp.concatenate([flat.astype(BF), blank], axis=0)
    total = jnp.dot(
        table_ref[...], flat_ref[...].reshape(-1, 2 * width), preferred_element_type=F32
    )
    fine = jnp.concatenate(
        [total[:, :width].reshape(rows, 8, width), total[:, width:].reshape(rows, 8, width)], axis=1
    )
    mixed = (patches_ref[...].astype(F32) + fine).astype(BF)
    mixed = mixed.reshape(lon_count, 2, rows // (2 * lon_count), 16, width)

    @pl.when(where_ref[1] == 0)
    def _():
        mine_ref[...] = mixed[:, 0]
        sent_ref[...] = mixed[:, 1]

    @pl.when(where_ref[1] != 0)
    def _():
        mine_ref[...] = mixed[:, 1]
        sent_ref[...] = mixed[:, 0]


def lat_inverse(where, own, other, table, patches, first_col):
    lon_count, slots, cols, width = own.shape
    rows = patches.shape[0]
    first_block = first_col // 16
    spec = pl.BlockSpec((lon_count, slots, 16, width), lambda i: (0, 0, i, 0))
    half = rows // (2 * lon_count)
    out_spec = pl.BlockSpec((lon_count, half, 16, width), lambda i: (0, 0, i, 0))
    return pl.pallas_call(
        lat_inverse_kernel,
        grid=(cols // 16,),
        in_specs=[
            pl.BlockSpec(memory_space=pltpu.SMEM),
            spec,
            spec,
            pl.BlockSpec(table.shape, lambda i: (0, 0)),
            pl.BlockSpec((rows, 16, width), lambda i: (0, first_block + i, 0)),
        ],
        out_specs=[out_spec, out_spec],
        out_shape=[jax.ShapeDtypeStruct((lon_count, half, cols, width), BF)] * 2,
        scratch_shapes=[
            pltpu.VMEM((2 * lon_count, table.shape[1] // (2 * lon_count), 2 * width), BF)
        ],
        compiler_params=pltpu.CompilerParams(vmem_limit_bytes=40 << 20),
        cost_estimate=pl.CostEstimate(
            flops=2 * table.size * cols // 8 * width // COST_SHARE,
            bytes_accessed=6 * rows * cols * width // COST_SHARE,
            transcendentals=0,
        ),
        name="lat_inverse",
    )(where, own, other, table, patches)


def modes_kernel(inputs, first_pair_ref, lat_keep_ref, lon_keep_ref, *refs):
    pair_refs = refs[:inputs]
    spare_refs = refs[inputs : 2 * inputs]
    forward_ref, inverse_ref, w_in_ref, b_in_ref, w_out_ref, b_out_ref = refs[
        2 * inputs : 2 * inputs + 6
    ]
    out_refs = refs[2 * inputs + 6 :]
    width = pair_refs[0].shape[-1]
    step = pl.program_id(0)
    pairs = pl.num_programs(0)
    pair_id = first_pair_ref[0] + step
    special = pair_id == 0
    keep = KEEP_LON

    def columns(refs, row):
        return jnp.concatenate([ref[row] for ref in refs], axis=0)

    both = jnp.concatenate([columns(pair_refs, 0), columns(pair_refs, 1)], axis=1)
    spectrum = jnp.dot(forward_ref[...], both, preferred_element_type=F32)
    a_re, a_im = spectrum[:keep, :width], spectrum[keep:, :width]
    b_re, b_im = spectrum[:keep, width:], spectrum[keep:, width:]

    def filtered(plus_re, plus_im, minus_re, minus_im):
        banded = jnp.concatenate(
            [
                jnp.concatenate([plus_re, plus_im], axis=1),
                jnp.concatenate([minus_re, minus_im], axis=1),
            ],
            axis=0,
        ).astype(BF)
        first = jnp.dot(banded, w_in_ref[...], preferred_element_type=F32) + b_in_ref[...]
        first = jnp.maximum(first, 0.0).astype(BF)
        second = jnp.dot(first, w_out_ref[...], preferred_element_type=F32) + b_out_ref[...]
        shrunk = second - jnp.clip(second, -shrink_level, shrink_level)
        freq = lax.broadcasted_iota(jnp.int32, (keep, 2 * width), 0)
        lon_ok = freq < lon_keep_ref[...]
        plus_ok = lon_ok & (pair_id < lat_keep_ref[...])
        minus_id = jnp.where(special, MLAT, pair_id)
        minus_ok = lon_ok & (minus_id <= lat_keep_ref[...])
        plus = jnp.where(plus_ok, shrunk[:keep], 0.0)
        minus = jnp.where(minus_ok, shrunk[keep:], 0.0)
        return plus[:, :width], plus[:, width:], minus[:, :width], minus[:, width:]

    def back(values, row):
        grid_values = jnp.dot(inverse_ref[...], values, preferred_element_type=F32).astype(BF)
        start = 0
        for ref in out_refs:
            cols = ref.shape[1]
            for r in range(grid_values.shape[1] // width):
                ref[row + r] = grid_values[start : start + cols, r * width : (r + 1) * width]
            start += cols

    @pl.when(special)
    def _():
        spare = jnp.dot(forward_ref[...], columns(spare_refs, 0), preferred_element_type=F32)
        e_re, e_im = spare[:keep], spare[keep:]
        p_re, p_im, m_re, m_im = filtered(a_re, a_im, b_re + e_im, b_im - e_re)
        values = jnp.concatenate(
            [jnp.concatenate([p_re, m_re], axis=1), jnp.concatenate([p_im, m_im], axis=1)], axis=0
        ).astype(BF)
        back(values, 2 * step)
        back(jnp.concatenate([-m_im, m_re], axis=0).astype(BF), 2 * pairs)

    @pl.when(jnp.logical_not(special))
    def _():
        p_re, p_im, m_re, m_im = filtered(a_re - b_im, a_im + b_re, a_re + b_im, a_im - b_re)
        values = jnp.concatenate(
            [
                jnp.concatenate([p_re + m_re, p_im - m_im], axis=1),
                jnp.concatenate([p_im + m_im, m_re - p_re], axis=1),
            ],
            axis=0,
        ).astype(BF)
        back(values, 2 * step)

    @pl.when(jnp.logical_and(step == 0, jnp.logical_not(special)))
    def _():
        for ref in out_refs:
            ref[2 * pairs] = jnp.zeros(ref.shape[1:], BF)


def modes(received, first_pair, lat_keep, lon_keep, forward, inverse, w_in, b_in, w_out, b_out):
    lon_count = len(received[0])
    flat = [values for chunk in received for values in chunk]
    slots, _, width = flat[0].shape
    pairs = slots // 2
    pair_specs = [pl.BlockSpec((2, r.shape[1], width), lambda i: (i, 0, 0)) for r in flat]
    spare_specs = [pl.BlockSpec((1, r.shape[1], width), lambda i: (slots - 1, 0, 0)) for r in flat]
    whole = lambda array: pl.BlockSpec(array.shape, lambda i: (0,) * array.ndim)
    out = pl.pallas_call(
        functools.partial(modes_kernel, len(flat)),
        grid=(pairs,),
        in_specs=[pl.BlockSpec(memory_space=pltpu.SMEM), whole(lat_keep), whole(lon_keep)]
        + pair_specs
        + spare_specs
        + [whole(forward), whole(inverse), whole(w_in), whole(b_in), whole(w_out), whole(b_out)],
        out_specs=[pl.BlockSpec(r.shape, lambda i: (0, 0, 0)) for r in flat],
        out_shape=[jax.ShapeDtypeStruct(r.shape, BF) for r in flat],
        compiler_params=pltpu.CompilerParams(vmem_limit_bytes=48 << 20),
        cost_estimate=pl.CostEstimate(
            flops=pairs * 2 * (2 * 2 * KEEP_LON * W * 2 * width + 4 * KEEP_LON * 4 * width * width) // COST_SHARE,
            bytes_accessed=4 * slots * W * width // COST_SHARE,
            transcendentals=0,
        ),
        name="modes",
    )(
        first_pair, lat_keep, lon_keep, *flat, *flat,
        forward, inverse, w_in, b_in, w_out, b_out,
    )
    return [list(out[i : i + lon_count]) for i in range(0, len(flat), lon_count)]


def mlp_kernel(
    where_ref, own_ref, other_ref, gain_ref, bias_ref, w_in_ref, b_in_ref, w_out_ref, b_out_ref,
    out_ref,
):
    _, rows, cols, width = own_ref.shape
    cells = rows * cols
    own = own_ref[0].reshape(cells, width)
    other = other_ref[0].reshape(cells, width)
    flip = where_ref[1] == 1
    low = jnp.where(flip, other, own)
    high = jnp.where(flip, own, other)
    wide = jnp.concatenate([low, high], axis=1).astype(F32)
    center = jnp.mean(wide, axis=1, keepdims=True)
    off = wide - center
    spread = jnp.mean(off * off, axis=1, keepdims=True)
    normed = (off * lax.rsqrt(spread + norm_epsilon) * gain_ref[...] + bias_ref[...]).astype(BF)
    hidden = jnp.dot(normed, w_in_ref[...], preferred_element_type=F32) + b_in_ref[...]
    hidden = (hidden * (0.5 + 0.5 * lax.erf(hidden * math.sqrt(0.5)))).astype(BF)
    total = jnp.dot(hidden, w_out_ref[...], preferred_element_type=F32) + wide + b_out_ref[...]
    total = total.astype(BF)
    out_ref[0, 0] = total[:, :width].reshape(rows, cols, width)
    out_ref[0, 1] = total[:, width:].reshape(rows, cols, width)


def mlp(where, own, other, gain, bias, w_in, b_in, w_out, b_out):
    lon_count, rows, cols, width = own.shape
    whole = lambda array: pl.BlockSpec(array.shape, lambda i, where: (0,) * array.ndim)
    cell_spec = pl.BlockSpec((1, rows, cols, width), lambda i, where: (i, 0, 0, 0))
    cells = lon_count * rows * cols
    return pl.pallas_call(
        mlp_kernel,
        grid_spec=pltpu.PrefetchScalarGridSpec(
            num_scalar_prefetch=1,
            grid=(lon_count,),
            in_specs=[cell_spec, cell_spec]
            + [whole(a) for a in (gain, bias, w_in, b_in, w_out, b_out)],
            out_specs=pl.BlockSpec((1, 2, rows, cols, width), lambda i, where: (i, 0, 0, 0, 0)),
        ),
        out_shape=jax.ShapeDtypeStruct((lon_count, 2, rows, cols, width), BF),
        compiler_params=pltpu.CompilerParams(vmem_limit_bytes=48 << 20),
        cost_estimate=pl.CostEstimate(
            flops=4 * cells * w_in.size // COST_SHARE,
            bytes_accessed=8 * cells * width // COST_SHARE,
            transcendentals=cells * w_in.shape[1] // COST_SHARE,
        ),
        name="channel_mlp",
    )(where, own, other, gain, bias, w_in, b_in, w_out, b_out)


def assemble_kernel(piece_ref, *refs):
    out_ref = refs[-1]
    half = piece_ref.shape[2]
    for c in range(2):
        out_ref[c * half : (c + 1) * half] = piece_ref[0, c]


def assemble(result, pieces, first_col, block_cols):
    lon_count, _, rows, cols, width = pieces.shape
    block = math.gcd(math.gcd(cols, block_cols), first_col)
    specs = [pl.BlockSpec((1, 2, rows, block, width), lambda z, j: (z, 0, 0, j, 0))]
    operands = [pieces]
    aliases = {}
    if result is not None:
        aliases = {1: 0}
        operands.append(result)
        specs.append(pl.BlockSpec(memory_space=pl.ANY))
    return pl.pallas_call(
        assemble_kernel,
        grid=(lon_count, cols // block),
        in_specs=specs,
        out_specs=pl.BlockSpec(
            (2 * rows, block, width),
            lambda z, j: (0, z * (block_cols // block) + first_col // block + j, 0),
        ),
        out_shape=jax.ShapeDtypeStruct((2 * rows, lon_count * block_cols, width), BF),
        input_output_aliases=aliases,
        cost_estimate=pl.CostEstimate(
            flops=0, bytes_accessed=8 * lon_count * rows * cols * width, transcendentals=0
        ),
        name="assemble",
    )(*operands)


def block_diagonal(weight):
    blocks, n = weight.shape[1], weight.shape[2]
    eye = jnp.eye(blocks, dtype=weight.dtype)
    spread = (weight[:, :, :, None, :] * eye[None, :, None, :, None]).reshape(
        2, blocks * n, blocks * n
    )
    return jnp.concatenate(
        [
            jnp.concatenate([spread[0], spread[1]], axis=1),
            jnp.concatenate([-spread[1], spread[0]], axis=1),
        ],
        axis=0,
    )


def swap(values, axis):
    return lax.ppermute(values, axis, [(0, 1), (1, 0)])


def shift(values, steps, lon_count):
    if steps == 0:
        return values
    return lax.ppermute(values, "lon", [(z, (z + steps) % lon_count) for z in range(lon_count)])


def column_plan(
    widths,
    patches,
    filter_norm_gain,
    filter_norm_bias,
    filter_in,
    filter_in_bias,
    filter_out,
    filter_out_bias,
    kept_lat,
    kept_lon,
    norm_gain,
    norm_bias,
    dense_in,
    dense_in_bias,
    dense_out,
    dense_out_bias,
):
    lon_count = lax.axis_size("lon")
    lat_count = lax.axis_size("lat")
    rows, cols, width = patches.shape
    chunks = len(widths)
    starts = [sum(widths[:i]) for i in range(chunks)]
    block_width = filter_in.shape[2]
    lat_id = lax.axis_index("lat")
    lon_id = lax.axis_index("lon")
    ch_id = lax.axis_index("ch")
    pairs = MLAT // (lat_count * lon_count)
    slots = 2 * pairs + 1

    lat_table = lat_tables(lat_count, lon_count).reshape(lat_count, lon_count, slots, H)
    forward_all, inverse_all = [], []
    for a in range(lat_count):
        here = lat_table[..., a * rows : (a + 1) * rows]
        ordered = np.concatenate([here[1 - a], here[a]], axis=0).reshape(-1, rows)
        forward_all.append(spread8(ordered))
        ordered = np.concatenate([here[a], here[1 - a]], axis=0)
        ordered = np.pad(ordered, ((0, 0), (0, slots % 2), (0, 0))).reshape(-1, rows)
        inverse_all.append(spread8(ordered.T))
    forward_lat = lax.dynamic_index_in_dim(jnp.asarray(np.stack(forward_all)), lat_id, 0, False)
    inverse_lat = None

    ids = np.arange(W).reshape(lon_count, cols)

    def column_order(devices):
        return np.concatenate([ids[devices, c : c + w].reshape(-1) for c, w in zip(starts, widths)])

    steps = np.arange(lon_count)
    from_here = [lon_tables(column_order((z - steps) % lon_count))[0] for z in range(lon_count)]
    to_there = [lon_tables(column_order((z + steps) % lon_count))[1] for z in range(lon_count)]

    fence = lax.optimization_barrier
    where = jnp.stack([lon_id, ch_id]).astype(jnp.int32)

    def row_transform(i, source):
        raw = source[:, starts[i] : starts[i] + widths[i]].astype(F32)
        center = jnp.mean(raw, axis=-1)
        off = raw - center[..., None]
        square = jnp.sum(off * off, axis=-1)
        theirs = swap(jnp.stack([center, square]), "ch")
        mean = 0.5 * (center + theirs[0])
        gap = center - theirs[0]
        spread = (square + theirs[1]) / C + 0.25 * gap * gap
        scale = lax.rsqrt(spread + norm_epsilon)
        prenormed = (
            (raw - mean[..., None]) * scale[..., None] * filter_norm_gain.astype(F32)
            + filter_norm_bias.astype(F32)
        ).astype(BF)
        return lat_forward(where, prenormed, forward_lat, lon_count)

    def mlp_weights(dense_in, dense_in_bias, dense_out, dense_out_bias):
        return (
            norm_gain.astype(F32)[None],
            norm_bias.astype(F32)[None],
            jnp.concatenate([dense_in, swap(dense_in, "ch")], axis=1),
            jnp.concatenate([dense_in_bias, swap(dense_in_bias, "ch")]).astype(F32)[None],
            jnp.concatenate([dense_out, swap(dense_out, "ch")], axis=0),
            lax.all_gather(dense_out_bias, "ch", axis=0, tiled=True).astype(F32)[None],
        )

    def filter_operands():
        return (
            ((lat_id * lon_count + lon_id) * pairs).astype(jnp.int32).reshape(1),
            jnp.tile(jnp.repeat(kept_lat, block_width), 2).reshape(1, -1),
            jnp.tile(jnp.repeat(kept_lon, block_width), 2).reshape(1, -1),
            lax.dynamic_index_in_dim(jnp.asarray(np.stack(from_here)), lon_id, 0, False),
            lax.dynamic_index_in_dim(jnp.asarray(np.stack(to_there)), lon_id, 0, False),
            block_diagonal(filter_in),
            filter_in_bias.reshape(1, -1).astype(F32),
            block_diagonal(filter_out),
            filter_out_bias.reshape(1, -1).astype(F32),
        )

    def along_lon(values):
        return [shift(values[s], s, lon_count) for s in range(lon_count)]

    def row_result(i, own, other):
        mine, sent = lat_inverse(where, own, other, inverse_lat, patches, starts[i])
        return mlp(where, mine, swap(sent, "ch"), *weights)

    def outward(outputs):
        shape = outputs.shape
        flat = outputs.reshape((shape[0] * 2,) + shape[2:])
        return lax.all_to_all(flat, ("lon", "ch"), 0, 0, tiled=True).reshape(shape)

    received, summed, sent, kept = [], None, None, None
    weights = None
    filter_args = None
    dense = (dense_in, dense_in_bias, dense_out, dense_out_bias)
    for step in range(chunks + 2):
        arrived = None
        if sent is not None:
            arrived = (kept, swap(sent, "lat"))
            sent = None
        if summed is not None:
            received.append(along_lon(summed))
            summed = None
        if step < chunks:
            sent, kept = row_transform(step, patches)
        elif step == chunks:
            filter_args = filter_operands()
        else:
            weights = mlp_weights(*dense)
            inverse_lat = lax.dynamic_index_in_dim(jnp.asarray(np.stack(inverse_all)), lat_id, 0, False)
        patches, arrived, sent, kept, received, filter_args, weights, inverse_lat, dense = fence(
            (patches, arrived, sent, kept, received, filter_args, weights, inverse_lat, dense)
        )
        if arrived is not None:
            summed = [
                (arrived[0][s].astype(F32) + arrived[1][s].astype(F32)).astype(BF)
                for s in range(lon_count)
            ]

    filtered = modes(received, *filter_args)

    owns = [None] * chunks
    others = [None] * chunks
    outputs = [None] * chunks
    for step in range(chunks):
        owns[step] = along_lon(filtered[step])
        if step >= 1:
            owns[step - 1] = jnp.stack(owns[step - 1])
            others[step - 1] = swap(owns[step - 1], "lat")
        if step >= 2:
            outputs[step - 2] = row_result(step - 2, owns[step - 2], others[step - 2])
        patches, filtered, owns, others, outputs = fence((patches, filtered, owns, others, outputs))

    result = None
    pieces = None
    for i in range(chunks):
        last = pieces
        pieces = outward(outputs[i])
        if last is not None:
            result = assemble(result, last, starts[i - 1], cols)
        if i + 1 < chunks and outputs[i + 1] is None:
            outputs[i + 1] = row_result(i + 1, owns[i + 1], others[i + 1])
        if i + 2 < chunks and others[i + 2] is None:
            owns[i + 2] = jnp.stack(owns[i + 2])
            others[i + 2] = swap(owns[i + 2], "lat")
        patches, owns, others, outputs, pieces, result = fence(
            (patches, owns, others, outputs, pieces, result)
        )
    result = assemble(result, pieces, starts[chunks - 1], cols)
    return result.reshape(1, 1, rows // lon_count, lon_count * cols, width)


def lon_forward(number, length):
    freq_ids = jnp.arange(number, dtype=jnp.int32)
    cell_ids = jnp.arange(length, dtype=jnp.int32)
    phase_turns = cell_ids[:, None] * freq_ids[None, :] % length
    angles = phase_turns.astype(jnp.float32) * (2.0 * math.pi / length)
    factor = 1.0 / math.sqrt(length)
    return jnp.stack([jnp.cos(angles) * factor, -jnp.sin(angles) * factor], axis=1).astype(
        jnp.bfloat16
    )


def lon_inverse(freq_ids, length):
    cell_ids = jnp.arange(length, dtype=jnp.int32)
    phase_turns = freq_ids[:, None] * cell_ids[None, :] % length
    angles = phase_turns.astype(jnp.float32) * (2.0 * math.pi / length)
    factor = 1.0 / math.sqrt(length)
    weight = jnp.where(freq_ids == 0, 1.0, 2.0).astype(jnp.float32)[:, None]
    return jnp.stack(
        [jnp.cos(angles) * factor * weight, -jnp.sin(angles) * factor * weight]
    ).astype(jnp.bfloat16)


def band_ids(half_band, length):
    slot_ids = jnp.arange(2 * half_band, dtype=jnp.int32)
    return jnp.where(slot_ids < half_band, slot_ids, slot_ids + length - 2 * half_band)


def lat_forward_table(row_ids, half_band, length):
    phase_turns = band_ids(half_band, length)[:, None] * row_ids[None, :] % length
    angles = phase_turns.astype(jnp.float32) * (2.0 * math.pi / length)
    factor = 1.0 / math.sqrt(length)
    cosine = jnp.cos(angles) * factor
    sine_part = jnp.sin(angles) * factor
    upper_half = jnp.concatenate([cosine, sine_part], axis=1)
    bottom = jnp.concatenate([-sine_part, cosine], axis=1)
    return jnp.concatenate([upper_half, bottom], axis=0).astype(jnp.bfloat16)


def lat_inverse_table(row_ids, half_band, length):
    phase_turns = row_ids[:, None] * band_ids(half_band, length)[None, :] % length
    angles = phase_turns.astype(jnp.float32) * (2.0 * math.pi / length)
    factor = 1.0 / math.sqrt(length)
    cosine = jnp.cos(angles) * factor
    sine_part = jnp.sin(angles) * factor
    upper_half = jnp.concatenate([cosine, -sine_part], axis=1)
    bottom = jnp.concatenate([sine_part, cosine], axis=1)
    return jnp.concatenate([upper_half, bottom], axis=0).astype(jnp.bfloat16)


def complex_layer(values, weight, offset):
    products = jnp.einsum("tjkbc,ubcd->tujkbd", values, weight, preferred_element_type=jnp.float32)
    offset = offset.astype(jnp.float32)
    real_part = products[0, 0] - products[1, 1] + offset[0]
    imag_part = products[1, 0] + products[0, 1] + offset[1]
    return jnp.stack([real_part, imag_part])


def channel_mlp(mixed_full, norm_gain, norm_bias, weight_in, bias_in, weight_out):
    wide = mixed_full.astype(jnp.float32)
    center = jnp.mean(wide, axis=-1, keepdims=True)
    spread = jnp.mean((wide - center) ** 2, axis=-1, keepdims=True)
    normed = (
        (wide - center) * lax.rsqrt(spread + norm_epsilon) * norm_gain.astype(jnp.float32)
        + norm_bias.astype(jnp.float32)
    ).astype(jnp.bfloat16)
    hidden = jnp.einsum("rwc,cu->rwu", normed, weight_in, preferred_element_type=jnp.float32)
    hidden = jax.nn.gelu(hidden + bias_in.astype(jnp.float32), approximate=False).astype(
        jnp.bfloat16
    )
    return jnp.einsum("rwu,uc->rwc", hidden, weight_out, preferred_element_type=jnp.float32)


def row_plan(
    patches,
    filter_norm_gain,
    filter_norm_bias,
    filter_in,
    filter_in_bias,
    filter_out,
    filter_out_bias,
    kept_lat,
    kept_lon,
    norm_gain,
    norm_bias,
    dense_in,
    dense_in_bias,
    dense_out,
    dense_out_bias,
):
    lon_count = lax.axis_size("lon")
    lat_count = lax.axis_size("lat")
    band_rows = patches.shape[0] // lon_count
    local_channels = patches.shape[2]
    local_blocks = filter_in.shape[1]
    block_width = filter_in.shape[2]
    row_span = lon_count * band_rows
    local_freqs = KEEP_LON // (lon_count * lat_count)
    local_rows = lax.all_to_all(patches, "lon", split_axis=0, concat_axis=1, tiled=True)
    raw = local_rows.astype(jnp.float32)
    cell_total = lax.psum(jnp.sum(raw, axis=-1, keepdims=True), "ch")
    pre_center = cell_total / C
    centered = raw - pre_center
    square_total = lax.psum(jnp.sum(centered * centered, axis=-1, keepdims=True), "ch")
    pre_spread = square_total / C
    prenormed = (
        centered * lax.rsqrt(pre_spread + norm_epsilon) * filter_norm_gain.astype(jnp.float32)
        + filter_norm_bias.astype(jnp.float32)
    ).astype(jnp.bfloat16)
    spectrum = jnp.einsum(
        "rwc,wtk->trkc", prenormed, lon_forward(KEEP_LON, W), preferred_element_type=jnp.float32
    )
    spectrum = spectrum.astype(jnp.bfloat16)
    slot_ids = jnp.arange(H, dtype=jnp.int32)
    group_ids = slot_ids // band_rows
    direct_rows = (
        group_ids % lat_count * row_span + group_ids // lat_count * band_rows + slot_ids % band_rows
    )
    pencil = lax.all_to_all(spectrum, ("lon", "lat"), split_axis=2, concat_axis=1, tiled=True)
    banded = jnp.dot(
        lat_forward_table(direct_rows, MLAT, H),
        pencil.reshape(2 * H, -1),
        preferred_element_type=jnp.float32,
    )
    banded = banded.astype(jnp.bfloat16).reshape(
        2, 2 * MLAT, local_freqs, local_blocks, block_width
    )
    first = complex_layer(banded, filter_in, filter_in_bias.reshape(2, local_blocks, block_width))
    first = jnp.maximum(first, 0.0).astype(jnp.bfloat16)
    second = complex_layer(first, filter_out, filter_out_bias.reshape(2, local_blocks, block_width))
    shrunk = jnp.sign(second) * jnp.maximum(jnp.abs(second) - shrink_level, 0.0)
    column_ids = (
        lax.axis_index("lon") * lat_count + lax.axis_index("lat")
    ) * local_freqs + jnp.arange(local_freqs, dtype=jnp.int32)
    band_slots = jnp.arange(2 * MLAT, dtype=jnp.int32)
    signed_band = jnp.where(band_slots < MLAT, band_slots, band_slots - 2 * MLAT)
    lat_ok = (signed_band[:, None] >= -kept_lat[None, :]) & (
        signed_band[:, None] < kept_lat[None, :]
    )
    lon_ok = column_ids[:, None] < kept_lon[None, :]
    keep_mask = (lat_ok[:, None, :] & lon_ok[None, :, :]).astype(jnp.float32)[..., None]
    kept_modes = (shrunk * keep_mask).astype(jnp.bfloat16).reshape(4 * MLAT, -1)
    spatial = jnp.dot(
        lat_inverse_table(direct_rows, MLAT, H), kept_modes, preferred_element_type=jnp.float32
    )
    spatial = spatial.astype(jnp.bfloat16).reshape(2, H, local_freqs, local_channels)
    returned = lax.all_to_all(spatial, ("lon", "lat"), split_axis=1, concat_axis=2, tiled=True)
    back_freqs = jnp.arange(KEEP_LON, dtype=jnp.int32)
    fine_part = jnp.einsum(
        "trkc,tkw->rwc", returned, lon_inverse(back_freqs, W), preferred_element_type=jnp.float32
    )
    mixed = (raw + fine_part).astype(jnp.bfloat16)
    gathered = lax.all_gather(mixed, "ch", axis=2, tiled=True)
    partial_terms = channel_mlp(gathered, norm_gain, norm_bias, dense_in, dense_in_bias, dense_out)
    summed = lax.psum_scatter(
        partial_terms.astype(jnp.bfloat16), "ch", scatter_dimension=2, tiled=True
    ).astype(jnp.float32)
    result = (mixed.astype(jnp.float32) + summed + dense_out_bias.astype(jnp.float32)).astype(
        jnp.bfloat16
    )
    return result.reshape(1, 1, band_rows, W, local_channels)


def solution(mesh):
    placed = (
        P(("grp", "lat"), "lon", "ch"),
        P("ch"),
        P("ch"),
        P(None, "ch", None, None),
        P(None, "ch"),
        P(None, "ch", None, None),
        P(None, "ch"),
        P("ch"),
        P("ch"),
        P(),
        P(),
        P(None, "ch"),
        P("ch"),
        P("ch", None),
        P("ch"),
    )
    sizes = mesh.shape
    lat_count, lon_count = sizes["lat"], sizes["lon"]
    cols = W // lon_count
    fits = lat_count == 2 and sizes["ch"] == 2 and MLAT % (lat_count * lon_count) == 0
    fits = fits and cols == 96 and H % (2 * lat_count * lon_count) == 0
    plan = functools.partial(column_plan, (32, 32, 32)) if fits else row_plan
    return jax.shard_map(
        plan,
        mesh=mesh,
        in_specs=placed,
        out_specs=P(("grp", "lat"), "lon", None, None, "ch"),
        check_vma=False,
    )
```

```python
import functools
import math

import jax
import jax.numpy as jnp
import numpy as np
from jax import lax
from jax.experimental import pallas as pl
from jax.experimental.pallas import tpu as pltpu
from jax.sharding import PartitionSpec as P

H = 256
W = 384
C = 768
MLAT = 64
KEEP_LON = 128

shrink_level = 0.01
norm_epsilon = 1e-05

COST_SHARE = 1

BF = jnp.bfloat16
F32 = jnp.float32


def angle_table(rows, cols, length):
    phase = rows[:, None] * cols[None, :] % length
    return phase * (2.0 * math.pi / length)


def lat_slots(lat_count, lon_count):
    per = MLAT // (lat_count * lon_count)
    freq, kind = [], []
    for dev in range(lat_count * lon_count):
        for pair in range(dev * per, dev * per + per):
            freq += [0, MLAT] if pair == 0 else [pair, pair]
            kind += [0, 0] if pair == 0 else [0, 1]
        freq.append(MLAT if dev == 0 else 0)
        kind.append(1 if dev == 0 else 2)
    return np.array(freq), np.array(kind)


def lat_tables(lat_count, lon_count):
    freq, kind = lat_slots(lat_count, lon_count)
    angles = angle_table(freq, np.arange(H), H)
    table = np.where(kind[:, None] == 0, np.cos(angles), -np.sin(angles)) / math.sqrt(H)
    table = np.where(kind[:, None] == 2, 0.0, table)
    return table.astype(np.float32)


def lon_tables(order):
    freqs = np.arange(KEEP_LON)
    angles = angle_table(freqs, order, W)
    factor = 1.0 / math.sqrt(W)
    weight = np.where(freqs == 0, 1.0, 2.0)[:, None]
    forward = np.concatenate([np.cos(angles) * factor, -np.sin(angles) * factor], axis=0)
    inverse = np.concatenate(
        [np.cos(angles) * factor * weight, -np.sin(angles) * factor * weight], axis=0
    ).T
    return forward.astype(np.float32).astype(jnp.bfloat16), inverse.astype(np.float32).astype(jnp.bfloat16)


def spread8(table):
    return np.kron(table, np.eye(8, dtype=np.float32)).astype(jnp.bfloat16)


def lat_forward_kernel(where_ref, cells_ref, table_ref, send_ref, keep_ref):
    rows, _, width = cells_ref.shape
    lon_count, slots, _, _ = send_ref.shape
    values = cells_ref[...].astype(F32).reshape(rows, 2, 8, width)
    pair = jnp.concatenate(
        [values[:, 0].reshape(rows * 8, width), values[:, 1].reshape(rows * 8, width)], axis=1
    ).astype(BF)
    half = table_ref.shape[0] // 2
    for part, out_ref in ((0, send_ref), (1, keep_ref)):
        total = jnp.dot(
            table_ref[part * half : (part + 1) * half, :], pair, preferred_element_type=F32
        )
        total = jnp.concatenate(
            [
                total[:, :width].reshape(lon_count, slots, 8, width),
                total[:, width:].reshape(lon_count, slots, 8, width),
            ],
            axis=2,
        ).astype(BF)
        for z in range(lon_count):
            out_ref[lax.rem(z + lon_count - where_ref[0], lon_count)] = total[z]


def lat_forward(where, cells, table, lon_count):
    rows, cols, width = cells.shape
    slots = table.shape[0] // (16 * lon_count)
    block = pl.BlockSpec((lon_count, slots, 16, width), lambda i: (0, 0, i, 0))
    return pl.pallas_call(
        lat_forward_kernel,
        grid=(cols // 16,),
        in_specs=[
            pl.BlockSpec(memory_space=pltpu.SMEM),
            pl.BlockSpec((rows, 16, width), lambda i: (0, i, 0)),
            pl.BlockSpec(table.shape, lambda i: (0, 0)),
        ],
        out_specs=[block, block],
        out_shape=[jax.ShapeDtypeStruct((lon_count, slots, cols, width), BF)] * 2,
        compiler_params=pltpu.CompilerParams(vmem_limit_bytes=40 << 20),
        cost_estimate=pl.CostEstimate(
            flops=2 * table.size * cols // 8 * width // COST_SHARE,
            bytes_accessed=4 * rows * cols * width // COST_SHARE,
            transcendentals=0,
        ),
        name="lat_forward",
    )(where, cells, table)


def lat_inverse_kernel(
    where_ref, own_ref, other_ref, table_ref, patches_ref, mine_ref, sent_ref, flat_ref
):
    rows, _, width = patches_ref.shape
    lon_count, slots = own_ref.shape[:2]
    blank = jnp.zeros((flat_ref.shape[1] - slots * 8, 2 * width), BF)
    for side, ref in enumerate((own_ref, other_ref)):
        for s in range(lon_count):
            values = ref[s].astype(F32).reshape(slots, 2, 8, width)
            flat = jnp.concatenate(
                [values[:, 0].reshape(slots * 8, width), values[:, 1].reshape(slots * 8, width)],
                axis=1,
            )
            source = lax.rem(where_ref[0] + (lon_count - s), lon_count)
            flat_ref[side * lon_count + source] = jnp.concatenate([flat.astype(BF), blank], axis=0)
    total = jnp.dot(
        table_ref[...], flat_ref[...].reshape(-1, 2 * width), preferred_element_type=F32
    )
    fine = jnp.concatenate(
        [total[:, :width].reshape(rows, 8, width), total[:, width:].reshape(rows, 8, width)], axis=1
    )
    mixed = (patches_ref[...].astype(F32) + fine).astype(BF)
    mixed = mixed.reshape(lon_count, 2, rows // (2 * lon_count), 16, width)

    @pl.when(where_ref[1] == 0)
    def _():
        mine_ref[...] = mixed[:, 0]
        sent_ref[...] = mixed[:, 1]

    @pl.when(where_ref[1] != 0)
    def _():
        mine_ref[...] = mixed[:, 1]
        sent_ref[...] = mixed[:, 0]


def lat_inverse(where, own, other, table, patches, first_col):
    lon_count, slots, cols, width = own.shape
    rows = patches.shape[0]
    first_block = first_col // 16
    spec = pl.BlockSpec((lon_count, slots, 16, width), lambda i: (0, 0, i, 0))
    half = rows // (2 * lon_count)
    out_spec = pl.BlockSpec((lon_count, half, 16, width), lambda i: (0, 0, i, 0))
    return pl.pallas_call(
        lat_inverse_kernel,
        grid=(cols // 16,),
        in_specs=[
            pl.BlockSpec(memory_space=pltpu.SMEM),
            spec,
            spec,
            pl.BlockSpec(table.shape, lambda i: (0, 0)),
            pl.BlockSpec((rows, 16, width), lambda i: (0, first_block + i, 0)),
        ],
        out_specs=[out_spec, out_spec],
        out_shape=[jax.ShapeDtypeStruct((lon_count, half, cols, width), BF)] * 2,
        scratch_shapes=[
            pltpu.VMEM((2 * lon_count, table.shape[1] // (2 * lon_count), 2 * width), BF)
        ],
        compiler_params=pltpu.CompilerParams(vmem_limit_bytes=40 << 20),
        cost_estimate=pl.CostEstimate(
            flops=2 * table.size * cols // 8 * width // COST_SHARE,
            bytes_accessed=6 * rows * cols * width // COST_SHARE,
            transcendentals=0,
        ),
        name="lat_inverse",
    )(where, own, other, table, patches)


def modes_kernel(inputs, first_pair_ref, lat_keep_ref, lon_keep_ref, *refs):
    pair_refs = refs[:inputs]
    spare_refs = refs[inputs : 2 * inputs]
    forward_ref, inverse_ref, w_in_ref, b_in_ref, w_out_ref, b_out_ref = refs[
        2 * inputs : 2 * inputs + 6
    ]
    out_refs, spare_ref = refs[2 * inputs + 6 : -1], refs[-1]
    width = pair_refs[0].shape[-1]
    per_step = pair_refs[0].shape[0] // 2
    step = pl.program_id(0)
    last_row = 2 * per_step * pl.num_programs(0)
    pair_id = first_pair_ref[0] + step * per_step
    special = pair_id == 0
    keep = KEEP_LON

    def columns(refs, row):
        return jnp.concatenate([ref[row] for ref in refs], axis=0)

    @pl.when(special)
    def _():
        spare_ref[...] = jnp.dot(
            forward_ref[...], columns(spare_refs, 0), preferred_element_type=F32
        )

    both = jnp.concatenate([columns(pair_refs, r) for r in range(2 * per_step)], axis=1)
    spectrum = jnp.dot(forward_ref[...], both, preferred_element_type=F32)
    banded = []
    for q in range(per_step):
        a = spectrum[:, 2 * q * width : (2 * q + 1) * width]
        b = spectrum[:, (2 * q + 1) * width : (2 * q + 2) * width]
        a_re, a_im, b_re, b_im = a[:keep], a[keep:], b[:keep], b[keep:]
        plus = [a_re - b_im, a_im + b_re]
        minus = [a_re + b_im, a_im - b_re]
        if q == 0:
            plus = [jnp.where(special, a_re, plus[0]), jnp.where(special, a_im, plus[1])]
            minus = [
                jnp.where(special, b_re + spare_ref[keep:], minus[0]),
                jnp.where(special, b_im - spare_ref[:keep], minus[1]),
            ]
        banded += [jnp.concatenate(plus, axis=1), jnp.concatenate(minus, axis=1)]
    banded = jnp.concatenate(banded, axis=0).astype(BF)
    first = jnp.dot(banded, w_in_ref[...], preferred_element_type=F32) + b_in_ref[...]
    first = jnp.maximum(first, 0.0).astype(BF)
    second = jnp.dot(first, w_out_ref[...], preferred_element_type=F32) + b_out_ref[...]
    shrunk = second - jnp.clip(second, -shrink_level, shrink_level)
    freq = lax.broadcasted_iota(jnp.int32, (keep, 2 * width), 0)
    lon_ok = freq < lon_keep_ref[...]
    upper, lower = [], []
    for q in range(per_step):
        plus_ok = lon_ok & (pair_id + q < lat_keep_ref[...])
        minus_id = jnp.where(special, MLAT, pair_id) if q == 0 else pair_id + q
        minus_ok = lon_ok & (minus_id <= lat_keep_ref[...])
        plus = jnp.where(plus_ok, shrunk[2 * q * keep : (2 * q + 1) * keep], 0.0)
        minus = jnp.where(minus_ok, shrunk[(2 * q + 1) * keep : (2 * q + 2) * keep], 0.0)
        p_re, p_im, m_re, m_im = plus[:, :width], plus[:, width:], minus[:, :width], minus[:, width:]
        tops = [p_re + m_re, p_im - m_im]
        bottoms = [p_im + m_im, m_re - p_re]
        if q == 0:
            tops = [jnp.where(special, p_re, tops[0]), jnp.where(special, m_re, tops[1])]
            bottoms = [jnp.where(special, p_im, bottoms[0]), jnp.where(special, m_im, bottoms[1])]
            loose = jnp.concatenate([-m_im, m_re], axis=0).astype(BF)
        upper += tops
        lower += bottoms
    values = jnp.concatenate(
        [jnp.concatenate(upper, axis=1), jnp.concatenate(lower, axis=1)], axis=0
    ).astype(BF)

    def back(values, row):
        grid_values = jnp.dot(inverse_ref[...], values, preferred_element_type=F32).astype(BF)
        start = 0
        for ref in out_refs:
            cols = ref.shape[1]
            for r in range(grid_values.shape[1] // width):
                ref[row + r] = grid_values[start : start + cols, r * width : (r + 1) * width]
            start += cols

    back(values, 2 * per_step * step)

    @pl.when(special)
    def _():
        back(loose, last_row)

    @pl.when(jnp.logical_and(step == 0, jnp.logical_not(special)))
    def _():
        for ref in out_refs:
            ref[last_row] = jnp.zeros(ref.shape[1:], BF)


def modes(received, first_pair, lat_keep, lon_keep, forward, inverse, w_in, b_in, w_out, b_out):
    lon_count = len(received[0])
    flat = [values for chunk in received for values in chunk]
    slots, _, width = flat[0].shape
    pairs = slots // 2
    per_step = 2 if pairs % 2 == 0 else 1
    pair_specs = [pl.BlockSpec((2 * per_step, r.shape[1], width), lambda i: (i, 0, 0)) for r in flat]
    spare_specs = [pl.BlockSpec((1, r.shape[1], width), lambda i: (slots - 1, 0, 0)) for r in flat]
    whole = lambda array: pl.BlockSpec(array.shape, lambda i: (0,) * array.ndim)
    out = pl.pallas_call(
        functools.partial(modes_kernel, len(flat)),
        grid=(pairs // per_step,),
        in_specs=[pl.BlockSpec(memory_space=pltpu.SMEM), whole(lat_keep), whole(lon_keep)]
        + pair_specs
        + spare_specs
        + [whole(forward), whole(inverse), whole(w_in), whole(b_in), whole(w_out), whole(b_out)],
        out_specs=[pl.BlockSpec(r.shape, lambda i: (0, 0, 0)) for r in flat],
        out_shape=[jax.ShapeDtypeStruct(r.shape, BF) for r in flat],
        scratch_shapes=[pltpu.VMEM((2 * KEEP_LON, width), F32)],
        compiler_params=pltpu.CompilerParams(vmem_limit_bytes=48 << 20),
        cost_estimate=pl.CostEstimate(
            flops=pairs * 2 * (2 * 2 * KEEP_LON * W * 2 * width + 4 * KEEP_LON * 4 * width * width),
            bytes_accessed=4 * slots * W * width,
            transcendentals=0,
        ),
        name="modes",
    )(
        first_pair, lat_keep, lon_keep, *flat, *flat,
        forward, inverse, w_in, b_in, w_out, b_out,
    )
    return [list(out[i : i + lon_count]) for i in range(0, len(flat), lon_count)]


def mlp_kernel(
    where_ref, own_ref, other_ref, gain_ref, bias_ref, w_in_ref, b_in_ref, w_out_ref, b_out_ref,
    out_ref,
):
    _, rows, cols, width = own_ref.shape
    cells = rows * cols
    own = own_ref[0].reshape(cells, width)
    other = other_ref[0].reshape(cells, width)
    flip = where_ref[1] == 1
    low = jnp.where(flip, other, own)
    high = jnp.where(flip, own, other)
    wide = jnp.concatenate([low, high], axis=1).astype(F32)
    center = jnp.mean(wide, axis=1, keepdims=True)
    off = wide - center
    spread = jnp.mean(off * off, axis=1, keepdims=True)
    normed = (off * lax.rsqrt(spread + norm_epsilon) * gain_ref[...] + bias_ref[...]).astype(BF)
    hidden = jnp.dot(normed, w_in_ref[...], preferred_element_type=F32) + b_in_ref[...]
    hidden = (hidden * (0.5 + 0.5 * lax.erf(hidden * math.sqrt(0.5)))).astype(BF)
    total = jnp.dot(hidden, w_out_ref[...], preferred_element_type=F32) + wide + b_out_ref[...]
    total = total.astype(BF)
    out_ref[0, 0] = total[:, :width].reshape(rows, cols, width)
    out_ref[0, 1] = total[:, width:].reshape(rows, cols, width)


def mlp(where, own, other, gain, bias, w_in, b_in, w_out, b_out):
    lon_count, rows, cols, width = own.shape
    whole = lambda array: pl.BlockSpec(array.shape, lambda i, where: (0,) * array.ndim)
    cell_spec = pl.BlockSpec((1, rows, cols, width), lambda i, where: (i, 0, 0, 0))
    cells = lon_count * rows * cols
    return pl.pallas_call(
        mlp_kernel,
        grid_spec=pltpu.PrefetchScalarGridSpec(
            num_scalar_prefetch=1,
            grid=(lon_count,),
            in_specs=[cell_spec, cell_spec]
            + [whole(a) for a in (gain, bias, w_in, b_in, w_out, b_out)],
            out_specs=pl.BlockSpec((1, 2, rows, cols, width), lambda i, where: (i, 0, 0, 0, 0)),
        ),
        out_shape=jax.ShapeDtypeStruct((lon_count, 2, rows, cols, width), BF),
        compiler_params=pltpu.CompilerParams(vmem_limit_bytes=48 << 20),
        cost_estimate=pl.CostEstimate(
            flops=4 * cells * w_in.size // COST_SHARE,
            bytes_accessed=8 * cells * width // COST_SHARE,
            transcendentals=cells * w_in.shape[1] // COST_SHARE,
        ),
        name="channel_mlp",
    )(where, own, other, gain, bias, w_in, b_in, w_out, b_out)


def assemble_kernel(piece_ref, *refs):
    out_ref = refs[-1]
    half = piece_ref.shape[2]
    for c in range(2):
        out_ref[c * half : (c + 1) * half] = piece_ref[0, c]


def assemble(result, pieces, first_col, block_cols):
    lon_count, _, rows, cols, width = pieces.shape
    block = math.gcd(math.gcd(cols, block_cols), first_col)
    specs = [pl.BlockSpec((1, 2, rows, block, width), lambda z, j: (z, 0, 0, j, 0))]
    operands = [pieces]
    aliases = {}
    if result is not None:
        aliases = {1: 0}
        operands.append(result)
        specs.append(pl.BlockSpec(memory_space=pl.ANY))
    return pl.pallas_call(
        assemble_kernel,
        grid=(lon_count, cols // block),
        in_specs=specs,
        out_specs=pl.BlockSpec(
            (2 * rows, block, width),
            lambda z, j: (0, z * (block_cols // block) + first_col // block + j, 0),
        ),
        out_shape=jax.ShapeDtypeStruct((2 * rows, lon_count * block_cols, width), BF),
        input_output_aliases=aliases,
        cost_estimate=pl.CostEstimate(
            flops=0, bytes_accessed=8 * lon_count * rows * cols * width, transcendentals=0
        ),
        name="assemble",
    )(*operands)


def block_diagonal(weight):
    blocks, n = weight.shape[1], weight.shape[2]
    eye = jnp.eye(blocks, dtype=weight.dtype)
    spread = (weight[:, :, :, None, :] * eye[None, :, None, :, None]).reshape(
        2, blocks * n, blocks * n
    )
    return jnp.concatenate(
        [
            jnp.concatenate([spread[0], spread[1]], axis=1),
            jnp.concatenate([-spread[1], spread[0]], axis=1),
        ],
        axis=0,
    )


def swap(values, axis):
    return lax.ppermute(values, axis, [(0, 1), (1, 0)])


def shift(values, steps, lon_count):
    if steps == 0:
        return values
    return lax.ppermute(values, "lon", [(z, (z + steps) % lon_count) for z in range(lon_count)])


def column_plan(
    widths,
    patches,
    filter_norm_gain,
    filter_norm_bias,
    filter_in,
    filter_in_bias,
    filter_out,
    filter_out_bias,
    kept_lat,
    kept_lon,
    norm_gain,
    norm_bias,
    dense_in,
    dense_in_bias,
    dense_out,
    dense_out_bias,
):
    lon_count = lax.axis_size("lon")
    lat_count = lax.axis_size("lat")
    rows, cols, width = patches.shape
    chunks = len(widths)
    starts = [sum(widths[:i]) for i in range(chunks)]
    block_width = filter_in.shape[2]
    lat_id = lax.axis_index("lat")
    lon_id = lax.axis_index("lon")
    ch_id = lax.axis_index("ch")
    pairs = MLAT // (lat_count * lon_count)
    slots = 2 * pairs + 1

    lat_table = lat_tables(lat_count, lon_count).reshape(lat_count, lon_count, slots, H)
    forward_all, inverse_all = [], []
    for a in range(lat_count):
        here = lat_table[..., a * rows : (a + 1) * rows]
        ordered = np.concatenate([here[1 - a], here[a]], axis=0).reshape(-1, rows)
        forward_all.append(spread8(ordered))
        ordered = np.concatenate([here[a], here[1 - a]], axis=0)
        ordered = np.pad(ordered, ((0, 0), (0, slots % 2), (0, 0))).reshape(-1, rows)
        inverse_all.append(spread8(ordered.T))
    forward_lat = lax.dynamic_index_in_dim(jnp.asarray(np.stack(forward_all)), lat_id, 0, False)
    inverse_lat = None

    ids = np.arange(W).reshape(lon_count, cols)

    def column_order(devices):
        return np.concatenate([ids[devices, c : c + w].reshape(-1) for c, w in zip(starts, widths)])

    steps = np.arange(lon_count)
    from_here = [lon_tables(column_order((z - steps) % lon_count))[0] for z in range(lon_count)]
    to_there = [lon_tables(column_order((z + steps) % lon_count))[1] for z in range(lon_count)]

    fence = lax.optimization_barrier
    where = jnp.stack([lon_id, ch_id]).astype(jnp.int32)

    def row_transform(i, source):
        raw = source[:, starts[i] : starts[i] + widths[i]].astype(F32)
        center = jnp.mean(raw, axis=-1)
        off = raw - center[..., None]
        square = jnp.sum(off * off, axis=-1)
        theirs = swap(jnp.stack([center, square]), "ch")
        mean = 0.5 * (center + theirs[0])
        gap = center - theirs[0]
        spread = (square + theirs[1]) / C + 0.25 * gap * gap
        scale = lax.rsqrt(spread + norm_epsilon)
        prenormed = (
            (raw - mean[..., None]) * scale[..., None] * filter_norm_gain.astype(F32)
            + filter_norm_bias.astype(F32)
        ).astype(BF)
        return lat_forward(where, prenormed, forward_lat, lon_count)

    def mlp_weights(dense_in, dense_in_bias, dense_out, dense_out_bias):
        return (
            norm_gain.astype(F32)[None],
            norm_bias.astype(F32)[None],
            jnp.concatenate([dense_in, swap(dense_in, "ch")], axis=1),
            jnp.concatenate([dense_in_bias, swap(dense_in_bias, "ch")]).astype(F32)[None],
            jnp.concatenate([dense_out, swap(dense_out, "ch")], axis=0),
            lax.all_gather(dense_out_bias, "ch", axis=0, tiled=True).astype(F32)[None],
        )

    def filter_operands():
        return (
            ((lat_id * lon_count + lon_id) * pairs).astype(jnp.int32).reshape(1),
            jnp.tile(jnp.repeat(kept_lat, block_width), 2).reshape(1, -1),
            jnp.tile(jnp.repeat(kept_lon, block_width), 2).reshape(1, -1),
            lax.dynamic_index_in_dim(jnp.asarray(np.stack(from_here)), lon_id, 0, False),
            lax.dynamic_index_in_dim(jnp.asarray(np.stack(to_there)), lon_id, 0, False),
            block_diagonal(filter_in),
            filter_in_bias.reshape(1, -1).astype(F32),
            block_diagonal(filter_out),
            filter_out_bias.reshape(1, -1).astype(F32),
        )

    def along_lon(values):
        return [shift(values[s], s, lon_count) for s in range(lon_count)]

    def row_result(i, own, other):
        mine, sent = lat_inverse(where, own, other, inverse_lat, patches, starts[i])
        return mlp(where, mine, swap(sent, "ch"), *weights)

    def outward(outputs):
        shape = outputs.shape
        flat = outputs.reshape((shape[0] * 2,) + shape[2:])
        return lax.all_to_all(flat, ("lon", "ch"), 0, 0, tiled=True).reshape(shape)

    received, summed, sent, kept = [], None, None, None
    weights = None
    filter_args = None
    dense = (dense_in, dense_in_bias, dense_out, dense_out_bias)
    for step in range(chunks + 2):
        arrived = None
        if sent is not None:
            arrived = (kept, swap(sent, "lat"))
            sent = None
        if summed is not None:
            received.append(along_lon(summed))
            summed = None
        if step < chunks:
            sent, kept = row_transform(step, patches)
        elif step == chunks:
            filter_args = filter_operands()
        else:
            weights = mlp_weights(*dense)
            inverse_lat = lax.dynamic_index_in_dim(jnp.asarray(np.stack(inverse_all)), lat_id, 0, False)
        patches, arrived, sent, kept, received, filter_args, weights, inverse_lat, dense = fence(
            (patches, arrived, sent, kept, received, filter_args, weights, inverse_lat, dense)
        )
        if arrived is not None:
            summed = [
                (arrived[0][s].astype(F32) + arrived[1][s].astype(F32)).astype(BF)
                for s in range(lon_count)
            ]

    filtered = modes(received, *filter_args)

    owns = [None] * chunks
    others = [None] * chunks
    outputs = [None] * chunks
    for step in range(chunks):
        owns[step] = along_lon(filtered[step])
        if step >= 1:
            owns[step - 1] = jnp.stack(owns[step - 1])
            others[step - 1] = swap(owns[step - 1], "lat")
        if step >= 2:
            outputs[step - 2] = row_result(step - 2, owns[step - 2], others[step - 2])
        patches, filtered, owns, others, outputs = fence((patches, filtered, owns, others, outputs))

    result = None
    pieces = None
    for i in range(chunks):
        last = pieces
        pieces = outward(outputs[i])
        if last is not None:
            result = assemble(result, last, starts[i - 1], cols)
        if i + 1 < chunks and outputs[i + 1] is None:
            outputs[i + 1] = row_result(i + 1, owns[i + 1], others[i + 1])
        if i + 2 < chunks and others[i + 2] is None:
            owns[i + 2] = jnp.stack(owns[i + 2])
            others[i + 2] = swap(owns[i + 2], "lat")
        patches, owns, others, outputs, pieces, result = fence(
            (patches, owns, others, outputs, pieces, result)
        )
    result = assemble(result, pieces, starts[chunks - 1], cols)
    return result.reshape(1, 1, rows // lon_count, lon_count * cols, width)


def lon_forward(number, length):
    freq_ids = jnp.arange(number, dtype=jnp.int32)
    cell_ids = jnp.arange(length, dtype=jnp.int32)
    phase_turns = cell_ids[:, None] * freq_ids[None, :] % length
    angles = phase_turns.astype(jnp.float32) * (2.0 * math.pi / length)
    factor = 1.0 / math.sqrt(length)
    return jnp.stack([jnp.cos(angles) * factor, -jnp.sin(angles) * factor], axis=1).astype(
        jnp.bfloat16
    )


def lon_inverse(freq_ids, length):
    cell_ids = jnp.arange(length, dtype=jnp.int32)
    phase_turns = freq_ids[:, None] * cell_ids[None, :] % length
    angles = phase_turns.astype(jnp.float32) * (2.0 * math.pi / length)
    factor = 1.0 / math.sqrt(length)
    weight = jnp.where(freq_ids == 0, 1.0, 2.0).astype(jnp.float32)[:, None]
    return jnp.stack(
        [jnp.cos(angles) * factor * weight, -jnp.sin(angles) * factor * weight]
    ).astype(jnp.bfloat16)


def band_ids(half_band, length):
    slot_ids = jnp.arange(2 * half_band, dtype=jnp.int32)
    return jnp.where(slot_ids < half_band, slot_ids, slot_ids + length - 2 * half_band)


def lat_forward_table(row_ids, half_band, length):
    phase_turns = band_ids(half_band, length)[:, None] * row_ids[None, :] % length
    angles = phase_turns.astype(jnp.float32) * (2.0 * math.pi / length)
    factor = 1.0 / math.sqrt(length)
    cosine = jnp.cos(angles) * factor
    sine_part = jnp.sin(angles) * factor
    upper_half = jnp.concatenate([cosine, sine_part], axis=1)
    bottom = jnp.concatenate([-sine_part, cosine], axis=1)
    return jnp.concatenate([upper_half, bottom], axis=0).astype(jnp.bfloat16)


def lat_inverse_table(row_ids, half_band, length):
    phase_turns = row_ids[:, None] * band_ids(half_band, length)[None, :] % length
    angles = phase_turns.astype(jnp.float32) * (2.0 * math.pi / length)
    factor = 1.0 / math.sqrt(length)
    cosine = jnp.cos(angles) * factor
    sine_part = jnp.sin(angles) * factor
    upper_half = jnp.concatenate([cosine, -sine_part], axis=1)
    bottom = jnp.concatenate([sine_part, cosine], axis=1)
    return jnp.concatenate([upper_half, bottom], axis=0).astype(jnp.bfloat16)


def complex_layer(values, weight, offset):
    products = jnp.einsum("tjkbc,ubcd->tujkbd", values, weight, preferred_element_type=jnp.float32)
    offset = offset.astype(jnp.float32)
    real_part = products[0, 0] - products[1, 1] + offset[0]
    imag_part = products[1, 0] + products[0, 1] + offset[1]
    return jnp.stack([real_part, imag_part])


def channel_mlp(mixed_full, norm_gain, norm_bias, weight_in, bias_in, weight_out):
    wide = mixed_full.astype(jnp.float32)
    center = jnp.mean(wide, axis=-1, keepdims=True)
    spread = jnp.mean((wide - center) ** 2, axis=-1, keepdims=True)
    normed = (
        (wide - center) * lax.rsqrt(spread + norm_epsilon) * norm_gain.astype(jnp.float32)
        + norm_bias.astype(jnp.float32)
    ).astype(jnp.bfloat16)
    hidden = jnp.einsum("rwc,cu->rwu", normed, weight_in, preferred_element_type=jnp.float32)
    hidden = jax.nn.gelu(hidden + bias_in.astype(jnp.float32), approximate=False).astype(
        jnp.bfloat16
    )
    return jnp.einsum("rwu,uc->rwc", hidden, weight_out, preferred_element_type=jnp.float32)


def row_plan(
    patches,
    filter_norm_gain,
    filter_norm_bias,
    filter_in,
    filter_in_bias,
    filter_out,
    filter_out_bias,
    kept_lat,
    kept_lon,
    norm_gain,
    norm_bias,
    dense_in,
    dense_in_bias,
    dense_out,
    dense_out_bias,
):
    lon_count = lax.axis_size("lon")
    lat_count = lax.axis_size("lat")
    band_rows = patches.shape[0] // lon_count
    local_channels = patches.shape[2]
    local_blocks = filter_in.shape[1]
    block_width = filter_in.shape[2]
    row_span = lon_count * band_rows
    local_freqs = KEEP_LON // (lon_count * lat_count)
    local_rows = lax.all_to_all(patches, "lon", split_axis=0, concat_axis=1, tiled=True)
    raw = local_rows.astype(jnp.float32)
    cell_total = lax.psum(jnp.sum(raw, axis=-1, keepdims=True), "ch")
    pre_center = cell_total / C
    centered = raw - pre_center
    square_total = lax.psum(jnp.sum(centered * centered, axis=-1, keepdims=True), "ch")
    pre_spread = square_total / C
    prenormed = (
        centered * lax.rsqrt(pre_spread + norm_epsilon) * filter_norm_gain.astype(jnp.float32)
        + filter_norm_bias.astype(jnp.float32)
    ).astype(jnp.bfloat16)
    spectrum = jnp.einsum(
        "rwc,wtk->trkc", prenormed, lon_forward(KEEP_LON, W), preferred_element_type=jnp.float32
    )
    spectrum = spectrum.astype(jnp.bfloat16)
    slot_ids = jnp.arange(H, dtype=jnp.int32)
    group_ids = slot_ids // band_rows
    direct_rows = (
        group_ids % lat_count * row_span + group_ids // lat_count * band_rows + slot_ids % band_rows
    )
    pencil = lax.all_to_all(spectrum, ("lon", "lat"), split_axis=2, concat_axis=1, tiled=True)
    banded = jnp.dot(
        lat_forward_table(direct_rows, MLAT, H),
        pencil.reshape(2 * H, -1),
        preferred_element_type=jnp.float32,
    )
    banded = banded.astype(jnp.bfloat16).reshape(
        2, 2 * MLAT, local_freqs, local_blocks, block_width
    )
    first = complex_layer(banded, filter_in, filter_in_bias.reshape(2, local_blocks, block_width))
    first = jnp.maximum(first, 0.0).astype(jnp.bfloat16)
    second = complex_layer(first, filter_out, filter_out_bias.reshape(2, local_blocks, block_width))
    shrunk = jnp.sign(second) * jnp.maximum(jnp.abs(second) - shrink_level, 0.0)
    column_ids = (
        lax.axis_index("lon") * lat_count + lax.axis_index("lat")
    ) * local_freqs + jnp.arange(local_freqs, dtype=jnp.int32)
    band_slots = jnp.arange(2 * MLAT, dtype=jnp.int32)
    signed_band = jnp.where(band_slots < MLAT, band_slots, band_slots - 2 * MLAT)
    lat_ok = (signed_band[:, None] >= -kept_lat[None, :]) & (
        signed_band[:, None] < kept_lat[None, :]
    )
    lon_ok = column_ids[:, None] < kept_lon[None, :]
    keep_mask = (lat_ok[:, None, :] & lon_ok[None, :, :]).astype(jnp.float32)[..., None]
    kept_modes = (shrunk * keep_mask).astype(jnp.bfloat16).reshape(4 * MLAT, -1)
    spatial = jnp.dot(
        lat_inverse_table(direct_rows, MLAT, H), kept_modes, preferred_element_type=jnp.float32
    )
    spatial = spatial.astype(jnp.bfloat16).reshape(2, H, local_freqs, local_channels)
    returned = lax.all_to_all(spatial, ("lon", "lat"), split_axis=1, concat_axis=2, tiled=True)
    back_freqs = jnp.arange(KEEP_LON, dtype=jnp.int32)
    fine_part = jnp.einsum(
        "trkc,tkw->rwc", returned, lon_inverse(back_freqs, W), preferred_element_type=jnp.float32
    )
    mixed = (raw + fine_part).astype(jnp.bfloat16)
    gathered = lax.all_gather(mixed, "ch", axis=2, tiled=True)
    partial_terms = channel_mlp(gathered, norm_gain, norm_bias, dense_in, dense_in_bias, dense_out)
    summed = lax.psum_scatter(
        partial_terms.astype(jnp.bfloat16), "ch", scatter_dimension=2, tiled=True
    ).astype(jnp.float32)
    result = (mixed.astype(jnp.float32) + summed + dense_out_bias.astype(jnp.float32)).astype(
        jnp.bfloat16
    )
    return result.reshape(1, 1, band_rows, W, local_channels)


def solution(mesh):
    placed = (
        P(("grp", "lat"), "lon", "ch"),
        P("ch"),
        P("ch"),
        P(None, "ch", None, None),
        P(None, "ch"),
        P(None, "ch", None, None),
        P(None, "ch"),
        P("ch"),
        P("ch"),
        P(),
        P(),
        P(None, "ch"),
        P("ch"),
        P("ch", None),
        P("ch"),
    )
    sizes = mesh.shape
    lat_count, lon_count = sizes["lat"], sizes["lon"]
    cols = W // lon_count
    fits = lat_count == 2 and sizes["ch"] == 2 and MLAT % (lat_count * lon_count) == 0
    fits = fits and cols == 96 and H % (2 * lat_count * lon_count) == 0
    plan = functools.partial(column_plan, (32, 32, 32)) if fits else row_plan
    return jax.shard_map(
        plan,
        mesh=mesh,
        in_specs=placed,
        out_specs=P(("grp", "lat"), "lon", None, None, "ch"),
        check_vma=False,
    )
```

```python
import functools
import math

import jax
import jax.numpy as jnp
import numpy as np
from jax import lax
from jax.experimental import pallas as pl
from jax.experimental.pallas import tpu as pltpu
from jax.sharding import PartitionSpec as P

H = 256
W = 384
C = 768
MLAT = 64
KEEP_LON = 128

shrink_level = 0.01
norm_epsilon = 1e-05

COST_SHARE = 1

BF = jnp.bfloat16
F32 = jnp.float32


def angle_table(rows, cols, length):
    phase = rows[:, None] * cols[None, :] % length
    return phase * (2.0 * math.pi / length)


def lat_slots(lat_count, lon_count):
    per = MLAT // (lat_count * lon_count)
    freq, kind = [], []
    for dev in range(lat_count * lon_count):
        for pair in range(dev * per, dev * per + per):
            freq += [0, MLAT] if pair == 0 else [pair, pair]
            kind += [0, 0] if pair == 0 else [0, 1]
        freq.append(MLAT if dev == 0 else 0)
        kind.append(1 if dev == 0 else 2)
    return np.array(freq), np.array(kind)


def lat_tables(lat_count, lon_count):
    freq, kind = lat_slots(lat_count, lon_count)
    angles = angle_table(freq, np.arange(H), H)
    table = np.where(kind[:, None] == 0, np.cos(angles), -np.sin(angles)) / math.sqrt(H)
    table = np.where(kind[:, None] == 2, 0.0, table)
    return table.astype(np.float32)


def lon_tables(order):
    freqs = np.arange(KEEP_LON)
    angles = angle_table(freqs, order, W)
    factor = 1.0 / math.sqrt(W)
    weight = np.where(freqs == 0, 1.0, 2.0)[:, None]
    forward = np.concatenate([np.cos(angles) * factor, -np.sin(angles) * factor], axis=0)
    inverse = np.concatenate(
        [np.cos(angles) * factor * weight, -np.sin(angles) * factor * weight], axis=0
    ).T
    return forward.astype(np.float32).astype(jnp.bfloat16), inverse.astype(np.float32).astype(jnp.bfloat16)


def spread8(table):
    return np.kron(table, np.eye(8, dtype=np.float32)).astype(jnp.bfloat16)


def lat_forward_kernel(where_ref, cells_ref, table_ref, send_ref, keep_ref):
    rows, _, width = cells_ref.shape
    lon_count, slots, _, _ = send_ref.shape
    values = cells_ref[...].astype(F32).reshape(rows, 2, 8, width)
    pair = jnp.concatenate(
        [values[:, 0].reshape(rows * 8, width), values[:, 1].reshape(rows * 8, width)], axis=1
    ).astype(BF)
    half = table_ref.shape[0] // 2
    for part, out_ref in ((0, send_ref), (1, keep_ref)):
        total = jnp.dot(
            table_ref[part * half : (part + 1) * half, :], pair, preferred_element_type=F32
        )
        total = jnp.concatenate(
            [
                total[:, :width].reshape(lon_count, slots, 8, width),
                total[:, width:].reshape(lon_count, slots, 8, width),
            ],
            axis=2,
        ).astype(BF)
        for z in range(lon_count):
            out_ref[lax.rem(z + lon_count - where_ref[0], lon_count)] = total[z]


def lat_forward(where, cells, table, lon_count):
    rows, cols, width = cells.shape
    slots = table.shape[0] // (16 * lon_count)
    block = pl.BlockSpec((lon_count, slots, 16, width), lambda i: (0, 0, i, 0))
    return pl.pallas_call(
        lat_forward_kernel,
        grid=(cols // 16,),
        in_specs=[
            pl.BlockSpec(memory_space=pltpu.SMEM),
            pl.BlockSpec((rows, 16, width), lambda i: (0, i, 0)),
            pl.BlockSpec(table.shape, lambda i: (0, 0)),
        ],
        out_specs=[block, block],
        out_shape=[jax.ShapeDtypeStruct((lon_count, slots, cols, width), BF)] * 2,
        compiler_params=pltpu.CompilerParams(vmem_limit_bytes=40 << 20),
        cost_estimate=pl.CostEstimate(
            flops=2 * table.size * cols // 8 * width // COST_SHARE,
            bytes_accessed=4 * rows * cols * width // COST_SHARE,
            transcendentals=0,
        ),
        name="lat_forward",
    )(where, cells, table)


def lat_inverse_kernel(
    where_ref, own_ref, other_ref, table_ref, patches_ref, mine_ref, sent_ref, flat_ref
):
    rows, _, width = patches_ref.shape
    lon_count, slots = own_ref.shape[:2]
    blank = jnp.zeros((flat_ref.shape[1] - slots * 8, 2 * width), BF)
    for side, ref in enumerate((own_ref, other_ref)):
        for s in range(lon_count):
            values = ref[s].astype(F32).reshape(slots, 2, 8, width)
            flat = jnp.concatenate(
                [values[:, 0].reshape(slots * 8, width), values[:, 1].reshape(slots * 8, width)],
                axis=1,
            )
            source = lax.rem(where_ref[0] + (lon_count - s), lon_count)
            flat_ref[side * lon_count + source] = jnp.concatenate([flat.astype(BF), blank], axis=0)
    total = jnp.dot(
        table_ref[...], flat_ref[...].reshape(-1, 2 * width), preferred_element_type=F32
    )
    fine = jnp.concatenate(
        [total[:, :width].reshape(rows, 8, width), total[:, width:].reshape(rows, 8, width)], axis=1
    )
    mixed = (patches_ref[...].astype(F32) + fine).astype(BF)
    mixed = mixed.reshape(lon_count, 2, rows // (2 * lon_count), 16, width)

    @pl.when(where_ref[1] == 0)
    def _():
        mine_ref[...] = mixed[:, 0]
        sent_ref[...] = mixed[:, 1]

    @pl.when(where_ref[1] != 0)
    def _():
        mine_ref[...] = mixed[:, 1]
        sent_ref[...] = mixed[:, 0]


def lat_inverse(where, own, other, table, patches, first_col):
    lon_count, slots, cols, width = own.shape
    rows = patches.shape[0]
    first_block = first_col // 16
    spec = pl.BlockSpec((lon_count, slots, 16, width), lambda i: (0, 0, i, 0))
    half = rows // (2 * lon_count)
    out_spec = pl.BlockSpec((lon_count, half, 16, width), lambda i: (0, 0, i, 0))
    return pl.pallas_call(
        lat_inverse_kernel,
        grid=(cols // 16,),
        in_specs=[
            pl.BlockSpec(memory_space=pltpu.SMEM),
            spec,
            spec,
            pl.BlockSpec(table.shape, lambda i: (0, 0)),
            pl.BlockSpec((rows, 16, width), lambda i: (0, first_block + i, 0)),
        ],
        out_specs=[out_spec, out_spec],
        out_shape=[jax.ShapeDtypeStruct((lon_count, half, cols, width), BF)] * 2,
        scratch_shapes=[
            pltpu.VMEM((2 * lon_count, table.shape[1] // (2 * lon_count), 2 * width), BF)
        ],
        compiler_params=pltpu.CompilerParams(vmem_limit_bytes=40 << 20),
        cost_estimate=pl.CostEstimate(
            flops=2 * table.size * cols // 8 * width // COST_SHARE,
            bytes_accessed=6 * rows * cols * width // COST_SHARE,
            transcendentals=0,
        ),
        name="lat_inverse",
    )(where, own, other, table, patches)


def modes_kernel(inputs, first_pair_ref, lat_keep_ref, lon_keep_ref, *refs):
    pair_refs = refs[:inputs]
    spare_refs = refs[inputs : 2 * inputs]
    forward_ref, inverse_ref, w_in_ref, b_in_ref, w_out_ref, b_out_ref = refs[
        2 * inputs : 2 * inputs + 6
    ]
    out_refs, spare_ref = refs[2 * inputs + 6 : -1], refs[-1]
    width = pair_refs[0].shape[-1]
    per_step = pair_refs[0].shape[0] // 2
    step = pl.program_id(0)
    last_row = 2 * per_step * pl.num_programs(0)
    pair_id = first_pair_ref[0] + step * per_step
    special = pair_id == 0
    keep = KEEP_LON

    def columns(refs, row):
        return jnp.concatenate([ref[row] for ref in refs], axis=0)

    @pl.when(special)
    def _():
        spare_ref[...] = jnp.dot(
            forward_ref[...], columns(spare_refs, 0), preferred_element_type=F32
        )

    both = jnp.concatenate([columns(pair_refs, r) for r in range(2 * per_step)], axis=1)
    spectrum = jnp.dot(forward_ref[...], both, preferred_element_type=F32)
    banded = []
    for q in range(per_step):
        a = spectrum[:, 2 * q * width : (2 * q + 1) * width]
        b = spectrum[:, (2 * q + 1) * width : (2 * q + 2) * width]
        a_re, a_im, b_re, b_im = a[:keep], a[keep:], b[:keep], b[keep:]
        plus = [a_re - b_im, a_im + b_re]
        minus = [a_re + b_im, a_im - b_re]
        if q == 0:
            plus = [jnp.where(special, a_re, plus[0]), jnp.where(special, a_im, plus[1])]
            minus = [
                jnp.where(special, b_re + spare_ref[keep:], minus[0]),
                jnp.where(special, b_im - spare_ref[:keep], minus[1]),
            ]
        banded += [jnp.concatenate(plus, axis=1), jnp.concatenate(minus, axis=1)]
    banded = jnp.concatenate(banded, axis=0).astype(BF)
    first = jnp.dot(banded, w_in_ref[...], preferred_element_type=F32) + b_in_ref[...]
    first = jnp.maximum(first, 0.0).astype(BF)
    second = jnp.dot(first, w_out_ref[...], preferred_element_type=F32) + b_out_ref[...]
    shrunk = second - jnp.clip(second, -shrink_level, shrink_level)
    freq = lax.broadcasted_iota(jnp.int32, (keep, 2 * width), 0)
    lon_ok = freq < lon_keep_ref[...]
    upper, lower = [], []
    for q in range(per_step):
        plus_ok = lon_ok & (pair_id + q < lat_keep_ref[...])
        minus_id = jnp.where(special, MLAT, pair_id) if q == 0 else pair_id + q
        minus_ok = lon_ok & (minus_id <= lat_keep_ref[...])
        plus = jnp.where(plus_ok, shrunk[2 * q * keep : (2 * q + 1) * keep], 0.0)
        minus = jnp.where(minus_ok, shrunk[(2 * q + 1) * keep : (2 * q + 2) * keep], 0.0)
        p_re, p_im, m_re, m_im = plus[:, :width], plus[:, width:], minus[:, :width], minus[:, width:]
        tops = [p_re + m_re, p_im - m_im]
        bottoms = [p_im + m_im, m_re - p_re]
        if q == 0:
            tops = [jnp.where(special, p_re, tops[0]), jnp.where(special, m_re, tops[1])]
            bottoms = [jnp.where(special, p_im, bottoms[0]), jnp.where(special, m_im, bottoms[1])]
            loose = jnp.concatenate([-m_im, m_re], axis=0).astype(BF)
        upper += tops
        lower += bottoms
    values = jnp.concatenate(
        [jnp.concatenate(upper, axis=1), jnp.concatenate(lower, axis=1)], axis=0
    ).astype(BF)

    def back(values, row):
        grid_values = jnp.dot(inverse_ref[...], values, preferred_element_type=F32).astype(BF)
        start = 0
        for ref in out_refs:
            cols = ref.shape[1]
            for r in range(grid_values.shape[1] // width):
                ref[row + r] = grid_values[start : start + cols, r * width : (r + 1) * width]
            start += cols

    back(values, 2 * per_step * step)

    @pl.when(special)
    def _():
        back(loose, last_row)

    @pl.when(jnp.logical_and(step == 0, jnp.logical_not(special)))
    def _():
        for ref in out_refs:
            ref[last_row] = jnp.zeros(ref.shape[1:], BF)


def modes(received, first_pair, lat_keep, lon_keep, forward, inverse, w_in, b_in, w_out, b_out):
    lon_count = len(received[0])
    flat = [values for chunk in received for values in chunk]
    slots, _, width = flat[0].shape
    pairs = slots // 2
    per_step = 2 if pairs % 2 == 0 else 1
    pair_specs = [pl.BlockSpec((2 * per_step, r.shape[1], width), lambda i: (i, 0, 0)) for r in flat]
    spare_specs = [pl.BlockSpec((1, r.shape[1], width), lambda i: (slots - 1, 0, 0)) for r in flat]
    whole = lambda array: pl.BlockSpec(array.shape, lambda i: (0,) * array.ndim)
    out = pl.pallas_call(
        functools.partial(modes_kernel, len(flat)),
        grid=(pairs // per_step,),
        in_specs=[pl.BlockSpec(memory_space=pltpu.SMEM), whole(lat_keep), whole(lon_keep)]
        + pair_specs
        + spare_specs
        + [whole(forward), whole(inverse), whole(w_in), whole(b_in), whole(w_out), whole(b_out)],
        out_specs=[pl.BlockSpec(r.shape, lambda i: (0, 0, 0)) for r in flat],
        out_shape=[jax.ShapeDtypeStruct(r.shape, BF) for r in flat],
        scratch_shapes=[pltpu.VMEM((2 * KEEP_LON, width), F32)],
        compiler_params=pltpu.CompilerParams(vmem_limit_bytes=48 << 20),
        cost_estimate=pl.CostEstimate(
            flops=pairs * 2 * (2 * 2 * KEEP_LON * W * 2 * width + 4 * KEEP_LON * 4 * width * width),
            bytes_accessed=4 * slots * W * width,
            transcendentals=0,
        ),
        name="modes",
    )(
        first_pair, lat_keep, lon_keep, *flat, *flat,
        forward, inverse, w_in, b_in, w_out, b_out,
    )
    return [list(out[i : i + lon_count]) for i in range(0, len(flat), lon_count)]


def mlp_kernel(
    where_ref, own_ref, other_ref, gain_ref, bias_ref, w_in_ref, b_in_ref, w_out_ref, b_out_ref,
    out_ref,
):
    _, rows, cols, width = own_ref.shape
    cells = rows * cols
    own = own_ref[0].reshape(cells, width)
    other = other_ref[0].reshape(cells, width)
    flip = where_ref[1] == 1
    low = jnp.where(flip, other, own)
    high = jnp.where(flip, own, other)
    wide = jnp.concatenate([low, high], axis=1).astype(F32)
    center = jnp.mean(wide, axis=1, keepdims=True)
    off = wide - center
    spread = jnp.mean(off * off, axis=1, keepdims=True)
    normed = (off * lax.rsqrt(spread + norm_epsilon) * gain_ref[...] + bias_ref[...]).astype(BF)
    hidden = jnp.dot(normed, w_in_ref[...], preferred_element_type=F32) + b_in_ref[...]
    hidden = (hidden * (0.5 + 0.5 * lax.erf(hidden * math.sqrt(0.5)))).astype(BF)
    total = jnp.dot(hidden, w_out_ref[...], preferred_element_type=F32) + wide + b_out_ref[...]
    total = total.astype(BF)
    out_ref[0, 0] = total[:, :width].reshape(rows, cols, width)
    out_ref[0, 1] = total[:, width:].reshape(rows, cols, width)


def mlp(where, own, other, gain, bias, w_in, b_in, w_out, b_out):
    lon_count, rows, cols, width = own.shape
    whole = lambda array: pl.BlockSpec(array.shape, lambda i, where: (0,) * array.ndim)
    cell_spec = pl.BlockSpec((1, rows, cols, width), lambda i, where: (i, 0, 0, 0))
    cells = lon_count * rows * cols
    return pl.pallas_call(
        mlp_kernel,
        grid_spec=pltpu.PrefetchScalarGridSpec(
            num_scalar_prefetch=1,
            grid=(lon_count,),
            in_specs=[cell_spec, cell_spec]
            + [whole(a) for a in (gain, bias, w_in, b_in, w_out, b_out)],
            out_specs=pl.BlockSpec((1, 2, rows, cols, width), lambda i, where: (i, 0, 0, 0, 0)),
        ),
        out_shape=jax.ShapeDtypeStruct((lon_count, 2, rows, cols, width), BF),
        compiler_params=pltpu.CompilerParams(vmem_limit_bytes=48 << 20),
        cost_estimate=pl.CostEstimate(
            flops=4 * cells * w_in.size // COST_SHARE,
            bytes_accessed=8 * cells * width // COST_SHARE,
            transcendentals=cells * w_in.shape[1] // COST_SHARE,
        ),
        name="channel_mlp",
    )(where, own, other, gain, bias, w_in, b_in, w_out, b_out)


def assemble_kernel(piece_ref, *refs):
    out_ref = refs[-1]
    half = piece_ref.shape[2]
    for c in range(2):
        out_ref[c * half : (c + 1) * half] = piece_ref[0, c]


def assemble(result, pieces, first_col, block_cols):
    lon_count, _, rows, cols, width = pieces.shape
    block = math.gcd(math.gcd(cols, block_cols), first_col)
    specs = [pl.BlockSpec((1, 2, rows, block, width), lambda z, j: (z, 0, 0, j, 0))]
    operands = [pieces]
    aliases = {}
    if result is not None:
        aliases = {1: 0}
        operands.append(result)
        specs.append(pl.BlockSpec(memory_space=pl.ANY))
    return pl.pallas_call(
        assemble_kernel,
        grid=(lon_count, cols // block),
        in_specs=specs,
        out_specs=pl.BlockSpec(
            (2 * rows, block, width),
            lambda z, j: (0, z * (block_cols // block) + first_col // block + j, 0),
        ),
        out_shape=jax.ShapeDtypeStruct((2 * rows, lon_count * block_cols, width), BF),
        input_output_aliases=aliases,
        cost_estimate=pl.CostEstimate(
            flops=0, bytes_accessed=8 * lon_count * rows * cols * width, transcendentals=0
        ),
        name="assemble",
    )(*operands)


def block_diagonal(weight):
    blocks, n = weight.shape[1], weight.shape[2]
    eye = jnp.eye(blocks, dtype=weight.dtype)
    spread = (weight[:, :, :, None, :] * eye[None, :, None, :, None]).reshape(
        2, blocks * n, blocks * n
    )
    return jnp.concatenate(
        [
            jnp.concatenate([spread[0], spread[1]], axis=1),
            jnp.concatenate([-spread[1], spread[0]], axis=1),
        ],
        axis=0,
    )


def swap(values, axis):
    return lax.ppermute(values, axis, [(0, 1), (1, 0)])


def shift(values, steps, lon_count):
    if steps == 0:
        return values
    return lax.ppermute(values, "lon", [(z, (z + steps) % lon_count) for z in range(lon_count)])


def column_plan(
    widths,
    patches,
    filter_norm_gain,
    filter_norm_bias,
    filter_in,
    filter_in_bias,
    filter_out,
    filter_out_bias,
    kept_lat,
    kept_lon,
    norm_gain,
    norm_bias,
    dense_in,
    dense_in_bias,
    dense_out,
    dense_out_bias,
):
    lon_count = lax.axis_size("lon")
    lat_count = lax.axis_size("lat")
    rows, cols, width = patches.shape
    chunks = len(widths)
    starts = [sum(widths[:i]) for i in range(chunks)]
    block_width = filter_in.shape[2]
    lat_id = lax.axis_index("lat")
    lon_id = lax.axis_index("lon")
    ch_id = lax.axis_index("ch")
    pairs = MLAT // (lat_count * lon_count)
    slots = 2 * pairs + 1

    lat_table = lat_tables(lat_count, lon_count).reshape(lat_count, lon_count, slots, H)
    forward_all, inverse_all = [], []
    for a in range(lat_count):
        here = lat_table[..., a * rows : (a + 1) * rows]
        ordered = np.concatenate([here[1 - a], here[a]], axis=0).reshape(-1, rows)
        forward_all.append(spread8(ordered))
        ordered = np.concatenate([here[a], here[1 - a]], axis=0)
        ordered = np.pad(ordered, ((0, 0), (0, slots % 2), (0, 0))).reshape(-1, rows)
        inverse_all.append(spread8(ordered.T))
    forward_lat = lax.dynamic_index_in_dim(jnp.asarray(np.stack(forward_all)), lat_id, 0, False)
    inverse_lat = None

    ids = np.arange(W).reshape(lon_count, cols)

    def column_order(devices):
        return np.concatenate([ids[devices, c : c + w].reshape(-1) for c, w in zip(starts, widths)])

    steps = np.arange(lon_count)
    from_here = [lon_tables(column_order((z - steps) % lon_count))[0] for z in range(lon_count)]
    to_there = [lon_tables(column_order((z + steps) % lon_count))[1] for z in range(lon_count)]

    fence = lax.optimization_barrier
    where = jnp.stack([lon_id, ch_id]).astype(jnp.int32)

    def row_transform(i, source):
        raw = source[:, starts[i] : starts[i] + widths[i]].astype(F32)
        center = jnp.mean(raw, axis=-1)
        off = raw - center[..., None]
        square = jnp.sum(off * off, axis=-1)
        theirs = swap(jnp.stack([center, square]), "ch")
        mean = 0.5 * (center + theirs[0])
        gap = center - theirs[0]
        spread = (square + theirs[1]) / C + 0.25 * gap * gap
        scale = lax.rsqrt(spread + norm_epsilon)
        prenormed = (
            (raw - mean[..., None]) * scale[..., None] * filter_norm_gain.astype(F32)
            + filter_norm_bias.astype(F32)
        ).astype(BF)
        return lat_forward(where, prenormed, forward_lat, lon_count)

    def mlp_weights(dense_in, dense_in_bias, dense_out, dense_out_bias):
        return (
            norm_gain.astype(F32)[None],
            norm_bias.astype(F32)[None],
            jnp.concatenate([dense_in, swap(dense_in, "ch")], axis=1),
            jnp.concatenate([dense_in_bias, swap(dense_in_bias, "ch")]).astype(F32)[None],
            jnp.concatenate([dense_out, swap(dense_out, "ch")], axis=0),
            lax.all_gather(dense_out_bias, "ch", axis=0, tiled=True).astype(F32)[None],
        )

    def filter_operands():
        return (
            ((lat_id * lon_count + lon_id) * pairs).astype(jnp.int32).reshape(1),
            jnp.tile(jnp.repeat(kept_lat, block_width), 2).reshape(1, -1),
            jnp.tile(jnp.repeat(kept_lon, block_width), 2).reshape(1, -1),
            lax.dynamic_index_in_dim(jnp.asarray(np.stack(from_here)), lon_id, 0, False),
            lax.dynamic_index_in_dim(jnp.asarray(np.stack(to_there)), lon_id, 0, False),
            block_diagonal(filter_in),
            filter_in_bias.reshape(1, -1).astype(F32),
            block_diagonal(filter_out),
            filter_out_bias.reshape(1, -1).astype(F32),
        )

    def along_lon(values):
        return [shift(values[s], s, lon_count) for s in range(lon_count)]

    def row_result(i, own, other):
        mine, sent = lat_inverse(where, own, other, inverse_lat, patches, starts[i])
        return mlp(where, mine, swap(sent, "ch"), *weights)

    def outward(outputs):
        shape = outputs.shape
        flat = outputs.reshape((shape[0] * 2,) + shape[2:])
        return lax.all_to_all(flat, ("lon", "ch"), 0, 0, tiled=True).reshape(shape)

    received, summed, sent, kept = [], None, None, None
    weights = None
    filter_args = None
    dense = (dense_in, dense_in_bias, dense_out, dense_out_bias)
    for step in range(chunks + 2):
        arrived = None
        if sent is not None:
            arrived = (kept, swap(sent, "lat"))
            sent = None
        if summed is not None:
            received.append(along_lon(summed))
            summed = None
        if step < chunks:
            sent, kept = row_transform(step, patches)
        elif step == chunks:
            filter_args = filter_operands()
        if step == 1:
            (tied, tied_lat), _ = fence(((dense, lat_id), kept))
            weights = mlp_weights(*tied)
            inverse_lat = lax.dynamic_index_in_dim(
                jnp.asarray(np.stack(inverse_all)), tied_lat, 0, False
            )
        patches, arrived, sent, kept, received, filter_args, weights, inverse_lat, dense = fence(
            (patches, arrived, sent, kept, received, filter_args, weights, inverse_lat, dense)
        )
        if arrived is not None:
            summed = [
                (arrived[0][s].astype(F32) + arrived[1][s].astype(F32)).astype(BF)
                for s in range(lon_count)
            ]

    filtered = modes(received, *filter_args)

    owns = [None] * chunks
    others = [None] * chunks
    outputs = [None] * chunks
    for step in range(chunks):
        owns[step] = along_lon(filtered[step])
        if step >= 1:
            owns[step - 1] = jnp.stack(owns[step - 1])
            others[step - 1] = swap(owns[step - 1], "lat")
        if step >= 2:
            outputs[step - 2] = row_result(step - 2, owns[step - 2], others[step - 2])
        patches, filtered, owns, others, outputs = fence((patches, filtered, owns, others, outputs))

    result = None
    pieces = None
    for i in range(chunks):
        last = pieces
        pieces = outward(outputs[i])
        if last is not None:
            result = assemble(result, last, starts[i - 1], cols)
        if i + 1 < chunks and outputs[i + 1] is None:
            outputs[i + 1] = row_result(i + 1, owns[i + 1], others[i + 1])
        if i + 2 < chunks and others[i + 2] is None:
            owns[i + 2] = jnp.stack(owns[i + 2])
            others[i + 2] = swap(owns[i + 2], "lat")
        patches, owns, others, outputs, pieces, result = fence(
            (patches, owns, others, outputs, pieces, result)
        )
    result = assemble(result, pieces, starts[chunks - 1], cols)
    return result.reshape(1, 1, rows // lon_count, lon_count * cols, width)


def lon_forward(number, length):
    freq_ids = jnp.arange(number, dtype=jnp.int32)
    cell_ids = jnp.arange(length, dtype=jnp.int32)
    phase_turns = cell_ids[:, None] * freq_ids[None, :] % length
    angles = phase_turns.astype(jnp.float32) * (2.0 * math.pi / length)
    factor = 1.0 / math.sqrt(length)
    return jnp.stack([jnp.cos(angles) * factor, -jnp.sin(angles) * factor], axis=1).astype(
        jnp.bfloat16
    )


def lon_inverse(freq_ids, length):
    cell_ids = jnp.arange(length, dtype=jnp.int32)
    phase_turns = freq_ids[:, None] * cell_ids[None, :] % length
    angles = phase_turns.astype(jnp.float32) * (2.0 * math.pi / length)
    factor = 1.0 / math.sqrt(length)
    weight = jnp.where(freq_ids == 0, 1.0, 2.0).astype(jnp.float32)[:, None]
    return jnp.stack(
        [jnp.cos(angles) * factor * weight, -jnp.sin(angles) * factor * weight]
    ).astype(jnp.bfloat16)


def band_ids(half_band, length):
    slot_ids = jnp.arange(2 * half_band, dtype=jnp.int32)
    return jnp.where(slot_ids < half_band, slot_ids, slot_ids + length - 2 * half_band)


def lat_forward_table(row_ids, half_band, length):
    phase_turns = band_ids(half_band, length)[:, None] * row_ids[None, :] % length
    angles = phase_turns.astype(jnp.float32) * (2.0 * math.pi / length)
    factor = 1.0 / math.sqrt(length)
    cosine = jnp.cos(angles) * factor
    sine_part = jnp.sin(angles) * factor
    upper_half = jnp.concatenate([cosine, sine_part], axis=1)
    bottom = jnp.concatenate([-sine_part, cosine], axis=1)
    return jnp.concatenate([upper_half, bottom], axis=0).astype(jnp.bfloat16)


def lat_inverse_table(row_ids, half_band, length):
    phase_turns = row_ids[:, None] * band_ids(half_band, length)[None, :] % length
    angles = phase_turns.astype(jnp.float32) * (2.0 * math.pi / length)
    factor = 1.0 / math.sqrt(length)
    cosine = jnp.cos(angles) * factor
    sine_part = jnp.sin(angles) * factor
    upper_half = jnp.concatenate([cosine, -sine_part], axis=1)
    bottom = jnp.concatenate([sine_part, cosine], axis=1)
    return jnp.concatenate([upper_half, bottom], axis=0).astype(jnp.bfloat16)


def complex_layer(values, weight, offset):
    products = jnp.einsum("tjkbc,ubcd->tujkbd", values, weight, preferred_element_type=jnp.float32)
    offset = offset.astype(jnp.float32)
    real_part = products[0, 0] - products[1, 1] + offset[0]
    imag_part = products[1, 0] + products[0, 1] + offset[1]
    return jnp.stack([real_part, imag_part])


def channel_mlp(mixed_full, norm_gain, norm_bias, weight_in, bias_in, weight_out):
    wide = mixed_full.astype(jnp.float32)
    center = jnp.mean(wide, axis=-1, keepdims=True)
    spread = jnp.mean((wide - center) ** 2, axis=-1, keepdims=True)
    normed = (
        (wide - center) * lax.rsqrt(spread + norm_epsilon) * norm_gain.astype(jnp.float32)
        + norm_bias.astype(jnp.float32)
    ).astype(jnp.bfloat16)
    hidden = jnp.einsum("rwc,cu->rwu", normed, weight_in, preferred_element_type=jnp.float32)
    hidden = jax.nn.gelu(hidden + bias_in.astype(jnp.float32), approximate=False).astype(
        jnp.bfloat16
    )
    return jnp.einsum("rwu,uc->rwc", hidden, weight_out, preferred_element_type=jnp.float32)


def row_plan(
    patches,
    filter_norm_gain,
    filter_norm_bias,
    filter_in,
    filter_in_bias,
    filter_out,
    filter_out_bias,
    kept_lat,
    kept_lon,
    norm_gain,
    norm_bias,
    dense_in,
    dense_in_bias,
    dense_out,
    dense_out_bias,
):
    lon_count = lax.axis_size("lon")
    lat_count = lax.axis_size("lat")
    band_rows = patches.shape[0] // lon_count
    local_channels = patches.shape[2]
    local_blocks = filter_in.shape[1]
    block_width = filter_in.shape[2]
    row_span = lon_count * band_rows
    local_freqs = KEEP_LON // (lon_count * lat_count)
    local_rows = lax.all_to_all(patches, "lon", split_axis=0, concat_axis=1, tiled=True)
    raw = local_rows.astype(jnp.float32)
    cell_total = lax.psum(jnp.sum(raw, axis=-1, keepdims=True), "ch")
    pre_center = cell_total / C
    centered = raw - pre_center
    square_total = lax.psum(jnp.sum(centered * centered, axis=-1, keepdims=True), "ch")
    pre_spread = square_total / C
    prenormed = (
        centered * lax.rsqrt(pre_spread + norm_epsilon) * filter_norm_gain.astype(jnp.float32)
        + filter_norm_bias.astype(jnp.float32)
    ).astype(jnp.bfloat16)
    spectrum = jnp.einsum(
        "rwc,wtk->trkc", prenormed, lon_forward(KEEP_LON, W), preferred_element_type=jnp.float32
    )
    spectrum = spectrum.astype(jnp.bfloat16)
    slot_ids = jnp.arange(H, dtype=jnp.int32)
    group_ids = slot_ids // band_rows
    direct_rows = (
        group_ids % lat_count * row_span + group_ids // lat_count * band_rows + slot_ids % band_rows
    )
    pencil = lax.all_to_all(spectrum, ("lon", "lat"), split_axis=2, concat_axis=1, tiled=True)
    banded = jnp.dot(
        lat_forward_table(direct_rows, MLAT, H),
        pencil.reshape(2 * H, -1),
        preferred_element_type=jnp.float32,
    )
    banded = banded.astype(jnp.bfloat16).reshape(
        2, 2 * MLAT, local_freqs, local_blocks, block_width
    )
    first = complex_layer(banded, filter_in, filter_in_bias.reshape(2, local_blocks, block_width))
    first = jnp.maximum(first, 0.0).astype(jnp.bfloat16)
    second = complex_layer(first, filter_out, filter_out_bias.reshape(2, local_blocks, block_width))
    shrunk = jnp.sign(second) * jnp.maximum(jnp.abs(second) - shrink_level, 0.0)
    column_ids = (
        lax.axis_index("lon") * lat_count + lax.axis_index("lat")
    ) * local_freqs + jnp.arange(local_freqs, dtype=jnp.int32)
    band_slots = jnp.arange(2 * MLAT, dtype=jnp.int32)
    signed_band = jnp.where(band_slots < MLAT, band_slots, band_slots - 2 * MLAT)
    lat_ok = (signed_band[:, None] >= -kept_lat[None, :]) & (
        signed_band[:, None] < kept_lat[None, :]
    )
    lon_ok = column_ids[:, None] < kept_lon[None, :]
    keep_mask = (lat_ok[:, None, :] & lon_ok[None, :, :]).astype(jnp.float32)[..., None]
    kept_modes = (shrunk * keep_mask).astype(jnp.bfloat16).reshape(4 * MLAT, -1)
    spatial = jnp.dot(
        lat_inverse_table(direct_rows, MLAT, H), kept_modes, preferred_element_type=jnp.float32
    )
    spatial = spatial.astype(jnp.bfloat16).reshape(2, H, local_freqs, local_channels)
    returned = lax.all_to_all(spatial, ("lon", "lat"), split_axis=1, concat_axis=2, tiled=True)
    back_freqs = jnp.arange(KEEP_LON, dtype=jnp.int32)
    fine_part = jnp.einsum(
        "trkc,tkw->rwc", returned, lon_inverse(back_freqs, W), preferred_element_type=jnp.float32
    )
    mixed = (raw + fine_part).astype(jnp.bfloat16)
    gathered = lax.all_gather(mixed, "ch", axis=2, tiled=True)
    partial_terms = channel_mlp(gathered, norm_gain, norm_bias, dense_in, dense_in_bias, dense_out)
    summed = lax.psum_scatter(
        partial_terms.astype(jnp.bfloat16), "ch", scatter_dimension=2, tiled=True
    ).astype(jnp.float32)
    result = (mixed.astype(jnp.float32) + summed + dense_out_bias.astype(jnp.float32)).astype(
        jnp.bfloat16
    )
    return result.reshape(1, 1, band_rows, W, local_channels)


def solution(mesh):
    placed = (
        P(("grp", "lat"), "lon", "ch"),
        P("ch"),
        P("ch"),
        P(None, "ch", None, None),
        P(None, "ch"),
        P(None, "ch", None, None),
        P(None, "ch"),
        P("ch"),
        P("ch"),
        P(),
        P(),
        P(None, "ch"),
        P("ch"),
        P("ch", None),
        P("ch"),
    )
    sizes = mesh.shape
    lat_count, lon_count = sizes["lat"], sizes["lon"]
    cols = W // lon_count
    fits = lat_count == 2 and sizes["ch"] == 2 and MLAT % (lat_count * lon_count) == 0
    fits = fits and cols == 96 and H % (2 * lat_count * lon_count) == 0
    plan = functools.partial(column_plan, (32, 32, 32)) if fits else row_plan
    return jax.shard_map(
        plan,
        mesh=mesh,
        in_specs=placed,
        out_specs=P(("grp", "lat"), "lon", None, None, "ch"),
        check_vma=False,
    )
```

```python
import functools
import math

import jax
import jax.numpy as jnp
import numpy as np
from jax import lax
from jax.experimental import pallas as pl
from jax.experimental.pallas import tpu as pltpu
from jax.sharding import PartitionSpec as P

H = 256
W = 384
C = 768
MLAT = 64
KEEP_LON = 128

shrink_level = 0.01
norm_epsilon = 1e-05

COST_SHARE = 1

BF = jnp.bfloat16
F32 = jnp.float32


def angle_table(rows, cols, length):
    phase = rows[:, None] * cols[None, :] % length
    return phase * (2.0 * math.pi / length)


def lat_slots(lat_count, lon_count):
    per = MLAT // (lat_count * lon_count)
    freq, kind = [], []
    for dev in range(lat_count * lon_count):
        for pair in range(dev * per, dev * per + per):
            freq += [0, MLAT] if pair == 0 else [pair, pair]
            kind += [0, 0] if pair == 0 else [0, 1]
        freq.append(MLAT if dev == 0 else 0)
        kind.append(1 if dev == 0 else 2)
    return np.array(freq), np.array(kind)


def lat_tables(lat_count, lon_count):
    freq, kind = lat_slots(lat_count, lon_count)
    angles = angle_table(freq, np.arange(H), H)
    table = np.where(kind[:, None] == 0, np.cos(angles), -np.sin(angles)) / math.sqrt(H)
    table = np.where(kind[:, None] == 2, 0.0, table)
    return table.astype(np.float32)


def lon_tables(order):
    freqs = np.arange(KEEP_LON)
    angles = angle_table(freqs, order, W)
    factor = 1.0 / math.sqrt(W)
    weight = np.where(freqs == 0, 1.0, 2.0)[:, None]
    forward = np.concatenate([np.cos(angles) * factor, -np.sin(angles) * factor], axis=0)
    inverse = np.concatenate(
        [np.cos(angles) * factor * weight, -np.sin(angles) * factor * weight], axis=0
    ).T
    return forward.astype(np.float32).astype(jnp.bfloat16), inverse.astype(np.float32).astype(jnp.bfloat16)


def spread8(table):
    return np.kron(table, np.eye(8, dtype=np.float32)).astype(jnp.bfloat16)


def lat_forward_kernel(where_ref, cells_ref, table_ref, send_ref, keep_ref):
    rows, _, width = cells_ref.shape
    lon_count, slots, _, _ = send_ref.shape
    values = cells_ref[...].astype(F32).reshape(rows, 2, 8, width)
    pair = jnp.concatenate(
        [values[:, 0].reshape(rows * 8, width), values[:, 1].reshape(rows * 8, width)], axis=1
    ).astype(BF)
    half = table_ref.shape[0] // 2
    for part, out_ref in ((0, send_ref), (1, keep_ref)):
        total = jnp.dot(
            table_ref[part * half : (part + 1) * half, :], pair, preferred_element_type=F32
        )
        total = jnp.concatenate(
            [
                total[:, :width].reshape(lon_count, slots, 8, width),
                total[:, width:].reshape(lon_count, slots, 8, width),
            ],
            axis=2,
        ).astype(BF)
        for z in range(lon_count):
            out_ref[lax.rem(z + lon_count - where_ref[0], lon_count)] = total[z]


def lat_forward(where, cells, table, lon_count):
    rows, cols, width = cells.shape
    slots = table.shape[0] // (16 * lon_count)
    block = pl.BlockSpec((lon_count, slots, 16, width), lambda i: (0, 0, i, 0))
    return pl.pallas_call(
        lat_forward_kernel,
        grid=(cols // 16,),
        in_specs=[
            pl.BlockSpec(memory_space=pltpu.SMEM),
            pl.BlockSpec((rows, 16, width), lambda i: (0, i, 0)),
            pl.BlockSpec(table.shape, lambda i: (0, 0)),
        ],
        out_specs=[block, block],
        out_shape=[jax.ShapeDtypeStruct((lon_count, slots, cols, width), BF)] * 2,
        compiler_params=pltpu.CompilerParams(vmem_limit_bytes=40 << 20),
        cost_estimate=pl.CostEstimate(
            flops=2 * table.size * cols // 8 * width // COST_SHARE,
            bytes_accessed=4 * rows * cols * width // COST_SHARE,
            transcendentals=0,
        ),
        name="lat_forward",
    )(where, cells, table)


def lat_inverse_kernel(
    where_ref, own_ref, other_ref, table_ref, patches_ref, mine_ref, sent_ref, flat_ref
):
    rows, _, width = patches_ref.shape
    lon_count, slots = own_ref.shape[:2]
    blank = jnp.zeros((flat_ref.shape[1] - slots * 8, 2 * width), BF)
    for side, ref in enumerate((own_ref, other_ref)):
        for s in range(lon_count):
            values = ref[s].astype(F32).reshape(slots, 2, 8, width)
            flat = jnp.concatenate(
                [values[:, 0].reshape(slots * 8, width), values[:, 1].reshape(slots * 8, width)],
                axis=1,
            )
            source = lax.rem(where_ref[0] + (lon_count - s), lon_count)
            flat_ref[side * lon_count + source] = jnp.concatenate([flat.astype(BF), blank], axis=0)
    total = jnp.dot(
        table_ref[...], flat_ref[...].reshape(-1, 2 * width), preferred_element_type=F32
    )
    fine = jnp.concatenate(
        [total[:, :width].reshape(rows, 8, width), total[:, width:].reshape(rows, 8, width)], axis=1
    )
    mixed = (patches_ref[...].astype(F32) + fine).astype(BF)
    mixed = mixed.reshape(lon_count, 2, rows // (2 * lon_count), 16, width)

    @pl.when(where_ref[1] == 0)
    def _():
        mine_ref[...] = mixed[:, 0]
        sent_ref[...] = mixed[:, 1]

    @pl.when(where_ref[1] != 0)
    def _():
        mine_ref[...] = mixed[:, 1]
        sent_ref[...] = mixed[:, 0]


def lat_inverse(where, own, other, table, patches, first_col):
    lon_count, slots, cols, width = own.shape
    rows = patches.shape[0]
    first_block = first_col // 16
    spec = pl.BlockSpec((lon_count, slots, 16, width), lambda i: (0, 0, i, 0))
    half = rows // (2 * lon_count)
    out_spec = pl.BlockSpec((lon_count, half, 16, width), lambda i: (0, 0, i, 0))
    return pl.pallas_call(
        lat_inverse_kernel,
        grid=(cols // 16,),
        in_specs=[
            pl.BlockSpec(memory_space=pltpu.SMEM),
            spec,
            spec,
            pl.BlockSpec(table.shape, lambda i: (0, 0)),
            pl.BlockSpec((rows, 16, width), lambda i: (0, first_block + i, 0)),
        ],
        out_specs=[out_spec, out_spec],
        out_shape=[jax.ShapeDtypeStruct((lon_count, half, cols, width), BF)] * 2,
        scratch_shapes=[
            pltpu.VMEM((2 * lon_count, table.shape[1] // (2 * lon_count), 2 * width), BF)
        ],
        compiler_params=pltpu.CompilerParams(vmem_limit_bytes=40 << 20),
        cost_estimate=pl.CostEstimate(
            flops=2 * table.size * cols // 8 * width // COST_SHARE,
            bytes_accessed=6 * rows * cols * width // COST_SHARE,
            transcendentals=0,
        ),
        name="lat_inverse",
    )(where, own, other, table, patches)


def modes_kernel(inputs, first_pair_ref, lat_keep_ref, lon_keep_ref, *refs):
    pair_refs = refs[:inputs]
    spare_refs = refs[inputs : 2 * inputs]
    forward_ref, inverse_ref, w_in_ref, b_in_ref, w_out_ref, b_out_ref = refs[
        2 * inputs : 2 * inputs + 6
    ]
    out_refs, spare_ref = refs[2 * inputs + 6 : -1], refs[-1]
    width = pair_refs[0].shape[-1]
    per_step = pair_refs[0].shape[0] // 2
    step = pl.program_id(0)
    last_row = 2 * per_step * pl.num_programs(0)
    pair_id = first_pair_ref[0] + step * per_step
    special = pair_id == 0
    keep = KEEP_LON

    def columns(refs, row):
        return jnp.concatenate([ref[row] for ref in refs], axis=0)

    @pl.when(special)
    def _():
        spare_ref[...] = jnp.dot(
            forward_ref[...], columns(spare_refs, 0), preferred_element_type=F32
        )

    both = jnp.concatenate([columns(pair_refs, r) for r in range(2 * per_step)], axis=1)
    spectrum = jnp.dot(forward_ref[...], both, preferred_element_type=F32)
    banded = []
    for q in range(per_step):
        a = spectrum[:, 2 * q * width : (2 * q + 1) * width]
        b = spectrum[:, (2 * q + 1) * width : (2 * q + 2) * width]
        a_re, a_im, b_re, b_im = a[:keep], a[keep:], b[:keep], b[keep:]
        plus = [a_re - b_im, a_im + b_re]
        minus = [a_re + b_im, a_im - b_re]
        if q == 0:
            plus = [jnp.where(special, a_re, plus[0]), jnp.where(special, a_im, plus[1])]
            minus = [
                jnp.where(special, b_re + spare_ref[keep:], minus[0]),
                jnp.where(special, b_im - spare_ref[:keep], minus[1]),
            ]
        banded += [jnp.concatenate(plus, axis=1), jnp.concatenate(minus, axis=1)]
    banded = jnp.concatenate(banded, axis=0).astype(BF)
    first = jnp.dot(banded, w_in_ref[...], preferred_element_type=F32) + b_in_ref[...]
    first = jnp.maximum(first, 0.0).astype(BF)
    second = jnp.dot(first, w_out_ref[...], preferred_element_type=F32) + b_out_ref[...]
    shrunk = second - jnp.clip(second, -shrink_level, shrink_level)
    freq = lax.broadcasted_iota(jnp.int32, (keep, 2 * width), 0)
    lon_ok = freq < lon_keep_ref[...]
    upper, lower = [], []
    for q in range(per_step):
        plus_ok = lon_ok & (pair_id + q < lat_keep_ref[...])
        minus_id = jnp.where(special, MLAT, pair_id) if q == 0 else pair_id + q
        minus_ok = lon_ok & (minus_id <= lat_keep_ref[...])
        plus = jnp.where(plus_ok, shrunk[2 * q * keep : (2 * q + 1) * keep], 0.0)
        minus = jnp.where(minus_ok, shrunk[(2 * q + 1) * keep : (2 * q + 2) * keep], 0.0)
        p_re, p_im, m_re, m_im = plus[:, :width], plus[:, width:], minus[:, :width], minus[:, width:]
        tops = [p_re + m_re, p_im - m_im]
        bottoms = [p_im + m_im, m_re - p_re]
        if q == 0:
            tops = [jnp.where(special, p_re, tops[0]), jnp.where(special, m_re, tops[1])]
            bottoms = [jnp.where(special, p_im, bottoms[0]), jnp.where(special, m_im, bottoms[1])]
            loose = jnp.concatenate([-m_im, m_re], axis=0).astype(BF)
        upper += tops
        lower += bottoms
    values = jnp.concatenate(
        [jnp.concatenate(upper, axis=1), jnp.concatenate(lower, axis=1)], axis=0
    ).astype(BF)

    def back(values, row):
        grid_values = jnp.dot(inverse_ref[...], values, preferred_element_type=F32).astype(BF)
        start = 0
        for ref in out_refs:
            cols = ref.shape[1]
            for r in range(grid_values.shape[1] // width):
                ref[row + r] = grid_values[start : start + cols, r * width : (r + 1) * width]
            start += cols

    back(values, 2 * per_step * step)

    @pl.when(special)
    def _():
        back(loose, last_row)

    @pl.when(jnp.logical_and(step == 0, jnp.logical_not(special)))
    def _():
        for ref in out_refs:
            ref[last_row] = jnp.zeros(ref.shape[1:], BF)


def modes(received, first_pair, lat_keep, lon_keep, forward, inverse, w_in, b_in, w_out, b_out):
    lon_count = len(received[0])
    flat = [values for chunk in received for values in chunk]
    slots, _, width = flat[0].shape
    pairs = slots // 2
    per_step = 2 if pairs % 2 == 0 else 1
    pair_specs = [pl.BlockSpec((2 * per_step, r.shape[1], width), lambda i: (i, 0, 0)) for r in flat]
    spare_specs = [pl.BlockSpec((1, r.shape[1], width), lambda i: (slots - 1, 0, 0)) for r in flat]
    whole = lambda array: pl.BlockSpec(array.shape, lambda i: (0,) * array.ndim)
    out = pl.pallas_call(
        functools.partial(modes_kernel, len(flat)),
        grid=(pairs // per_step,),
        in_specs=[pl.BlockSpec(memory_space=pltpu.SMEM), whole(lat_keep), whole(lon_keep)]
        + pair_specs
        + spare_specs
        + [whole(forward), whole(inverse), whole(w_in), whole(b_in), whole(w_out), whole(b_out)],
        out_specs=[pl.BlockSpec(r.shape, lambda i: (0, 0, 0)) for r in flat],
        out_shape=[jax.ShapeDtypeStruct(r.shape, BF) for r in flat],
        scratch_shapes=[pltpu.VMEM((2 * KEEP_LON, width), F32)],
        compiler_params=pltpu.CompilerParams(vmem_limit_bytes=48 << 20),
        cost_estimate=pl.CostEstimate(
            flops=pairs * 2 * (2 * 2 * KEEP_LON * W * 2 * width + 4 * KEEP_LON * 4 * width * width),
            bytes_accessed=4 * slots * W * width,
            transcendentals=0,
        ),
        name="modes",
    )(
        first_pair, lat_keep, lon_keep, *flat, *flat,
        forward, inverse, w_in, b_in, w_out, b_out,
    )
    return [list(out[i : i + lon_count]) for i in range(0, len(flat), lon_count)]


def mlp_kernel(
    where_ref, own_ref, other_ref, gain_ref, bias_ref, w_in_ref, b_in_ref, w_out_ref, b_out_ref,
    out_ref,
):
    _, rows, cols, width = own_ref.shape
    cells = rows * cols
    own = own_ref[0].reshape(cells, width)
    other = other_ref[0].reshape(cells, width)
    flip = where_ref[1] == 1
    low = jnp.where(flip, other, own)
    high = jnp.where(flip, own, other)
    wide = jnp.concatenate([low, high], axis=1).astype(F32)
    center = jnp.mean(wide, axis=1, keepdims=True)
    off = wide - center
    spread = jnp.mean(off * off, axis=1, keepdims=True)
    normed = (off * lax.rsqrt(spread + norm_epsilon) * gain_ref[...] + bias_ref[...]).astype(BF)
    hidden = jnp.dot(normed, w_in_ref[...], preferred_element_type=F32) + b_in_ref[...]
    hidden = (hidden * (0.5 + 0.5 * lax.erf(hidden * math.sqrt(0.5)))).astype(BF)
    total = jnp.dot(hidden, w_out_ref[...], preferred_element_type=F32) + wide + b_out_ref[...]
    total = total.astype(BF)
    out_ref[0, 0] = total[:, :width].reshape(rows, cols, width)
    out_ref[0, 1] = total[:, width:].reshape(rows, cols, width)


def mlp(where, own, other, gain, bias, w_in, b_in, w_out, b_out):
    lon_count, rows, cols, width = own.shape
    whole = lambda array: pl.BlockSpec(array.shape, lambda i, where: (0,) * array.ndim)
    cell_spec = pl.BlockSpec((1, rows, cols, width), lambda i, where: (i, 0, 0, 0))
    cells = lon_count * rows * cols
    return pl.pallas_call(
        mlp_kernel,
        grid_spec=pltpu.PrefetchScalarGridSpec(
            num_scalar_prefetch=1,
            grid=(lon_count,),
            in_specs=[cell_spec, cell_spec]
            + [whole(a) for a in (gain, bias, w_in, b_in, w_out, b_out)],
            out_specs=pl.BlockSpec((1, 2, rows, cols, width), lambda i, where: (i, 0, 0, 0, 0)),
        ),
        out_shape=jax.ShapeDtypeStruct((lon_count, 2, rows, cols, width), BF),
        compiler_params=pltpu.CompilerParams(vmem_limit_bytes=48 << 20),
        cost_estimate=pl.CostEstimate(
            flops=4 * cells * w_in.size // COST_SHARE,
            bytes_accessed=8 * cells * width // COST_SHARE,
            transcendentals=cells * w_in.shape[1] // COST_SHARE,
        ),
        name="channel_mlp",
    )(where, own, other, gain, bias, w_in, b_in, w_out, b_out)


def assemble_kernel(piece_ref, *refs):
    out_ref = refs[-1]
    half = piece_ref.shape[2]
    for c in range(2):
        out_ref[c * half : (c + 1) * half] = piece_ref[0, c]


def assemble(result, pieces, first_col, block_cols):
    lon_count, _, rows, cols, width = pieces.shape
    block = math.gcd(math.gcd(cols, block_cols), first_col)
    specs = [pl.BlockSpec((1, 2, rows, block, width), lambda z, j: (z, 0, 0, j, 0))]
    operands = [pieces]
    aliases = {}
    if result is not None:
        aliases = {1: 0}
        operands.append(result)
        specs.append(pl.BlockSpec(memory_space=pl.ANY))
    return pl.pallas_call(
        assemble_kernel,
        grid=(lon_count, cols // block),
        in_specs=specs,
        out_specs=pl.BlockSpec(
            (2 * rows, block, width),
            lambda z, j: (0, z * (block_cols // block) + first_col // block + j, 0),
        ),
        out_shape=jax.ShapeDtypeStruct((2 * rows, lon_count * block_cols, width), BF),
        input_output_aliases=aliases,
        cost_estimate=pl.CostEstimate(
            flops=0, bytes_accessed=8 * lon_count * rows * cols * width, transcendentals=0
        ),
        name="assemble",
    )(*operands)


def block_diagonal(weight):
    blocks, n = weight.shape[1], weight.shape[2]
    eye = jnp.eye(blocks, dtype=weight.dtype)
    spread = (weight[:, :, :, None, :] * eye[None, :, None, :, None]).reshape(
        2, blocks * n, blocks * n
    )
    return jnp.concatenate(
        [
            jnp.concatenate([spread[0], spread[1]], axis=1),
            jnp.concatenate([-spread[1], spread[0]], axis=1),
        ],
        axis=0,
    )


def swap(values, axis):
    return lax.ppermute(values, axis, [(0, 1), (1, 0)])


def shift(values, steps, lon_count):
    if steps == 0:
        return values
    return lax.ppermute(values, "lon", [(z, (z + steps) % lon_count) for z in range(lon_count)])


def column_plan(
    widths,
    patches,
    filter_norm_gain,
    filter_norm_bias,
    filter_in,
    filter_in_bias,
    filter_out,
    filter_out_bias,
    kept_lat,
    kept_lon,
    norm_gain,
    norm_bias,
    dense_in,
    dense_in_bias,
    dense_out,
    dense_out_bias,
):
    lon_count = lax.axis_size("lon")
    lat_count = lax.axis_size("lat")
    rows, cols, width = patches.shape
    chunks = len(widths)
    starts = [sum(widths[:i]) for i in range(chunks)]
    block_width = filter_in.shape[2]
    lat_id = lax.axis_index("lat")
    lon_id = lax.axis_index("lon")
    ch_id = lax.axis_index("ch")
    pairs = MLAT // (lat_count * lon_count)
    slots = 2 * pairs + 1

    lat_table = lat_tables(lat_count, lon_count).reshape(lat_count, lon_count, slots, H)
    forward_all, inverse_all = [], []
    for a in range(lat_count):
        here = lat_table[..., a * rows : (a + 1) * rows]
        ordered = np.concatenate([here[1 - a], here[a]], axis=0).reshape(-1, rows)
        forward_all.append(spread8(ordered))
        ordered = np.concatenate([here[a], here[1 - a]], axis=0)
        ordered = np.pad(ordered, ((0, 0), (0, slots % 2), (0, 0))).reshape(-1, rows)
        inverse_all.append(spread8(ordered.T))
    forward_lat = lax.dynamic_index_in_dim(jnp.asarray(np.stack(forward_all)), lat_id, 0, False)
    inverse_lat = None

    ids = np.arange(W).reshape(lon_count, cols)

    def column_order(devices):
        return np.concatenate([ids[devices, c : c + w].reshape(-1) for c, w in zip(starts, widths)])

    steps = np.arange(lon_count)
    from_here = [lon_tables(column_order((z - steps) % lon_count))[0] for z in range(lon_count)]
    to_there = [lon_tables(column_order((z + steps) % lon_count))[1] for z in range(lon_count)]

    fence = lax.optimization_barrier
    where = jnp.stack([lon_id, ch_id]).astype(jnp.int32)

    def row_transform(i, source):
        raw = source[:, starts[i] : starts[i] + widths[i]].astype(F32)
        center = jnp.mean(raw, axis=-1)
        off = raw - center[..., None]
        square = jnp.sum(off * off, axis=-1)
        theirs = swap(jnp.stack([center, square]), "ch")
        mean = 0.5 * (center + theirs[0])
        gap = center - theirs[0]
        spread = (square + theirs[1]) / C + 0.25 * gap * gap
        scale = lax.rsqrt(spread + norm_epsilon)
        prenormed = (
            (raw - mean[..., None]) * scale[..., None] * filter_norm_gain.astype(F32)
            + filter_norm_bias.astype(F32)
        ).astype(BF)
        return lat_forward(where, prenormed, forward_lat, lon_count)

    def mlp_weights(dense_in, dense_in_bias, dense_out, dense_out_bias):
        return (
            norm_gain.astype(F32)[None],
            norm_bias.astype(F32)[None],
            jnp.concatenate([dense_in, swap(dense_in, "ch")], axis=1),
            jnp.concatenate([dense_in_bias, swap(dense_in_bias, "ch")]).astype(F32)[None],
            jnp.concatenate([dense_out, swap(dense_out, "ch")], axis=0),
            lax.all_gather(dense_out_bias, "ch", axis=0, tiled=True).astype(F32)[None],
        )

    def filter_operands():
        return (
            ((lat_id * lon_count + lon_id) * pairs).astype(jnp.int32).reshape(1),
            jnp.tile(jnp.repeat(kept_lat, block_width), 2).reshape(1, -1),
            jnp.tile(jnp.repeat(kept_lon, block_width), 2).reshape(1, -1),
            lax.dynamic_index_in_dim(jnp.asarray(np.stack(from_here)), lon_id, 0, False),
            lax.dynamic_index_in_dim(jnp.asarray(np.stack(to_there)), lon_id, 0, False),
            block_diagonal(filter_in),
            filter_in_bias.reshape(1, -1).astype(F32),
            block_diagonal(filter_out),
            filter_out_bias.reshape(1, -1).astype(F32),
        )

    def along_lon(values):
        return [shift(values[s], s, lon_count) for s in range(lon_count)]

    def row_result(i, own, other):
        mine, sent = lat_inverse(where, own, other, inverse_lat, patches, starts[i])
        return mlp(where, mine, swap(sent, "ch"), *weights)

    def outward(outputs):
        shape = outputs.shape
        flat = outputs.reshape((shape[0] * 2,) + shape[2:])
        return lax.all_to_all(flat, ("lon", "ch"), 0, 0, tiled=True).reshape(shape)

    received, summed, sent, kept = [], None, None, None
    weights = None
    filter_args = None
    ahead = None
    dense = (dense_in, dense_in_bias, dense_out, dense_out_bias)
    for step in range(chunks + 2):
        arrived = None
        if sent is not None:
            arrived = (kept, swap(sent, "lat"))
            sent = None
        if summed is not None:
            received.append(along_lon(summed))
            summed = None
        if ahead is not None:
            (sent, kept), ahead = ahead, None
        elif step < chunks:
            sent, kept = row_transform(step, patches)
        if step == chunks:
            filter_args = filter_operands()
        if step == 1 and chunks > 2:
            ahead = row_transform(2, fence((patches, kept))[0])
        if step > chunks:
            weights = mlp_weights(*dense)
            inverse_lat = lax.dynamic_index_in_dim(jnp.asarray(np.stack(inverse_all)), lat_id, 0, False)
        patches, arrived, sent, kept, received, filter_args, weights, inverse_lat, ahead, dense = fence(
            (patches, arrived, sent, kept, received, filter_args, weights, inverse_lat, ahead, dense)
        )
        if arrived is not None:
            summed = [
                (arrived[0][s].astype(F32) + arrived[1][s].astype(F32)).astype(BF)
                for s in range(lon_count)
            ]

    filtered = modes(received, *filter_args)

    owns = [None] * chunks
    others = [None] * chunks
    outputs = [None] * chunks
    for step in range(chunks):
        owns[step] = along_lon(filtered[step])
        if step >= 1:
            owns[step - 1] = jnp.stack(owns[step - 1])
            others[step - 1] = swap(owns[step - 1], "lat")
        if step >= 2:
            outputs[step - 2] = row_result(step - 2, owns[step - 2], others[step - 2])
        patches, filtered, owns, others, outputs = fence((patches, filtered, owns, others, outputs))

    result = None
    pieces = None
    for i in range(chunks):
        last = pieces
        pieces = outward(outputs[i])
        if last is not None:
            result = assemble(result, last, starts[i - 1], cols)
        if i + 1 < chunks and outputs[i + 1] is None:
            outputs[i + 1] = row_result(i + 1, owns[i + 1], others[i + 1])
        if i + 2 < chunks and others[i + 2] is None:
            owns[i + 2] = jnp.stack(owns[i + 2])
            others[i + 2] = swap(owns[i + 2], "lat")
        patches, owns, others, outputs, pieces, result = fence(
            (patches, owns, others, outputs, pieces, result)
        )
    result = assemble(result, pieces, starts[chunks - 1], cols)
    return result.reshape(1, 1, rows // lon_count, lon_count * cols, width)


def lon_forward(number, length):
    freq_ids = jnp.arange(number, dtype=jnp.int32)
    cell_ids = jnp.arange(length, dtype=jnp.int32)
    phase_turns = cell_ids[:, None] * freq_ids[None, :] % length
    angles = phase_turns.astype(jnp.float32) * (2.0 * math.pi / length)
    factor = 1.0 / math.sqrt(length)
    return jnp.stack([jnp.cos(angles) * factor, -jnp.sin(angles) * factor], axis=1).astype(
        jnp.bfloat16
    )


def lon_inverse(freq_ids, length):
    cell_ids = jnp.arange(length, dtype=jnp.int32)
    phase_turns = freq_ids[:, None] * cell_ids[None, :] % length
    angles = phase_turns.astype(jnp.float32) * (2.0 * math.pi / length)
    factor = 1.0 / math.sqrt(length)
    weight = jnp.where(freq_ids == 0, 1.0, 2.0).astype(jnp.float32)[:, None]
    return jnp.stack(
        [jnp.cos(angles) * factor * weight, -jnp.sin(angles) * factor * weight]
    ).astype(jnp.bfloat16)


def band_ids(half_band, length):
    slot_ids = jnp.arange(2 * half_band, dtype=jnp.int32)
    return jnp.where(slot_ids < half_band, slot_ids, slot_ids + length - 2 * half_band)


def lat_forward_table(row_ids, half_band, length):
    phase_turns = band_ids(half_band, length)[:, None] * row_ids[None, :] % length
    angles = phase_turns.astype(jnp.float32) * (2.0 * math.pi / length)
    factor = 1.0 / math.sqrt(length)
    cosine = jnp.cos(angles) * factor
    sine_part = jnp.sin(angles) * factor
    upper_half = jnp.concatenate([cosine, sine_part], axis=1)
    bottom = jnp.concatenate([-sine_part, cosine], axis=1)
    return jnp.concatenate([upper_half, bottom], axis=0).astype(jnp.bfloat16)


def lat_inverse_table(row_ids, half_band, length):
    phase_turns = row_ids[:, None] * band_ids(half_band, length)[None, :] % length
    angles = phase_turns.astype(jnp.float32) * (2.0 * math.pi / length)
    factor = 1.0 / math.sqrt(length)
    cosine = jnp.cos(angles) * factor
    sine_part = jnp.sin(angles) * factor
    upper_half = jnp.concatenate([cosine, -sine_part], axis=1)
    bottom = jnp.concatenate([sine_part, cosine], axis=1)
    return jnp.concatenate([upper_half, bottom], axis=0).astype(jnp.bfloat16)


def complex_layer(values, weight, offset):
    products = jnp.einsum("tjkbc,ubcd->tujkbd", values, weight, preferred_element_type=jnp.float32)
    offset = offset.astype(jnp.float32)
    real_part = products[0, 0] - products[1, 1] + offset[0]
    imag_part = products[1, 0] + products[0, 1] + offset[1]
    return jnp.stack([real_part, imag_part])


def channel_mlp(mixed_full, norm_gain, norm_bias, weight_in, bias_in, weight_out):
    wide = mixed_full.astype(jnp.float32)
    center = jnp.mean(wide, axis=-1, keepdims=True)
    spread = jnp.mean((wide - center) ** 2, axis=-1, keepdims=True)
    normed = (
        (wide - center) * lax.rsqrt(spread + norm_epsilon) * norm_gain.astype(jnp.float32)
        + norm_bias.astype(jnp.float32)
    ).astype(jnp.bfloat16)
    hidden = jnp.einsum("rwc,cu->rwu", normed, weight_in, preferred_element_type=jnp.float32)
    hidden = jax.nn.gelu(hidden + bias_in.astype(jnp.float32), approximate=False).astype(
        jnp.bfloat16
    )
    return jnp.einsum("rwu,uc->rwc", hidden, weight_out, preferred_element_type=jnp.float32)


def row_plan(
    patches,
    filter_norm_gain,
    filter_norm_bias,
    filter_in,
    filter_in_bias,
    filter_out,
    filter_out_bias,
    kept_lat,
    kept_lon,
    norm_gain,
    norm_bias,
    dense_in,
    dense_in_bias,
    dense_out,
    dense_out_bias,
):
    lon_count = lax.axis_size("lon")
    lat_count = lax.axis_size("lat")
    band_rows = patches.shape[0] // lon_count
    local_channels = patches.shape[2]
    local_blocks = filter_in.shape[1]
    block_width = filter_in.shape[2]
    row_span = lon_count * band_rows
    local_freqs = KEEP_LON // (lon_count * lat_count)
    local_rows = lax.all_to_all(patches, "lon", split_axis=0, concat_axis=1, tiled=True)
    raw = local_rows.astype(jnp.float32)
    cell_total = lax.psum(jnp.sum(raw, axis=-1, keepdims=True), "ch")
    pre_center = cell_total / C
    centered = raw - pre_center
    square_total = lax.psum(jnp.sum(centered * centered, axis=-1, keepdims=True), "ch")
    pre_spread = square_total / C
    prenormed = (
        centered * lax.rsqrt(pre_spread + norm_epsilon) * filter_norm_gain.astype(jnp.float32)
        + filter_norm_bias.astype(jnp.float32)
    ).astype(jnp.bfloat16)
    spectrum = jnp.einsum(
        "rwc,wtk->trkc", prenormed, lon_forward(KEEP_LON, W), preferred_element_type=jnp.float32
    )
    spectrum = spectrum.astype(jnp.bfloat16)
    slot_ids = jnp.arange(H, dtype=jnp.int32)
    group_ids = slot_ids // band_rows
    direct_rows = (
        group_ids % lat_count * row_span + group_ids // lat_count * band_rows + slot_ids % band_rows
    )
    pencil = lax.all_to_all(spectrum, ("lon", "lat"), split_axis=2, concat_axis=1, tiled=True)
    banded = jnp.dot(
        lat_forward_table(direct_rows, MLAT, H),
        pencil.reshape(2 * H, -1),
        preferred_element_type=jnp.float32,
    )
    banded = banded.astype(jnp.bfloat16).reshape(
        2, 2 * MLAT, local_freqs, local_blocks, block_width
    )
    first = complex_layer(banded, filter_in, filter_in_bias.reshape(2, local_blocks, block_width))
    first = jnp.maximum(first, 0.0).astype(jnp.bfloat16)
    second = complex_layer(first, filter_out, filter_out_bias.reshape(2, local_blocks, block_width))
    shrunk = jnp.sign(second) * jnp.maximum(jnp.abs(second) - shrink_level, 0.0)
    column_ids = (
        lax.axis_index("lon") * lat_count + lax.axis_index("lat")
    ) * local_freqs + jnp.arange(local_freqs, dtype=jnp.int32)
    band_slots = jnp.arange(2 * MLAT, dtype=jnp.int32)
    signed_band = jnp.where(band_slots < MLAT, band_slots, band_slots - 2 * MLAT)
    lat_ok = (signed_band[:, None] >= -kept_lat[None, :]) & (
        signed_band[:, None] < kept_lat[None, :]
    )
    lon_ok = column_ids[:, None] < kept_lon[None, :]
    keep_mask = (lat_ok[:, None, :] & lon_ok[None, :, :]).astype(jnp.float32)[..., None]
    kept_modes = (shrunk * keep_mask).astype(jnp.bfloat16).reshape(4 * MLAT, -1)
    spatial = jnp.dot(
        lat_inverse_table(direct_rows, MLAT, H), kept_modes, preferred_element_type=jnp.float32
    )
    spatial = spatial.astype(jnp.bfloat16).reshape(2, H, local_freqs, local_channels)
    returned = lax.all_to_all(spatial, ("lon", "lat"), split_axis=1, concat_axis=2, tiled=True)
    back_freqs = jnp.arange(KEEP_LON, dtype=jnp.int32)
    fine_part = jnp.einsum(
        "trkc,tkw->rwc", returned, lon_inverse(back_freqs, W), preferred_element_type=jnp.float32
    )
    mixed = (raw + fine_part).astype(jnp.bfloat16)
    gathered = lax.all_gather(mixed, "ch", axis=2, tiled=True)
    partial_terms = channel_mlp(gathered, norm_gain, norm_bias, dense_in, dense_in_bias, dense_out)
    summed = lax.psum_scatter(
        partial_terms.astype(jnp.bfloat16), "ch", scatter_dimension=2, tiled=True
    ).astype(jnp.float32)
    result = (mixed.astype(jnp.float32) + summed + dense_out_bias.astype(jnp.float32)).astype(
        jnp.bfloat16
    )
    return result.reshape(1, 1, band_rows, W, local_channels)


def solution(mesh):
    placed = (
        P(("grp", "lat"), "lon", "ch"),
        P("ch"),
        P("ch"),
        P(None, "ch", None, None),
        P(None, "ch"),
        P(None, "ch", None, None),
        P(None, "ch"),
        P("ch"),
        P("ch"),
        P(),
        P(),
        P(None, "ch"),
        P("ch"),
        P("ch", None),
        P("ch"),
    )
    sizes = mesh.shape
    lat_count, lon_count = sizes["lat"], sizes["lon"]
    cols = W // lon_count
    fits = lat_count == 2 and sizes["ch"] == 2 and MLAT % (lat_count * lon_count) == 0
    fits = fits and cols == 96 and H % (2 * lat_count * lon_count) == 0
    plan = functools.partial(column_plan, (32, 32, 32)) if fits else row_plan
    return jax.shard_map(
        plan,
        mesh=mesh,
        in_specs=placed,
        out_specs=P(("grp", "lat"), "lon", None, None, "ch"),
        check_vma=False,
    )
```

```python
import functools
import math

import jax
import jax.numpy as jnp
import numpy as np
from jax import lax
from jax.experimental import pallas as pl
from jax.experimental.pallas import tpu as pltpu
from jax.sharding import PartitionSpec as P

H = 256
W = 384
C = 768
MLAT = 64
KEEP_LON = 128

shrink_level = 0.01
norm_epsilon = 1e-05

COST_SHARE = 1

BF = jnp.bfloat16
F32 = jnp.float32


def angle_table(rows, cols, length):
    phase = rows[:, None] * cols[None, :] % length
    return phase * (2.0 * math.pi / length)


def lat_slots(lat_count, lon_count):
    per = MLAT // (lat_count * lon_count)
    freq, kind = [], []
    for dev in range(lat_count * lon_count):
        for pair in range(dev * per, dev * per + per):
            freq += [0, MLAT] if pair == 0 else [pair, pair]
            kind += [0, 0] if pair == 0 else [0, 1]
        freq.append(MLAT if dev == 0 else 0)
        kind.append(1 if dev == 0 else 2)
    return np.array(freq), np.array(kind)


def lat_tables(lat_count, lon_count):
    freq, kind = lat_slots(lat_count, lon_count)
    angles = angle_table(freq, np.arange(H), H)
    table = np.where(kind[:, None] == 0, np.cos(angles), -np.sin(angles)) / math.sqrt(H)
    table = np.where(kind[:, None] == 2, 0.0, table)
    return table.astype(np.float32)


def lon_tables(order):
    freqs = np.arange(KEEP_LON)
    angles = angle_table(freqs, order, W)
    factor = 1.0 / math.sqrt(W)
    weight = np.where(freqs == 0, 1.0, 2.0)[:, None]
    forward = np.concatenate([np.cos(angles) * factor, -np.sin(angles) * factor], axis=0)
    inverse = np.concatenate(
        [np.cos(angles) * factor * weight, -np.sin(angles) * factor * weight], axis=0
    ).T
    return forward.astype(np.float32).astype(jnp.bfloat16), inverse.astype(np.float32).astype(jnp.bfloat16)


def spread8(table):
    return np.kron(table, np.eye(8, dtype=np.float32)).astype(jnp.bfloat16)


def lat_forward_kernel(where_ref, cells_ref, table_ref, send_ref, keep_ref):
    rows, _, width = cells_ref.shape
    lon_count, slots, _, _ = send_ref.shape
    values = cells_ref[...].astype(F32).reshape(rows, 2, 8, width)
    pair = jnp.concatenate(
        [values[:, 0].reshape(rows * 8, width), values[:, 1].reshape(rows * 8, width)], axis=1
    ).astype(BF)
    half = table_ref.shape[0] // 2
    for part, out_ref in ((0, send_ref), (1, keep_ref)):
        total = jnp.dot(
            table_ref[part * half : (part + 1) * half, :], pair, preferred_element_type=F32
        )
        total = jnp.concatenate(
            [
                total[:, :width].reshape(lon_count, slots, 8, width),
                total[:, width:].reshape(lon_count, slots, 8, width),
            ],
            axis=2,
        ).astype(BF)
        for z in range(lon_count):
            out_ref[lax.rem(z + lon_count - where_ref[0], lon_count)] = total[z]


def lat_forward(where, cells, table, lon_count):
    rows, cols, width = cells.shape
    slots = table.shape[0] // (16 * lon_count)
    block = pl.BlockSpec((lon_count, slots, 16, width), lambda i: (0, 0, i, 0))
    return pl.pallas_call(
        lat_forward_kernel,
        grid=(cols // 16,),
        in_specs=[
            pl.BlockSpec(memory_space=pltpu.SMEM),
            pl.BlockSpec((rows, 16, width), lambda i: (0, i, 0)),
            pl.BlockSpec(table.shape, lambda i: (0, 0)),
        ],
        out_specs=[block, block],
        out_shape=[jax.ShapeDtypeStruct((lon_count, slots, cols, width), BF)] * 2,
        compiler_params=pltpu.CompilerParams(vmem_limit_bytes=40 << 20),
        cost_estimate=pl.CostEstimate(
            flops=2 * table.size * cols // 8 * width // COST_SHARE,
            bytes_accessed=4 * rows * cols * width // COST_SHARE,
            transcendentals=0,
        ),
        name="lat_forward",
    )(where, cells, table)


def lat_inverse_kernel(
    where_ref, own_ref, other_ref, table_ref, patches_ref, mine_ref, sent_ref, flat_ref
):
    rows, _, width = patches_ref.shape
    lon_count, slots = own_ref.shape[:2]
    blank = jnp.zeros((flat_ref.shape[1] - slots * 8, 2 * width), BF)
    for side, ref in enumerate((own_ref, other_ref)):
        for s in range(lon_count):
            values = ref[s].astype(F32).reshape(slots, 2, 8, width)
            flat = jnp.concatenate(
                [values[:, 0].reshape(slots * 8, width), values[:, 1].reshape(slots * 8, width)],
                axis=1,
            )
            source = lax.rem(where_ref[0] + (lon_count - s), lon_count)
            flat_ref[side * lon_count + source] = jnp.concatenate([flat.astype(BF), blank], axis=0)
    total = jnp.dot(
        table_ref[...], flat_ref[...].reshape(-1, 2 * width), preferred_element_type=F32
    )
    fine = jnp.concatenate(
        [total[:, :width].reshape(rows, 8, width), total[:, width:].reshape(rows, 8, width)], axis=1
    )
    mixed = (patches_ref[...].astype(F32) + fine).astype(BF)
    mixed = mixed.reshape(lon_count, 2, rows // (2 * lon_count), 16, width)

    @pl.when(where_ref[1] == 0)
    def _():
        mine_ref[...] = mixed[:, 0]
        sent_ref[...] = mixed[:, 1]

    @pl.when(where_ref[1] != 0)
    def _():
        mine_ref[...] = mixed[:, 1]
        sent_ref[...] = mixed[:, 0]


def lat_inverse(where, own, other, table, patches, first_col):
    lon_count, slots, cols, width = own.shape
    rows = patches.shape[0]
    first_block = first_col // 16
    spec = pl.BlockSpec((lon_count, slots, 16, width), lambda i: (0, 0, i, 0))
    half = rows // (2 * lon_count)
    out_spec = pl.BlockSpec((lon_count, half, 16, width), lambda i: (0, 0, i, 0))
    return pl.pallas_call(
        lat_inverse_kernel,
        grid=(cols // 16,),
        in_specs=[
            pl.BlockSpec(memory_space=pltpu.SMEM),
            spec,
            spec,
            pl.BlockSpec(table.shape, lambda i: (0, 0)),
            pl.BlockSpec((rows, 16, width), lambda i: (0, first_block + i, 0)),
        ],
        out_specs=[out_spec, out_spec],
        out_shape=[jax.ShapeDtypeStruct((lon_count, half, cols, width), BF)] * 2,
        scratch_shapes=[
            pltpu.VMEM((2 * lon_count, table.shape[1] // (2 * lon_count), 2 * width), BF)
        ],
        compiler_params=pltpu.CompilerParams(vmem_limit_bytes=40 << 20),
        cost_estimate=pl.CostEstimate(
            flops=2 * table.size * cols // 8 * width // COST_SHARE,
            bytes_accessed=6 * rows * cols * width // COST_SHARE,
            transcendentals=0,
        ),
        name="lat_inverse",
    )(where, own, other, table, patches)


def modes_kernel(inputs, first_pair_ref, lat_keep_ref, lon_keep_ref, *refs):
    pair_refs = refs[:inputs]
    spare_refs = refs[inputs : 2 * inputs]
    forward_ref, inverse_ref, w_in_ref, b_in_ref, w_out_ref, b_out_ref = refs[
        2 * inputs : 2 * inputs + 6
    ]
    out_refs, spare_ref = refs[2 * inputs + 6 : -1], refs[-1]
    width = pair_refs[0].shape[-1]
    per_step = pair_refs[0].shape[0] // 2
    step = pl.program_id(0)
    last_row = 2 * per_step * pl.num_programs(0)
    pair_id = first_pair_ref[0] + step * per_step
    special = pair_id == 0
    keep = KEEP_LON

    def columns(refs, row):
        return jnp.concatenate([ref[row] for ref in refs], axis=0)

    @pl.when(special)
    def _():
        spare_ref[...] = jnp.dot(
            forward_ref[...], columns(spare_refs, 0), preferred_element_type=F32
        )

    both = jnp.concatenate([columns(pair_refs, r) for r in range(2 * per_step)], axis=1)
    spectrum = jnp.dot(forward_ref[...], both, preferred_element_type=F32)
    banded = []
    for q in range(per_step):
        a = spectrum[:, 2 * q * width : (2 * q + 1) * width]
        b = spectrum[:, (2 * q + 1) * width : (2 * q + 2) * width]
        a_re, a_im, b_re, b_im = a[:keep], a[keep:], b[:keep], b[keep:]
        plus = [a_re - b_im, a_im + b_re]
        minus = [a_re + b_im, a_im - b_re]
        if q == 0:
            plus = [jnp.where(special, a_re, plus[0]), jnp.where(special, a_im, plus[1])]
            minus = [
                jnp.where(special, b_re + spare_ref[keep:], minus[0]),
                jnp.where(special, b_im - spare_ref[:keep], minus[1]),
            ]
        banded += [jnp.concatenate(plus, axis=1), jnp.concatenate(minus, axis=1)]
    banded = jnp.concatenate(banded, axis=0).astype(BF)
    first = jnp.dot(banded, w_in_ref[...], preferred_element_type=F32) + b_in_ref[...]
    first = jnp.maximum(first, 0.0).astype(BF)
    second = jnp.dot(first, w_out_ref[...], preferred_element_type=F32) + b_out_ref[...]
    shrunk = second - jnp.clip(second, -shrink_level, shrink_level)
    freq = lax.broadcasted_iota(jnp.int32, (keep, 2 * width), 0)
    lon_ok = freq < lon_keep_ref[...]
    upper, lower = [], []
    for q in range(per_step):
        plus_ok = lon_ok & (pair_id + q < lat_keep_ref[...])
        minus_id = jnp.where(special, MLAT, pair_id) if q == 0 else pair_id + q
        minus_ok = lon_ok & (minus_id <= lat_keep_ref[...])
        plus = jnp.where(plus_ok, shrunk[2 * q * keep : (2 * q + 1) * keep], 0.0)
        minus = jnp.where(minus_ok, shrunk[(2 * q + 1) * keep : (2 * q + 2) * keep], 0.0)
        p_re, p_im, m_re, m_im = plus[:, :width], plus[:, width:], minus[:, :width], minus[:, width:]
        tops = [p_re + m_re, p_im - m_im]
        bottoms = [p_im + m_im, m_re - p_re]
        if q == 0:
            tops = [jnp.where(special, p_re, tops[0]), jnp.where(special, m_re, tops[1])]
            bottoms = [jnp.where(special, p_im, bottoms[0]), jnp.where(special, m_im, bottoms[1])]
            loose = jnp.concatenate([-m_im, m_re], axis=0).astype(BF)
        upper += tops
        lower += bottoms
    values = jnp.concatenate(
        [jnp.concatenate(upper, axis=1), jnp.concatenate(lower, axis=1)], axis=0
    ).astype(BF)

    def back(values, row):
        grid_values = jnp.dot(inverse_ref[...], values, preferred_element_type=F32).astype(BF)
        start = 0
        for ref in out_refs:
            cols = ref.shape[1]
            for r in range(grid_values.shape[1] // width):
                ref[row + r] = grid_values[start : start + cols, r * width : (r + 1) * width]
            start += cols

    back(values, 2 * per_step * step)

    @pl.when(special)
    def _():
        back(loose, last_row)

    @pl.when(jnp.logical_and(step == 0, jnp.logical_not(special)))
    def _():
        for ref in out_refs:
            ref[last_row] = jnp.zeros(ref.shape[1:], BF)


def modes(received, first_pair, lat_keep, lon_keep, forward, inverse, w_in, b_in, w_out, b_out):
    lon_count = len(received[0])
    flat = [values for chunk in received for values in chunk]
    slots, _, width = flat[0].shape
    pairs = slots // 2
    per_step = 2 if pairs % 2 == 0 else 1
    pair_specs = [pl.BlockSpec((2 * per_step, r.shape[1], width), lambda i: (i, 0, 0)) for r in flat]
    spare_specs = [pl.BlockSpec((1, r.shape[1], width), lambda i: (slots - 1, 0, 0)) for r in flat]
    whole = lambda array: pl.BlockSpec(array.shape, lambda i: (0,) * array.ndim)
    out = pl.pallas_call(
        functools.partial(modes_kernel, len(flat)),
        grid=(pairs // per_step,),
        in_specs=[pl.BlockSpec(memory_space=pltpu.SMEM), whole(lat_keep), whole(lon_keep)]
        + pair_specs
        + spare_specs
        + [whole(forward), whole(inverse), whole(w_in), whole(b_in), whole(w_out), whole(b_out)],
        out_specs=[pl.BlockSpec(r.shape, lambda i: (0, 0, 0)) for r in flat],
        out_shape=[jax.ShapeDtypeStruct(r.shape, BF) for r in flat],
        scratch_shapes=[pltpu.VMEM((2 * KEEP_LON, width), F32)],
        compiler_params=pltpu.CompilerParams(vmem_limit_bytes=48 << 20),
        cost_estimate=pl.CostEstimate(
            flops=pairs * 2 * (2 * 2 * KEEP_LON * W * 2 * width + 4 * KEEP_LON * 4 * width * width),
            bytes_accessed=4 * slots * W * width,
            transcendentals=0,
        ),
        name="modes",
    )(
        first_pair, lat_keep, lon_keep, *flat, *flat,
        forward, inverse, w_in, b_in, w_out, b_out,
    )
    return [list(out[i : i + lon_count]) for i in range(0, len(flat), lon_count)]


def mlp_kernel(
    where_ref, own_ref, other_ref, gain_ref, bias_ref, w_in_ref, b_in_ref, w_out_ref, b_out_ref,
    out_ref,
):
    _, rows, cols, width = own_ref.shape
    cells = rows * cols
    own = own_ref[0].reshape(cells, width)
    other = other_ref[0].reshape(cells, width)
    flip = where_ref[1] == 1
    low = jnp.where(flip, other, own)
    high = jnp.where(flip, own, other)
    wide = jnp.concatenate([low, high], axis=1).astype(F32)
    center = jnp.mean(wide, axis=1, keepdims=True)
    off = wide - center
    spread = jnp.mean(off * off, axis=1, keepdims=True)
    normed = (off * lax.rsqrt(spread + norm_epsilon) * gain_ref[...] + bias_ref[...]).astype(BF)
    hidden = jnp.dot(normed, w_in_ref[...], preferred_element_type=F32) + b_in_ref[...]
    hidden = (hidden * (0.5 + 0.5 * lax.erf(hidden * math.sqrt(0.5)))).astype(BF)
    total = jnp.dot(hidden, w_out_ref[...], preferred_element_type=F32) + wide + b_out_ref[...]
    total = total.astype(BF)
    out_ref[0, 0] = total[:, :width].reshape(rows, cols, width)
    out_ref[0, 1] = total[:, width:].reshape(rows, cols, width)


def mlp(where, own, other, gain, bias, w_in, b_in, w_out, b_out):
    lon_count, rows, cols, width = own.shape
    whole = lambda array: pl.BlockSpec(array.shape, lambda i, where: (0,) * array.ndim)
    cell_spec = pl.BlockSpec((1, rows, cols, width), lambda i, where: (i, 0, 0, 0))
    cells = lon_count * rows * cols
    return pl.pallas_call(
        mlp_kernel,
        grid_spec=pltpu.PrefetchScalarGridSpec(
            num_scalar_prefetch=1,
            grid=(lon_count,),
            in_specs=[cell_spec, cell_spec]
            + [whole(a) for a in (gain, bias, w_in, b_in, w_out, b_out)],
            out_specs=pl.BlockSpec((1, 2, rows, cols, width), lambda i, where: (i, 0, 0, 0, 0)),
        ),
        out_shape=jax.ShapeDtypeStruct((lon_count, 2, rows, cols, width), BF),
        compiler_params=pltpu.CompilerParams(vmem_limit_bytes=48 << 20),
        cost_estimate=pl.CostEstimate(
            flops=4 * cells * w_in.size // COST_SHARE,
            bytes_accessed=8 * cells * width // COST_SHARE,
            transcendentals=cells * w_in.shape[1] // COST_SHARE,
        ),
        name="channel_mlp",
    )(where, own, other, gain, bias, w_in, b_in, w_out, b_out)


def assemble_kernel(piece_ref, *refs):
    out_ref = refs[-1]
    half = piece_ref.shape[2]
    for c in range(2):
        out_ref[c * half : (c + 1) * half] = piece_ref[0, c]


def assemble(result, pieces, first_col, block_cols):
    lon_count, _, rows, cols, width = pieces.shape
    block = math.gcd(math.gcd(cols, block_cols), first_col)
    specs = [pl.BlockSpec((1, 2, rows, block, width), lambda z, j: (z, 0, 0, j, 0))]
    operands = [pieces]
    aliases = {}
    if result is not None:
        aliases = {1: 0}
        operands.append(result)
        specs.append(pl.BlockSpec(memory_space=pl.ANY))
    return pl.pallas_call(
        assemble_kernel,
        grid=(lon_count, cols // block),
        in_specs=specs,
        out_specs=pl.BlockSpec(
            (2 * rows, block, width),
            lambda z, j: (0, z * (block_cols // block) + first_col // block + j, 0),
        ),
        out_shape=jax.ShapeDtypeStruct((2 * rows, lon_count * block_cols, width), BF),
        input_output_aliases=aliases,
        cost_estimate=pl.CostEstimate(
            flops=0, bytes_accessed=8 * lon_count * rows * cols * width, transcendentals=0
        ),
        name="assemble",
    )(*operands)


def block_diagonal(weight):
    blocks, n = weight.shape[1], weight.shape[2]
    eye = jnp.eye(blocks, dtype=weight.dtype)
    spread = (weight[:, :, :, None, :] * eye[None, :, None, :, None]).reshape(
        2, blocks * n, blocks * n
    )
    return jnp.concatenate(
        [
            jnp.concatenate([spread[0], spread[1]], axis=1),
            jnp.concatenate([-spread[1], spread[0]], axis=1),
        ],
        axis=0,
    )


def swap(values, axis):
    return lax.ppermute(values, axis, [(0, 1), (1, 0)])


def shift(values, steps, lon_count):
    if steps == 0:
        return values
    return lax.ppermute(values, "lon", [(z, (z + steps) % lon_count) for z in range(lon_count)])


def column_plan(
    widths,
    patches,
    filter_norm_gain,
    filter_norm_bias,
    filter_in,
    filter_in_bias,
    filter_out,
    filter_out_bias,
    kept_lat,
    kept_lon,
    norm_gain,
    norm_bias,
    dense_in,
    dense_in_bias,
    dense_out,
    dense_out_bias,
):
    lon_count = lax.axis_size("lon")
    lat_count = lax.axis_size("lat")
    rows, cols, width = patches.shape
    chunks = len(widths)
    starts = [sum(widths[:i]) for i in range(chunks)]
    block_width = filter_in.shape[2]
    lat_id = lax.axis_index("lat")
    lon_id = lax.axis_index("lon")
    ch_id = lax.axis_index("ch")
    pairs = MLAT // (lat_count * lon_count)
    slots = 2 * pairs + 1

    lat_table = lat_tables(lat_count, lon_count).reshape(lat_count, lon_count, slots, H)
    forward_all, inverse_all = [], []
    for a in range(lat_count):
        here = lat_table[..., a * rows : (a + 1) * rows]
        ordered = np.concatenate([here[1 - a], here[a]], axis=0).reshape(-1, rows)
        forward_all.append(spread8(ordered))
        ordered = np.concatenate([here[a], here[1 - a]], axis=0)
        ordered = np.pad(ordered, ((0, 0), (0, slots % 2), (0, 0))).reshape(-1, rows)
        inverse_all.append(spread8(ordered.T))
    forward_lat = lax.dynamic_index_in_dim(jnp.asarray(np.stack(forward_all)), lat_id, 0, False)
    inverse_lat = None

    ids = np.arange(W).reshape(lon_count, cols)

    def column_order(devices):
        return np.concatenate([ids[devices, c : c + w].reshape(-1) for c, w in zip(starts, widths)])

    steps = np.arange(lon_count)
    from_here = [lon_tables(column_order((z - steps) % lon_count))[0] for z in range(lon_count)]
    to_there = [lon_tables(column_order((z + steps) % lon_count))[1] for z in range(lon_count)]

    fence = lax.optimization_barrier
    where = jnp.stack([lon_id, ch_id]).astype(jnp.int32)

    def row_transform(i, source):
        raw = source[:, starts[i] : starts[i] + widths[i]].astype(F32)
        center = jnp.mean(raw, axis=-1)
        off = raw - center[..., None]
        square = jnp.sum(off * off, axis=-1)
        theirs = swap(jnp.stack([center, square]), "ch")
        mean = 0.5 * (center + theirs[0])
        gap = center - theirs[0]
        spread = (square + theirs[1]) / C + 0.25 * gap * gap
        scale = lax.rsqrt(spread + norm_epsilon)
        prenormed = (
            (raw - mean[..., None]) * scale[..., None] * filter_norm_gain.astype(F32)
            + filter_norm_bias.astype(F32)
        ).astype(BF)
        return lat_forward(where, prenormed, forward_lat, lon_count)

    def mlp_weights(dense_in, dense_in_bias, dense_out, dense_out_bias):
        return (
            norm_gain.astype(F32)[None],
            norm_bias.astype(F32)[None],
            jnp.concatenate([dense_in, swap(dense_in, "ch")], axis=1),
            jnp.concatenate([dense_in_bias, swap(dense_in_bias, "ch")]).astype(F32)[None],
            jnp.concatenate([dense_out, swap(dense_out, "ch")], axis=0),
            lax.all_gather(dense_out_bias, "ch", axis=0, tiled=True).astype(F32)[None],
        )

    def filter_operands():
        return (
            ((lat_id * lon_count + lon_id) * pairs).astype(jnp.int32).reshape(1),
            jnp.tile(jnp.repeat(kept_lat, block_width), 2).reshape(1, -1),
            jnp.tile(jnp.repeat(kept_lon, block_width), 2).reshape(1, -1),
            lax.dynamic_index_in_dim(jnp.asarray(np.stack(from_here)), lon_id, 0, False),
            lax.dynamic_index_in_dim(jnp.asarray(np.stack(to_there)), lon_id, 0, False),
            block_diagonal(filter_in),
            filter_in_bias.reshape(1, -1).astype(F32),
            block_diagonal(filter_out),
            filter_out_bias.reshape(1, -1).astype(F32),
        )

    def along_lon(values):
        return [shift(values[s], s, lon_count) for s in range(lon_count)]

    def row_result(i, own, other):
        mine, sent = lat_inverse(where, own, other, inverse_lat, patches, starts[i])
        return mlp(where, mine, swap(sent, "ch"), *weights)

    def outward(outputs):
        shape = outputs.shape
        flat = outputs.reshape((shape[0] * 2,) + shape[2:])
        return lax.all_to_all(flat, ("lon", "ch"), 0, 0, tiled=True).reshape(shape)

    received, summed, sent, kept = [], None, None, None
    weights = None
    filter_args = None
    ahead = None
    dense = (dense_in, dense_in_bias, dense_out, dense_out_bias)
    for step in range(chunks + 2):
        arrived = None
        if sent is not None:
            arrived = (kept, swap(sent, "lat"))
            sent = None
        if summed is not None:
            received.append(along_lon(summed))
            summed = None
        if ahead is not None:
            (sent, kept), ahead = ahead, None
        elif step < chunks:
            sent, kept = row_transform(step, patches)
        if step == chunks:
            filter_args = filter_operands()
        if step == 1 and chunks > 2:
            ahead = row_transform(2, fence((patches, kept))[0])
        patches, arrived, sent, kept, received, filter_args, weights, inverse_lat, ahead, dense = fence(
            (patches, arrived, sent, kept, received, filter_args, weights, inverse_lat, ahead, dense)
        )
        if arrived is not None:
            summed = [
                (arrived[0][s].astype(F32) + arrived[1][s].astype(F32)).astype(BF)
                for s in range(lon_count)
            ]

    filtered = modes(received, *filter_args)

    owns = [None] * chunks
    others = [None] * chunks
    outputs = [None] * chunks
    for step in range(chunks):
        owns[step] = along_lon(filtered[step])
        if step >= 1:
            owns[step - 1] = jnp.stack(owns[step - 1])
            others[step - 1] = swap(owns[step - 1], "lat")
        if step >= 2:
            outputs[step - 2] = row_result(step - 2, owns[step - 2], others[step - 2])
        if step == 0:
            dense = fence((dense, owns[0][lon_count // 2]))[0]
            weights = mlp_weights(*dense)
            inverse_lat = lax.dynamic_index_in_dim(jnp.asarray(np.stack(inverse_all)), lat_id, 0, False)
        patches, filtered, owns, others, outputs, weights, inverse_lat = fence(
            (patches, filtered, owns, others, outputs, weights, inverse_lat)
        )

    result = None
    pieces = None
    for i in range(chunks):
        last = pieces
        pieces = outward(outputs[i])
        if last is not None:
            result = assemble(result, last, starts[i - 1], cols)
        if i + 1 < chunks and outputs[i + 1] is None:
            outputs[i + 1] = row_result(i + 1, owns[i + 1], others[i + 1])
        if i + 2 < chunks and others[i + 2] is None:
            owns[i + 2] = jnp.stack(owns[i + 2])
            others[i + 2] = swap(owns[i + 2], "lat")
        patches, owns, others, outputs, pieces, result = fence(
            (patches, owns, others, outputs, pieces, result)
        )
    result = assemble(result, pieces, starts[chunks - 1], cols)
    return result.reshape(1, 1, rows // lon_count, lon_count * cols, width)


def lon_forward(number, length):
    freq_ids = jnp.arange(number, dtype=jnp.int32)
    cell_ids = jnp.arange(length, dtype=jnp.int32)
    phase_turns = cell_ids[:, None] * freq_ids[None, :] % length
    angles = phase_turns.astype(jnp.float32) * (2.0 * math.pi / length)
    factor = 1.0 / math.sqrt(length)
    return jnp.stack([jnp.cos(angles) * factor, -jnp.sin(angles) * factor], axis=1).astype(
        jnp.bfloat16
    )


def lon_inverse(freq_ids, length):
    cell_ids = jnp.arange(length, dtype=jnp.int32)
    phase_turns = freq_ids[:, None] * cell_ids[None, :] % length
    angles = phase_turns.astype(jnp.float32) * (2.0 * math.pi / length)
    factor = 1.0 / math.sqrt(length)
    weight = jnp.where(freq_ids == 0, 1.0, 2.0).astype(jnp.float32)[:, None]
    return jnp.stack(
        [jnp.cos(angles) * factor * weight, -jnp.sin(angles) * factor * weight]
    ).astype(jnp.bfloat16)


def band_ids(half_band, length):
    slot_ids = jnp.arange(2 * half_band, dtype=jnp.int32)
    return jnp.where(slot_ids < half_band, slot_ids, slot_ids + length - 2 * half_band)


def lat_forward_table(row_ids, half_band, length):
    phase_turns = band_ids(half_band, length)[:, None] * row_ids[None, :] % length
    angles = phase_turns.astype(jnp.float32) * (2.0 * math.pi / length)
    factor = 1.0 / math.sqrt(length)
    cosine = jnp.cos(angles) * factor
    sine_part = jnp.sin(angles) * factor
    upper_half = jnp.concatenate([cosine, sine_part], axis=1)
    bottom = jnp.concatenate([-sine_part, cosine], axis=1)
    return jnp.concatenate([upper_half, bottom], axis=0).astype(jnp.bfloat16)


def lat_inverse_table(row_ids, half_band, length):
    phase_turns = row_ids[:, None] * band_ids(half_band, length)[None, :] % length
    angles = phase_turns.astype(jnp.float32) * (2.0 * math.pi / length)
    factor = 1.0 / math.sqrt(length)
    cosine = jnp.cos(angles) * factor
    sine_part = jnp.sin(angles) * factor
    upper_half = jnp.concatenate([cosine, -sine_part], axis=1)
    bottom = jnp.concatenate([sine_part, cosine], axis=1)
    return jnp.concatenate([upper_half, bottom], axis=0).astype(jnp.bfloat16)


def complex_layer(values, weight, offset):
    products = jnp.einsum("tjkbc,ubcd->tujkbd", values, weight, preferred_element_type=jnp.float32)
    offset = offset.astype(jnp.float32)
    real_part = products[0, 0] - products[1, 1] + offset[0]
    imag_part = products[1, 0] + products[0, 1] + offset[1]
    return jnp.stack([real_part, imag_part])


def channel_mlp(mixed_full, norm_gain, norm_bias, weight_in, bias_in, weight_out):
    wide = mixed_full.astype(jnp.float32)
    center = jnp.mean(wide, axis=-1, keepdims=True)
    spread = jnp.mean((wide - center) ** 2, axis=-1, keepdims=True)
    normed = (
        (wide - center) * lax.rsqrt(spread + norm_epsilon) * norm_gain.astype(jnp.float32)
        + norm_bias.astype(jnp.float32)
    ).astype(jnp.bfloat16)
    hidden = jnp.einsum("rwc,cu->rwu", normed, weight_in, preferred_element_type=jnp.float32)
    hidden = jax.nn.gelu(hidden + bias_in.astype(jnp.float32), approximate=False).astype(
        jnp.bfloat16
    )
    return jnp.einsum("rwu,uc->rwc", hidden, weight_out, preferred_element_type=jnp.float32)


def row_plan(
    patches,
    filter_norm_gain,
    filter_norm_bias,
    filter_in,
    filter_in_bias,
    filter_out,
    filter_out_bias,
    kept_lat,
    kept_lon,
    norm_gain,
    norm_bias,
    dense_in,
    dense_in_bias,
    dense_out,
    dense_out_bias,
):
    lon_count = lax.axis_size("lon")
    lat_count = lax.axis_size("lat")
    band_rows = patches.shape[0] // lon_count
    local_channels = patches.shape[2]
    local_blocks = filter_in.shape[1]
    block_width = filter_in.shape[2]
    row_span = lon_count * band_rows
    local_freqs = KEEP_LON // (lon_count * lat_count)
    local_rows = lax.all_to_all(patches, "lon", split_axis=0, concat_axis=1, tiled=True)
    raw = local_rows.astype(jnp.float32)
    cell_total = lax.psum(jnp.sum(raw, axis=-1, keepdims=True), "ch")
    pre_center = cell_total / C
    centered = raw - pre_center
    square_total = lax.psum(jnp.sum(centered * centered, axis=-1, keepdims=True), "ch")
    pre_spread = square_total / C
    prenormed = (
        centered * lax.rsqrt(pre_spread + norm_epsilon) * filter_norm_gain.astype(jnp.float32)
        + filter_norm_bias.astype(jnp.float32)
    ).astype(jnp.bfloat16)
    spectrum = jnp.einsum(
        "rwc,wtk->trkc", prenormed, lon_forward(KEEP_LON, W), preferred_element_type=jnp.float32
    )
    spectrum = spectrum.astype(jnp.bfloat16)
    slot_ids = jnp.arange(H, dtype=jnp.int32)
    group_ids = slot_ids // band_rows
    direct_rows = (
        group_ids % lat_count * row_span + group_ids // lat_count * band_rows + slot_ids % band_rows
    )
    pencil = lax.all_to_all(spectrum, ("lon", "lat"), split_axis=2, concat_axis=1, tiled=True)
    banded = jnp.dot(
        lat_forward_table(direct_rows, MLAT, H),
        pencil.reshape(2 * H, -1),
        preferred_element_type=jnp.float32,
    )
    banded = banded.astype(jnp.bfloat16).reshape(
        2, 2 * MLAT, local_freqs, local_blocks, block_width
    )
    first = complex_layer(banded, filter_in, filter_in_bias.reshape(2, local_blocks, block_width))
    first = jnp.maximum(first, 0.0).astype(jnp.bfloat16)
    second = complex_layer(first, filter_out, filter_out_bias.reshape(2, local_blocks, block_width))
    shrunk = jnp.sign(second) * jnp.maximum(jnp.abs(second) - shrink_level, 0.0)
    column_ids = (
        lax.axis_index("lon") * lat_count + lax.axis_index("lat")
    ) * local_freqs + jnp.arange(local_freqs, dtype=jnp.int32)
    band_slots = jnp.arange(2 * MLAT, dtype=jnp.int32)
    signed_band = jnp.where(band_slots < MLAT, band_slots, band_slots - 2 * MLAT)
    lat_ok = (signed_band[:, None] >= -kept_lat[None, :]) & (
        signed_band[:, None] < kept_lat[None, :]
    )
    lon_ok = column_ids[:, None] < kept_lon[None, :]
    keep_mask = (lat_ok[:, None, :] & lon_ok[None, :, :]).astype(jnp.float32)[..., None]
    kept_modes = (shrunk * keep_mask).astype(jnp.bfloat16).reshape(4 * MLAT, -1)
    spatial = jnp.dot(
        lat_inverse_table(direct_rows, MLAT, H), kept_modes, preferred_element_type=jnp.float32
    )
    spatial = spatial.astype(jnp.bfloat16).reshape(2, H, local_freqs, local_channels)
    returned = lax.all_to_all(spatial, ("lon", "lat"), split_axis=1, concat_axis=2, tiled=True)
    back_freqs = jnp.arange(KEEP_LON, dtype=jnp.int32)
    fine_part = jnp.einsum(
        "trkc,tkw->rwc", returned, lon_inverse(back_freqs, W), preferred_element_type=jnp.float32
    )
    mixed = (raw + fine_part).astype(jnp.bfloat16)
    gathered = lax.all_gather(mixed, "ch", axis=2, tiled=True)
    partial_terms = channel_mlp(gathered, norm_gain, norm_bias, dense_in, dense_in_bias, dense_out)
    summed = lax.psum_scatter(
        partial_terms.astype(jnp.bfloat16), "ch", scatter_dimension=2, tiled=True
    ).astype(jnp.float32)
    result = (mixed.astype(jnp.float32) + summed + dense_out_bias.astype(jnp.float32)).astype(
        jnp.bfloat16
    )
    return result.reshape(1, 1, band_rows, W, local_channels)


def solution(mesh):
    placed = (
        P(("grp", "lat"), "lon", "ch"),
        P("ch"),
        P("ch"),
        P(None, "ch", None, None),
        P(None, "ch"),
        P(None, "ch", None, None),
        P(None, "ch"),
        P("ch"),
        P("ch"),
        P(),
        P(),
        P(None, "ch"),
        P("ch"),
        P("ch", None),
        P("ch"),
    )
    sizes = mesh.shape
    lat_count, lon_count = sizes["lat"], sizes["lon"]
    cols = W // lon_count
    fits = lat_count == 2 and sizes["ch"] == 2 and MLAT % (lat_count * lon_count) == 0
    fits = fits and cols == 96 and H % (2 * lat_count * lon_count) == 0
    plan = functools.partial(column_plan, (32, 32, 32)) if fits else row_plan
    return jax.shard_map(
        plan,
        mesh=mesh,
        in_specs=placed,
        out_specs=P(("grp", "lat"), "lon", None, None, "ch"),
        check_vma=False,
    )
```
